32 devices in a mesh: groups: 2 (over x), expert: 16 (over z, y, core).
Axes of the slice: x: 2, y: 2, z: 4, core: 2. Of those that a mesh axis runs over, the one named last changes fastest.
Arguments:
- tokens: bfloat16 [96, 256, 1280], P(('groups', 'expert')), parts along dimension 0, may hold values from -40 to 40
- router: bfloat16 [1280, 4], P(None, 'groups'), parts along dimension 1, may hold values from -1 to 1
- w_in: bfloat16 [32, 1280, 640], P(('groups', 'expert')), parts along dimension 0, may hold values from -0.15625 to 0.15625
- w_out: bfloat16 [32, 640, 1280], P(('groups', 'expert')), parts along dimension 0, may hold values from -0.078125 to 0.078125
- d_out: bfloat16 [96, 256, 1280], P(('groups', 'expert')), parts along dimension 0, may hold values from -6 to 6
Outputs:
- grad_tokens: bfloat16 [96, 256, 1280], P(('groups', 'expert')), parts along dimension 0
- grad_w_in: bfloat16 [32, 1280, 640], P(('groups', 'expert')), parts along dimension 0
- grad_w_out: bfloat16 [32, 640, 1280], P(('groups', 'expert')), parts along dimension 0
- grad_router: float32 [1280, 4], P(None, 'groups'), parts along dimension 1
The draws below stay inside these ranges and needn't reach their ends.
There are 2 independent parts, one for each index of `groups`. The reference program is written for one: setup_inputs(seed, part) draws one part's arguments, and reference() takes and returns one part's arrays. A program takes and returns all parts, laid end to end along the dimension named above; each array names one. Nothing has to cross between parts.
All inputs are finite; a program needn't handle non-finite values.
Results may differ from the reference program's by a relative error of at most 0.0083.
Values may be sent and summed in bfloat16 or wider, within the bound.
No kernel may reach another device: no remote copies, remote signals or barrier semaphores. Data moves between devices by JAX's collectives and lax.ppermute only.
A program may use at most 64 MiB of HBM per device.

```python
import jax
import jax.numpy as jnp
from jax import lax

D = 1280
FF = 5120
M = 256
FF_DEV = 640
SPLIT = 8
EXPERTS = 2
IMAGES = 48


def router_directions(key):
    return jnp.clip(jax.random.normal(key, (D, EXPERTS), jnp.float32), -6.0, 6.0)


def draw_router(key, part):
    directions = router_directions(key)
    return (0.03 * directions).astype(jnp.bfloat16)


def draw_tokens(key, part):
    key = jax.random.fold_in(key, 7)
    noise_key = jax.random.fold_in(key, 0)
    values = jax.random.normal(noise_key, (IMAGES, M, D), jnp.float32)
    return jnp.clip(values, -40.0, 40.0).astype(jnp.bfloat16)


def block_levels(key, extent, cuts, low, high):
    def one(dim, blocks):
        draws = jax.random.uniform(jax.random.fold_in(jax.random.fold_in(key, 6), dim), (blocks,), jnp.float32, low / len(cuts), high / len(cuts))
        return jnp.repeat(jnp.exp(draws), extent[dim] // blocks).reshape((-1,) + (1,) * (len(extent) - dim - 1))

    gain = one(*cuts[0])
    for cut in cuts[1:]:
        gain = gain * one(*cut)
    return gain


def centred(key, extent, spread, most, cuts=(), kind=jnp.bfloat16):
    drawn = spread * jax.random.normal(key, extent, jnp.float32)
    if cuts:
        drawn = drawn * block_levels(key, extent, cuts, -0.22, 0.18)
    return jnp.clip(drawn, -most, most).astype(kind)


def setup_inputs(seed: int = 0, part: int = 0) -> dict:
    keys = jax.random.split(jax.random.key(seed), 6)
    part_keys = jax.random.split(jax.random.fold_in(keys[5], part), 6)
    tokens = draw_tokens(jax.random.fold_in(jax.random.fold_in(keys[5], part), 71), part)
    router = draw_router(jax.random.fold_in(jax.random.fold_in(keys[5], part), 71), part)
    w_in = centred(part_keys[2], (EXPERTS * SPLIT, D, FF_DEV), D ** -0.5, 0.15625, ((0, 16),))
    w_out = centred(part_keys[3], (EXPERTS * SPLIT, FF_DEV, D), FF ** -0.5, 0.078125, ((0, 16),))
    d_out = centred(part_keys[4], (IMAGES, M, D), 1.0, 6.0, ((0, 16),))
    return dict(tokens=tokens, router=router, w_in=w_in, w_out=w_out, d_out=d_out)


def gelu_grad(pre, grad):
    return jax.vjp(lambda value: jax.nn.gelu(value, approximate=True), pre)[1](grad)[0]

def reference(tokens, router, w_in, w_out, d_out):
    f32 = jnp.float32
    bf16 = jnp.bfloat16
    logits = jnp.einsum('bmd,ds->bsm', tokens.astype(f32), router.astype(f32))
    dispatch = jax.nn.softmax(logits, axis=2)
    combine = jax.nn.softmax(logits, axis=1)
    disp_b = dispatch.astype(bf16)
    comb_b = combine.astype(bf16)
    slot_in = jnp.einsum('bsm,bmd->bsd', disp_b.astype(f32), tokens.astype(f32)).astype(bf16)
    grad_slot_out = jnp.einsum('bsm,bmd->bsd', comb_b.astype(f32), d_out.astype(f32)).astype(bf16)
    slot_outs = []
    slot_grads = []
    grads_in = []
    grads_out = []
    for expert in range(EXPERTS):
        first = w_in[expert * SPLIT:(expert + 1) * SPLIT]
        second = w_out[expert * SPLIT:(expert + 1) * SPLIT]
        w_one = jnp.transpose(first, (1, 0, 2)).reshape(D, FF)
        w_two = second.reshape(FF, D)
        rows_in = slot_in[:, expert, :]
        rows_grad = grad_slot_out[:, expert, :]
        hidden_pre = jnp.dot(rows_in, w_one, preferred_element_type=f32)
        hidden = jax.nn.gelu(hidden_pre, approximate=True).astype(bf16)
        slot_outs.append(jnp.dot(hidden, w_two, preferred_element_type=f32).astype(bf16))
        grad_hidden = jnp.dot(rows_grad, w_two.T, preferred_element_type=f32)
        grad_pre = gelu_grad(hidden_pre, grad_hidden).astype(bf16)
        grad_two = jnp.dot(hidden.T, rows_grad, preferred_element_type=f32).astype(bf16)
        grad_one = jnp.dot(rows_in.T, grad_pre, preferred_element_type=f32).astype(bf16)
        grads_out.append(grad_two.reshape(SPLIT, FF_DEV, D))
        grads_in.append(jnp.transpose(grad_one.reshape(D, SPLIT, FF_DEV), (1, 0, 2)))
        slot_grads.append(jnp.dot(grad_pre, w_one.T, preferred_element_type=f32).astype(bf16))
    slot_out = jnp.stack(slot_outs, axis=1)
    grad_slot_in = jnp.stack(slot_grads, axis=1)
    grad_combine = jnp.einsum('bmd,bsd->bsm', d_out.astype(f32), slot_out.astype(f32))
    grad_dispatch = jnp.einsum('bsd,bmd->bsm', grad_slot_in.astype(f32), tokens.astype(f32))
    grad_logits = dispatch * (grad_dispatch - lax.optimization_barrier(jnp.sum(dispatch * grad_dispatch, axis=2, keepdims=True)))
    grad_logits = grad_logits + combine * (grad_combine - lax.optimization_barrier(jnp.sum(combine * grad_combine, axis=1, keepdims=True)))
    gl_b = grad_logits.astype(bf16)
    grad_tokens = jnp.einsum('bsm,bsd->bmd', disp_b.astype(f32), grad_slot_in.astype(f32))
    grad_tokens = grad_tokens + jnp.einsum('bsm,ds->bmd', gl_b.astype(f32), router.astype(f32))
    grad_router = jnp.einsum('bmd,bsm->ds', tokens.astype(f32), gl_b.astype(f32))
    return (grad_tokens.astype(bf16), jnp.concatenate(grads_in, axis=0), jnp.concatenate(grads_out, axis=0), grad_router)
```

```python
import jax
import jax.numpy as jnp
from jax import lax
from jax.sharding import PartitionSpec as P


def gelu_grad(pre, grad):
    return jax.vjp(lambda value: jax.nn.gelu(value, approximate=True), pre)[1](grad)[0]


def exchange(blocks):
    return lax.all_to_all(blocks, "expert", split_axis=0, concat_axis=0, tiled=True)


def per_device(tokens, router, w_in, w_out, d_out):
    f32 = jnp.float32
    bf16 = jnp.bfloat16
    devices = lax.axis_size("expert")
    slots = router.shape[1]
    split_count = devices // slots
    images = tokens.shape[0]
    width = tokens.shape[2]
    logits = jnp.einsum("bmd,ds->bsm", tokens, router, preferred_element_type=f32)
    dispatch = jax.nn.softmax(logits, axis=2)
    combine = jax.nn.softmax(logits, axis=1)
    disp_b = dispatch.astype(bf16)
    comb_b = combine.astype(bf16)
    slot_in = jnp.einsum("bsm,bmd->sbd", disp_b, tokens, preferred_element_type=f32).astype(bf16)
    grad_slot_out = jnp.einsum("bsm,bmd->sbd", comb_b, d_out, preferred_element_type=f32).astype(
        bf16
    )
    rows = jnp.concatenate([slot_in, grad_slot_out], axis=1)
    rows = jnp.broadcast_to(rows[:, None], (slots, split_count, 2 * images, width))
    rows = exchange(rows.reshape(devices, 2 * images, width))
    rows_in = rows[:, :images].reshape(devices * images, width)
    rows_grad = rows[:, images:].reshape(devices * images, width)
    w_one = w_in[0]
    w_two = w_out[0]
    hidden_pre = jnp.dot(rows_in, w_one, preferred_element_type=f32)
    hidden = jax.nn.gelu(hidden_pre, approximate=True).astype(bf16)
    out_part = jnp.dot(hidden, w_two, preferred_element_type=f32)
    grad_hidden = jnp.einsum("bd,fd->bf", rows_grad, w_two, preferred_element_type=f32)
    grad_pre = gelu_grad(hidden_pre, grad_hidden).astype(bf16)
    slot_part = jnp.einsum("bf,df->bd", grad_pre, w_one, preferred_element_type=f32)
    grad_two = jnp.einsum("bf,bd->fd", hidden, rows_grad, preferred_element_type=f32).astype(bf16)
    grad_one = jnp.einsum("bd,bf->df", rows_in, grad_pre, preferred_element_type=f32).astype(bf16)
    grad_w_in, grad_w_out = (grad_one[None], grad_two[None])
    shares = jnp.concatenate(
        [
            out_part.astype(bf16).reshape(devices, images, width),
            slot_part.astype(bf16).reshape(devices, images, width),
        ],
        axis=1,
    )
    shares = exchange(shares).reshape(slots, split_count, 2 * images, width)
    summed = jnp.sum(shares.astype(f32), axis=1).astype(bf16)
    slot_out = summed[:, :images]
    grad_slot_in = summed[:, images:]
    grad_combine = jnp.einsum("bmd,sbd->bsm", d_out, slot_out, preferred_element_type=f32)
    grad_dispatch = jnp.einsum("sbd,bmd->bsm", grad_slot_in, tokens, preferred_element_type=f32)
    grad_logits = dispatch * (
        grad_dispatch - jnp.sum(dispatch * grad_dispatch, axis=2, keepdims=True)
    )
    grad_logits = grad_logits + combine * (
        grad_combine - jnp.sum(combine * grad_combine, axis=1, keepdims=True)
    )
    gl_b = grad_logits.astype(bf16)
    router_terms = jnp.einsum("bmd,bsm->sd", tokens, gl_b, preferred_element_type=f32)
    terms = exchange(jnp.broadcast_to(router_terms[None], (devices, slots, width)))
    grad_router = jnp.sum(terms, axis=0).T
    grad_tokens = jnp.einsum("bsm,sbd->bmd", disp_b, grad_slot_in, preferred_element_type=f32)
    grad_tokens = grad_tokens + jnp.einsum("bsm,ds->bmd", gl_b, router, preferred_element_type=f32)
    return (grad_tokens.astype(bf16), grad_w_in, grad_w_out, grad_router)


def solution(mesh):
    in_specs = (
        P(("groups", "expert"), None, None),
        P(None, "groups"),
        P(("groups", "expert"), None, None),
        P(("groups", "expert"), None, None),
        P(("groups", "expert"), None, None),
    )
    out_specs = (
        P(("groups", "expert"), None, None),
        P(("groups", "expert"), None, None),
        P(("groups", "expert"), None, None),
        P(None, "groups"),
    )
    return jax.shard_map(
        per_device, mesh=mesh, in_specs=in_specs, out_specs=out_specs, check_vma=False
    )
```

```python
import jax
import jax.numpy as jnp
from jax import lax
from jax.sharding import PartitionSpec as P


def gelu_grad(pre, grad):
    return jax.vjp(lambda value: jax.nn.gelu(value, approximate=True), pre)[1](grad)[0]


def permute(block, move):
    count = lax.axis_size("expert")
    return lax.ppermute(block, "expert", [(source, move(source)) for source in range(count)])


def bits_of(count):
    return [1 << place for place in range(count.bit_length() - 1)]


def per_device(tokens, router, w_in, w_out, d_out):
    f32 = jnp.float32
    bf16 = jnp.bfloat16
    devices = lax.axis_size("expert")
    slots = router.shape[1]
    split_count = devices // slots
    images = tokens.shape[0]
    width = tokens.shape[2]
    logits = jnp.einsum("bmd,ds->bsm", tokens, router, preferred_element_type=f32)
    dispatch = jax.nn.softmax(logits, axis=2)
    combine = jax.nn.softmax(logits, axis=1)
    disp_b = dispatch.astype(bf16)
    comb_b = combine.astype(bf16)
    slot_in = jnp.einsum("bsm,bmd->sbd", disp_b, tokens, preferred_element_type=f32).astype(bf16)
    grad_slot_out = jnp.einsum("bsm,bmd->sbd", comb_b, d_out, preferred_element_type=f32).astype(
        bf16
    )
    rows = jnp.concatenate([slot_in, grad_slot_out], axis=1)
    own = lax.axis_index("expert") // split_count
    held = [lax.dynamic_index_in_dim(rows, own, 0, keepdims=False)]
    for far in range(1, slots):
        sent = lax.dynamic_index_in_dim(rows, (own + far) % slots, 0, keepdims=False)
        held.append(permute(sent, lambda d: (d + far * split_count) % devices))
    rows = jnp.stack(held)
    for bit in reversed(bits_of(split_count)):
        rows = jnp.stack([rows, permute(rows, lambda d: d ^ bit)])
    rows = rows.reshape(devices, 2 * images, width)
    rows_in = rows[:, :images].reshape(devices * images, width)
    rows_grad = rows[:, images:].reshape(devices * images, width)
    w_one = w_in[0]
    w_two = w_out[0]
    hidden_pre = jnp.dot(rows_in, w_one, preferred_element_type=f32)
    hidden = jax.nn.gelu(hidden_pre, approximate=True).astype(bf16)
    out_part = jnp.dot(hidden, w_two, preferred_element_type=f32)
    grad_hidden = jnp.einsum("bd,fd->bf", rows_grad, w_two, preferred_element_type=f32)
    grad_pre = gelu_grad(hidden_pre, grad_hidden).astype(bf16)
    slot_part = jnp.einsum("bf,df->bd", grad_pre, w_one, preferred_element_type=f32)
    grad_two = jnp.einsum("bf,bd->fd", hidden, rows_grad, preferred_element_type=f32).astype(bf16)
    grad_one = jnp.einsum("bd,bf->df", rows_in, grad_pre, preferred_element_type=f32).astype(bf16)
    grad_w_in, grad_w_out = (grad_one[None], grad_two[None])
    shares = jnp.concatenate(
        [
            out_part.astype(bf16).reshape(devices, images, width),
            slot_part.astype(bf16).reshape(devices, images, width),
        ],
        axis=1,
    )
    for bit in bits_of(split_count):
        shares = shares.reshape((2, -1) + shares.shape[1:])
        received = permute(shares[1], lambda d: d ^ bit)
        shares = (shares[0].astype(f32) + received.astype(f32)).astype(bf16)
    held = [shares[0]]
    for far in range(1, slots):
        held.append(permute(shares[slots - far], lambda d: (d + far * split_count) % devices))
    held = jnp.stack(held)
    summed = jnp.stack(
        [
            lax.dynamic_index_in_dim(held, (own - slot) % slots, 0, keepdims=False)
            for slot in range(slots)
        ]
    )
    slot_out = summed[:, :images]
    grad_slot_in = summed[:, images:]
    grad_combine = jnp.einsum("bmd,sbd->bsm", d_out, slot_out, preferred_element_type=f32)
    grad_dispatch = jnp.einsum("sbd,bmd->bsm", grad_slot_in, tokens, preferred_element_type=f32)
    grad_logits = dispatch * (
        grad_dispatch - jnp.sum(dispatch * grad_dispatch, axis=2, keepdims=True)
    )
    grad_logits = grad_logits + combine * (
        grad_combine - jnp.sum(combine * grad_combine, axis=1, keepdims=True)
    )
    gl_b = grad_logits.astype(bf16)
    router_terms = jnp.einsum("bmd,bsm->sd", tokens, gl_b, preferred_element_type=f32)
    total = router_terms
    for shift in range(1, devices):
        total = total + permute(router_terms, lambda d: d ^ shift)
    grad_router = total.T
    grad_tokens = jnp.einsum("bsm,sbd->bmd", disp_b, grad_slot_in, preferred_element_type=f32)
    grad_tokens = grad_tokens + jnp.einsum("bsm,ds->bmd", gl_b, router, preferred_element_type=f32)
    return (grad_tokens.astype(bf16), grad_w_in, grad_w_out, grad_router)


def solution(mesh):
    in_specs = (
        P(("groups", "expert"), None, None),
        P(None, "groups"),
        P(("groups", "expert"), None, None),
        P(("groups", "expert"), None, None),
        P(("groups", "expert"), None, None),
    )
    out_specs = (
        P(("groups", "expert"), None, None),
        P(("groups", "expert"), None, None),
        P(("groups", "expert"), None, None),
        P(None, "groups"),
    )
    return jax.shard_map(
        per_device, mesh=mesh, in_specs=in_specs, out_specs=out_specs, check_vma=False
    )
```

```python
import jax
import jax.numpy as jnp
from jax import lax
from jax.sharding import PartitionSpec as P


def gelu_grad(pre, grad):
    return jax.vjp(lambda value: jax.nn.gelu(value, approximate=True), pre)[1](grad)[0]


def exchange(blocks):
    count = lax.axis_size("expert")
    groups = [list(range(core, count, 2)) for core in range(2)]
    return lax.all_to_all(
        blocks, "expert", split_axis=0, concat_axis=0, axis_index_groups=groups, tiled=True
    )


def other_core(block):
    count = lax.axis_size("expert")
    return lax.ppermute(block, "expert", [(device, device ^ 1) for device in range(count)])


def per_device(tokens, router, w_in, w_out, d_out):
    f32 = jnp.float32
    bf16 = jnp.bfloat16
    devices = lax.axis_size("expert")
    slots = router.shape[1]
    split_count = devices // slots
    images = tokens.shape[0]
    width = tokens.shape[2]
    logits = jnp.einsum("bmd,ds->bsm", tokens, router, preferred_element_type=f32)
    dispatch = jax.nn.softmax(logits, axis=2)
    combine = jax.nn.softmax(logits, axis=1)
    disp_b = dispatch.astype(bf16)
    comb_b = combine.astype(bf16)
    slot_in = jnp.einsum("bsm,bmd->sbd", disp_b, tokens, preferred_element_type=f32).astype(bf16)
    grad_slot_out = jnp.einsum("bsm,bmd->sbd", comb_b, d_out, preferred_element_type=f32).astype(
        bf16
    )
    chips = devices // 2
    rows = jnp.concatenate([slot_in, grad_slot_out], axis=1)
    rows = jnp.broadcast_to(rows[:, None], (slots, split_count // 2, 2 * images, width))
    rows = exchange(rows.reshape(chips, 2 * images, width))
    rows = jnp.stack([rows, other_core(rows)]).reshape(devices, 2 * images, width)
    rows_in = rows[:, :images].reshape(devices * images, width)
    rows_grad = rows[:, images:].reshape(devices * images, width)
    w_one = w_in[0]
    w_two = w_out[0]
    hidden_pre = jnp.dot(rows_in, w_one, preferred_element_type=f32)
    hidden = jax.nn.gelu(hidden_pre, approximate=True).astype(bf16)
    out_part = jnp.dot(hidden, w_two, preferred_element_type=f32)
    grad_hidden = jnp.einsum("bd,fd->bf", rows_grad, w_two, preferred_element_type=f32)
    grad_pre = gelu_grad(hidden_pre, grad_hidden).astype(bf16)
    slot_part = jnp.einsum("bf,df->bd", grad_pre, w_one, preferred_element_type=f32)
    grad_two = jnp.einsum("bf,bd->fd", hidden, rows_grad, preferred_element_type=f32).astype(bf16)
    grad_one = jnp.einsum("bd,bf->df", rows_in, grad_pre, preferred_element_type=f32).astype(bf16)
    grad_w_in, grad_w_out = (grad_one[None], grad_two[None])
    shares = jnp.concatenate(
        [
            out_part.astype(bf16).reshape(devices, images, width),
            slot_part.astype(bf16).reshape(devices, images, width),
        ],
        axis=1,
    )
    shares = shares.reshape(2, chips, 2 * images, width)
    shares = shares[0].astype(f32) + other_core(shares[1]).astype(f32)
    shares = exchange(shares.astype(bf16)).reshape(slots, split_count // 2, 2 * images, width)
    summed = jnp.sum(shares.astype(f32), axis=1).astype(bf16)
    slot_out = summed[:, :images]
    grad_slot_in = summed[:, images:]
    grad_combine = jnp.einsum("bmd,sbd->bsm", d_out, slot_out, preferred_element_type=f32)
    grad_dispatch = jnp.einsum("sbd,bmd->bsm", grad_slot_in, tokens, preferred_element_type=f32)
    grad_logits = dispatch * (
        grad_dispatch - jnp.sum(dispatch * grad_dispatch, axis=2, keepdims=True)
    )
    grad_logits = grad_logits + combine * (
        grad_combine - jnp.sum(combine * grad_combine, axis=1, keepdims=True)
    )
    gl_b = grad_logits.astype(bf16)
    router_terms = jnp.einsum("bmd,bsm->sd", tokens, gl_b, preferred_element_type=f32)
    terms = router_terms + other_core(router_terms)
    terms = exchange(jnp.broadcast_to(terms[None], (chips, slots, width)))
    grad_router = jnp.sum(terms, axis=0).T
    grad_tokens = jnp.einsum("bsm,sbd->bmd", disp_b, grad_slot_in, preferred_element_type=f32)
    grad_tokens = grad_tokens + jnp.einsum("bsm,ds->bmd", gl_b, router, preferred_element_type=f32)
    return (grad_tokens.astype(bf16), grad_w_in, grad_w_out, grad_router)


def solution(mesh):
    in_specs = (
        P(("groups", "expert"), None, None),
        P(None, "groups"),
        P(("groups", "expert"), None, None),
        P(("groups", "expert"), None, None),
        P(("groups", "expert"), None, None),
    )
    out_specs = (
        P(("groups", "expert"), None, None),
        P(("groups", "expert"), None, None),
        P(("groups", "expert"), None, None),
        P(None, "groups"),
    )
    return jax.shard_map(
        per_device, mesh=mesh, in_specs=in_specs, out_specs=out_specs, check_vma=False
    )
```

```python
import functools

import jax
import jax.numpy as jnp
from jax import lax
from jax.experimental import pallas as pl
from jax.experimental.pallas import tpu as pltpu
from jax.sharding import PartitionSpec as P

F32 = jnp.float32
BF16 = jnp.bfloat16
NT = (((1,), (1,)), ((), ()))
TN = (((0,), (0,)), ((), ()))
NN = (((1,), (0,)), ((), ()))

VMEM = pl.BlockSpec(memory_space=pltpu.VMEM)
HBM = pl.BlockSpec(memory_space=pltpu.HBM)
VMEM_LIMIT = 40 * 1024 * 1024


def dot(left, right, dims=NN):
    return lax.dot_general(left, right, dims, preferred_element_type=F32)


def in_vmem(array):
    return pltpu.with_memory_space_constraint(array, pltpu.VMEM)


def in_hbm(array):
    return pltpu.with_memory_space_constraint(array, pltpu.HBM)


def vmem_out(shape, dtype):
    return pltpu.VMEM(shape, dtype)


def call(kernel, outs, ins, out_specs, in_specs, scratch=(), cost=None):
    return pl.pallas_call(
        kernel,
        out_shape=outs,
        in_specs=in_specs,
        out_specs=out_specs,
        scratch_shapes=list(scratch),
        compiler_params=pltpu.CompilerParams(vmem_limit_bytes=VMEM_LIMIT),
        cost_estimate=pl.CostEstimate(flops=cost[0], bytes_accessed=cost[1], transcendentals=0),
    )(*ins)


def block_rows(images):
    return -(-2 * images // 8) * 8


def rows_kernel(
    split_chips, tokens, router_t, d_out, send, tok, dout, disp_out, comb_out, block, sems
):
    images = tok.shape[0]
    slots = router_t.shape[0]
    fetch_tok = [
        pltpu.make_async_copy(tokens.at[b], tok.at[b], sems.at[b]) for b in range(images)
    ]
    fetch_dout = [
        pltpu.make_async_copy(d_out.at[b], dout.at[b], sems.at[images + b]) for b in range(images)
    ]
    for copy in fetch_tok + fetch_dout:
        copy.start()
    block[...] = jnp.zeros_like(block)
    combs = []
    for b in range(images):
        fetch_tok[b].wait()
        logits = dot(router_t[...], tok[b], NT)
        exps = jnp.exp(logits - jnp.max(logits, axis=1, keepdims=True))
        disp = exps / jnp.sum(exps, axis=1, keepdims=True)
        exps = jnp.exp(logits - jnp.max(logits, axis=0, keepdims=True))
        comb = exps / jnp.sum(exps, axis=0, keepdims=True)
        disp_out[b] = disp
        comb_out[b] = comb
        combs.append(comb.astype(BF16))
        block[:, b, :] = dot(disp.astype(BF16), tok[b])
    for b in range(images):
        fetch_dout[b].wait()
        block[:, images + b, :] = dot(combs[b], dout[b])
    for slot in range(slots):
        rows = block[slot].astype(BF16)
        for chip in range(split_chips):
            send[slot * split_chips + chip] = rows


def experts_kernel(images, near, far, w_in, w_out, own, other, hid_out, grad_out):
    chips, rows, width = near.shape
    half = chips * rows
    x = jnp.concatenate([near[...].reshape(half, width), far[...].reshape(half, width)], axis=0)
    pre = dot(x, w_in[...])
    grad_hidden = dot(x, w_out[...], NT)
    place = lax.broadcasted_iota(jnp.int32, pre.shape, 0) % rows
    slot_row = place < images
    grad_hidden = pltpu.roll(grad_hidden, 2 * half - images, 0)
    scale = 0.7978845608028654
    square = pre * pre
    tanh = jnp.tanh(scale * pre * (1.0 + 0.044715 * square))
    cdf = 0.5 * (1.0 + tanh)
    slope = cdf + (0.5 * scale) * pre * (1.0 - tanh * tanh) * (1.0 + (3 * 0.044715) * square)
    hidden = jnp.where(slot_row, pre * cdf, 0.0)
    grad_pre = jnp.where(slot_row, slope * grad_hidden, 0.0)
    grad_low = pltpu.roll(grad_pre, images, 0).astype(BF16)
    shares = dot(hidden.astype(BF16), w_out[...]) + dot(grad_low, w_in[...], NT)
    own[...] = shares[:half].reshape(own.shape)
    other[...] = shares[half:].astype(BF16).reshape(other.shape)
    hid_out[...] = pltpu.roll(hidden, images, 0).astype(BF16)
    grad_out[...] = grad_pre.astype(BF16)


def add_kernel(own, received, total):
    total[...] = (own[...] + received[...].astype(F32)).astype(BF16)


def weights_kernel(near, far, hid, grad, g_in, g_out, buf_in, buf_out, sem_in, sem_out):
    chips, rows, width = near.shape
    half = chips * rows
    parts = buf_in.shape[0]
    step_in = g_in.shape[0] // parts
    step_out = g_out.shape[0] // parts
    x = jnp.concatenate([near[...].reshape(half, width), far[...].reshape(half, width)], axis=0)
    copies = []
    for i in range(parts):
        buf_out[i] = dot(hid[:, i * step_out : (i + 1) * step_out], x, TN).astype(BF16)
        copy = pltpu.make_async_copy(
            buf_out.at[i], g_out.at[pl.ds(i * step_out, step_out)], sem_out.at[i]
        )
        copy.start()
        copies.append(copy)
        buf_in[i] = dot(x[:, i * step_in : (i + 1) * step_in], grad[...], TN).astype(BF16)
        copy = pltpu.make_async_copy(
            buf_in.at[i], g_in.at[pl.ds(i * step_in, step_in)], sem_in.at[i]
        )
        copy.start()
        copies.append(copy)
    for copy in copies:
        copy.wait()


def logits_kernel(split_chips, shares, tok, dout, disp, comb, router_t, terms_out, left, right):
    images, slots, _ = disp.shape
    rows = shares.shape[1]
    summed = []
    for slot in range(slots):
        total = shares[slot * split_chips].astype(F32)
        for chip in range(1, split_chips):
            total = total + shares[slot * split_chips + chip].astype(F32)
        summed.append(total)
    stacked = jnp.concatenate(summed, axis=0).astype(BF16)
    terms = None
    for b in range(images):
        by_dout = dot(stacked, dout[b], NT)
        by_tok = dot(stacked, tok[b], NT)
        grad_comb = jnp.concatenate(
            [by_dout[s * rows + b : s * rows + b + 1] for s in range(slots)], axis=0
        )
        grad_disp = jnp.concatenate(
            [by_tok[s * rows + images + b : s * rows + images + b + 1] for s in range(slots)],
            axis=0,
        )
        dispatch = disp[b]
        combine = comb[b]
        grad_logits = dispatch * (
            grad_disp - jnp.sum(dispatch * grad_disp, axis=1, keepdims=True)
        ) + combine * (grad_comb - jnp.sum(combine * grad_comb, axis=0, keepdims=True))
        term = dot(grad_logits.astype(BF16), tok[b])
        terms = term if terms is None else terms + term
        left[b] = jnp.concatenate([dispatch, grad_logits], axis=0)
        right[b] = jnp.concatenate(
            [summed[s][images + b : images + b + 1] for s in range(slots)]
            + [router_t[...].astype(F32)],
            axis=0,
        )
    terms_out[...] = jnp.broadcast_to(terms.astype(BF16)[None], terms_out.shape)


def tokens_kernel(left, right, grad_tokens, buf, sems):
    images, parts = buf.shape[:2]
    step = buf.shape[2]
    copies = []
    for b in range(images):
        rhs = right[b].astype(BF16)
        for i in range(parts):
            lhs = left[b, :, i * step : (i + 1) * step].astype(BF16)
            buf[b, i] = dot(lhs, rhs, TN).astype(BF16)
            copy = pltpu.make_async_copy(
                buf.at[b, i], grad_tokens.at[b, pl.ds(i * step, step)], sems.at[b, i]
            )
            copy.start()
            copies.append(copy)
    for copy in copies:
        copy.wait()


def swap_chips(blocks):
    count = lax.axis_size("expert")
    groups = [list(range(core, count, 2)) for core in range(2)]
    return lax.all_to_all(
        blocks, "expert", split_axis=0, concat_axis=0, axis_index_groups=groups, tiled=True
    )


def swap_cores(block):
    count = lax.axis_size("expert")
    return lax.ppermute(block, "expert", [(device, device ^ 1) for device in range(count)])


def per_device(tokens, router, w_in, w_out, d_out):
    devices = lax.axis_size("expert")
    chips = devices // 2
    slots = router.shape[1]
    split_chips = chips // slots
    images, count, width = tokens.shape
    hidden_units = w_in.shape[2]
    rows = block_rows(images)
    router_t = router.T
    big = images * count * width

    send, tok, dout, disp, comb = call(
        functools.partial(rows_kernel, split_chips),
        (
            vmem_out((chips, rows, width), BF16),
            vmem_out((images, count, width), BF16),
            vmem_out((images, count, width), BF16),
            vmem_out((images, slots, count), F32),
            vmem_out((images, slots, count), F32),
        ),
        (in_hbm(tokens), router_t, in_hbm(d_out)),
        (VMEM,) * 5,
        (HBM, VMEM, HBM),
        [pltpu.VMEM((slots, rows, width), F32), pltpu.SemaphoreType.DMA((2 * images,))],
        (6 * slots * big, 4 * big),
    )
    near = swap_chips(send)
    far = swap_cores(near)
    near, far = in_vmem(near), in_vmem(far)
    half = chips * rows
    own, other, hid, grad = call(
        functools.partial(experts_kernel, images),
        (
            vmem_out((chips, rows, width), F32),
            vmem_out((chips, rows, width), BF16),
            vmem_out((2 * half, hidden_units), BF16),
            vmem_out((2 * half, hidden_units), BF16),
        ),
        (near, far, in_vmem(w_in[0]), in_vmem(w_out[0])),
        (VMEM,) * 4,
        (VMEM,) * 4,
        (),
        (8 * 2 * half * width * hidden_units, 4 * width * hidden_units),
    )
    total = call(
        add_kernel,
        vmem_out((chips, rows, width), BF16),
        (in_vmem(own), in_vmem(swap_cores(other))),
        VMEM,
        (VMEM,) * 2,
        (),
        (half * width, 8 * half * width),
    )
    shares = swap_chips(total)
    parts = 5
    g_in, g_out = call(
        weights_kernel,
        (
            jax.ShapeDtypeStruct((width, hidden_units), BF16),
            jax.ShapeDtypeStruct((hidden_units, width), BF16),
        ),
        (near, far, in_vmem(hid), in_vmem(grad)),
        (HBM,) * 2,
        (VMEM,) * 4,
        [
            pltpu.VMEM((parts, width // parts, hidden_units), BF16),
            pltpu.VMEM((parts, hidden_units // parts, width), BF16),
            pltpu.SemaphoreType.DMA((parts,)),
            pltpu.SemaphoreType.DMA((parts,)),
        ],
        (8 * half * width * hidden_units, 4 * width * hidden_units),
    )
    terms, left, right = call(
        functools.partial(logits_kernel, split_chips),
        (
            vmem_out((devices, slots, width), BF16),
            vmem_out((images, 2 * slots, count), F32),
            vmem_out((images, 2 * slots, width), F32),
        ),
        (
            in_vmem(shares),
            in_vmem(tok),
            in_vmem(dout),
            in_vmem(disp),
            in_vmem(comb),
            router_t,
        ),
        (VMEM,) * 3,
        (VMEM,) * 6,
        (),
        (6 * slots * big, 4 * big),
    )
    terms = lax.all_to_all(terms, "expert", split_axis=0, concat_axis=0, tiled=True)
    pieces = 2
    grad_tokens = call(
        tokens_kernel,
        jax.ShapeDtypeStruct(tokens.shape, BF16),
        (in_vmem(left), in_vmem(right)),
        HBM,
        (VMEM,) * 2,
        [
            pltpu.VMEM((images, pieces, count // pieces, width), BF16),
            pltpu.SemaphoreType.DMA((images, pieces)),
        ],
        (4 * slots * big, 2 * big),
    )
    grad_router = jnp.sum(terms.astype(F32), axis=0).T
    return (grad_tokens, g_in[None], g_out[None], grad_router)


def solution(mesh):
    in_specs = (
        P(("groups", "expert"), None, None),
        P(None, "groups"),
        P(("groups", "expert"), None, None),
        P(("groups", "expert"), None, None),
        P(("groups", "expert"), None, None),
    )
    out_specs = (
        P(("groups", "expert"), None, None),
        P(("groups", "expert"), None, None),
        P(("groups", "expert"), None, None),
        P(None, "groups"),
    )
    return jax.shard_map(
        per_device, mesh=mesh, in_specs=in_specs, out_specs=out_specs, check_vma=False
    )
```

```python
import functools

import jax
import jax.numpy as jnp
from jax import lax
from jax.experimental import pallas as pl
from jax.experimental.pallas import tpu as pltpu
from jax.sharding import PartitionSpec as P

F32 = jnp.float32
BF16 = jnp.bfloat16
NT = (((1,), (1,)), ((), ()))
TN = (((0,), (0,)), ((), ()))
NN = (((1,), (0,)), ((), ()))

VMEM = pl.BlockSpec(memory_space=pltpu.VMEM)
HBM = pl.BlockSpec(memory_space=pltpu.HBM)
VMEM_LIMIT = 40 * 1024 * 1024


def dot(left, right, dims=NN):
    return lax.dot_general(left, right, dims, preferred_element_type=F32)


def in_vmem(array):
    return pltpu.with_memory_space_constraint(array, pltpu.VMEM)


def in_hbm(array):
    return pltpu.with_memory_space_constraint(array, pltpu.HBM)


def vmem_out(shape, dtype):
    return pltpu.VMEM(shape, dtype)


def call(kernel, outs, ins, out_specs, in_specs, scratch=(), cost=None):
    return pl.pallas_call(
        kernel,
        out_shape=outs,
        in_specs=in_specs,
        out_specs=out_specs,
        scratch_shapes=list(scratch),
        compiler_params=pltpu.CompilerParams(vmem_limit_bytes=VMEM_LIMIT),
        cost_estimate=pl.CostEstimate(flops=cost[0], bytes_accessed=cost[1], transcendentals=0),
    )(*ins)


def block_shape(images, width):
    extra = width // 5
    main = width - extra
    ends = -(-2 * images * extra // main)
    return -(-(2 * images + ends) // 8) * 8, main, extra


def end_place(images, main, extra, row):
    per = main // extra
    return 2 * images + row // per, row % per * extra


def pack(images, scratch, values):
    main = scratch.shape[2]
    extra = values.shape[2] - main
    scratch[...] = values[:, :, :main]
    for row in range(2 * images):
        to, column = end_place(images, main, extra, row)
        scratch[:, to, column : column + extra] = values[:, row, main:]


def unpack(images, scratch, values):
    main = values.shape[2]
    extra = scratch.shape[2]
    scratch[...] = jnp.zeros_like(scratch)
    for row in range(2 * images):
        at, column = end_place(images, main, extra, row)
        scratch[:, row, :] = values[:, at, column : column + extra]


def rows_kernel(
    split_chips,
    tokens,
    router_hbm,
    d_out,
    send,
    tok,
    dout,
    disp_out,
    comb_out,
    router_t,
    block,
    sems,
    router_sem,
):
    images = tok.shape[0]
    slots = router_t.shape[0]
    main = send.shape[2]
    extra = tok.shape[2] - main
    fetch_router = pltpu.make_async_copy(router_hbm, router_t, router_sem)
    fetch_router.start()
    fetch_tok = [
        pltpu.make_async_copy(tokens.at[b], tok.at[b], sems.at[b]) for b in range(images)
    ]
    fetch_dout = [
        pltpu.make_async_copy(d_out.at[b], dout.at[b], sems.at[images + b]) for b in range(images)
    ]
    for copy in fetch_tok + fetch_dout:
        copy.start()
    block[...] = jnp.zeros_like(block)

    def put(row, values):
        to, column = end_place(images, main, extra, row)
        block[:, row, :] = values[:, :main]
        block[:, to, column : column + extra] = values[:, main:]

    fetch_router.wait()
    logits = []
    for b in range(images):
        fetch_tok[b].wait()
        logits.append(dot(router_t[...], tok[b], NT))
    disps = []
    combs = []
    for b in range(images):
        exps = jnp.exp(logits[b] - jnp.max(logits[b], axis=1, keepdims=True))
        disps.append(exps / jnp.sum(exps, axis=1, keepdims=True))
        exps = jnp.exp(logits[b] - jnp.max(logits[b], axis=0, keepdims=True))
        combs.append(exps / jnp.sum(exps, axis=0, keepdims=True))
        disp_out[b] = disps[b]
        comb_out[b] = combs[b]
    for b in range(images):
        put(b, dot(disps[b].astype(BF16), tok[b]))
    for b in range(images):
        fetch_dout[b].wait()
        put(images + b, dot(combs[b].astype(BF16), dout[b]))
    for slot in range(slots):
        rows = block[slot].astype(BF16)
        for chip in range(split_chips):
            send[slot * split_chips + chip] = rows


def experts_kernel(images, near, far, w_in, w_out, other, x_out, hid_out, grad_out, ends, packed):
    chips, rows, main = near.shape
    half = chips * rows
    width = x_out.shape[1]
    for i, blocks in enumerate((near, far)):
        unpack(images, ends.at[pl.ds(i * chips, chips)], blocks[...].astype(F32))
    x = jnp.concatenate(
        [
            jnp.concatenate(
                [near[...].reshape(half, main), far[...].reshape(half, main)], axis=0
            ),
            ends[...].reshape(2 * half, width - main).astype(BF16),
        ],
        axis=1,
    )
    x_out[...] = x
    pre = dot(x, w_in[...])
    grad_hidden = dot(x, w_out[...], NT)
    place = lax.broadcasted_iota(jnp.int32, pre.shape, 0) % rows
    slot_row = place < images
    grad_hidden = pltpu.roll(grad_hidden, 2 * half - images, 0)
    scale = 0.7978845608028654
    square = pre * pre
    tanh = jnp.tanh(scale * pre * (1.0 + 0.044715 * square))
    cdf = 0.5 * (1.0 + tanh)
    slope = cdf + (0.5 * scale) * pre * (1.0 - tanh * tanh) * (1.0 + (3 * 0.044715) * square)
    hidden = jnp.where(slot_row, pre * cdf, 0.0).astype(BF16)
    grad_pre = jnp.where(slot_row, slope * grad_hidden, 0.0)
    grad_low = pltpu.roll(grad_pre, images, 0).astype(BF16)
    hid_out[...] = hidden
    grad_out[...] = grad_low
    shares = dot(hidden[half:], w_out[...]) + dot(grad_low[half:], w_in[...], NT)
    pack(images, packed, shares.reshape(chips, rows, width))
    other[...] = packed[...].astype(BF16)


def own_kernel(images, hid, grad, w_in, w_out, own):
    chips, rows, _ = own.shape
    half = chips * rows
    shares = dot(hid[:half], w_out[...]) + dot(grad[:half], w_in[...], NT)
    pack(images, own, shares.reshape(chips, rows, shares.shape[1]))


def add_kernel(own, received, total):
    total[...] = (own[...] + received[...].astype(F32)).astype(BF16)


def weights_kernel(images, x, hid, grad, g_in, g_out, buf_in, buf_out, sem_in, sem_out):
    parts = buf_in.shape[0]
    step_in = g_in.shape[0] // parts
    step_out = g_out.shape[0] // parts
    count = x.shape[0]
    hid_low = pltpu.roll(hid[...].astype(F32), images, 0).astype(BF16)
    grad_high = pltpu.roll(grad[...].astype(F32), count - images, 0).astype(BF16)
    copies = []
    for i in range(parts):
        buf_out[i] = dot(hid_low[:, i * step_out : (i + 1) * step_out], x[...], TN).astype(BF16)
        copy = pltpu.make_async_copy(
            buf_out.at[i], g_out.at[pl.ds(i * step_out, step_out)], sem_out.at[i]
        )
        copy.start()
        copies.append(copy)
        buf_in[i] = dot(x[:, i * step_in : (i + 1) * step_in], grad_high, TN).astype(BF16)
        copy = pltpu.make_async_copy(
            buf_in.at[i], g_in.at[pl.ds(i * step_in, step_in)], sem_in.at[i]
        )
        copy.start()
        copies.append(copy)
    for copy in copies:
        copy.wait()


def logits_kernel(
    split_chips, shares, tok, dout, disp, comb, router_t, terms_out, left, right, ends
):
    images, slots, count = disp.shape
    chips, rows, main = shares.shape
    width = tok.shape[2]
    summed = []
    for slot in range(slots):
        total = shares[slot * split_chips].astype(F32)
        for chip in range(1, split_chips):
            total = total + shares[slot * split_chips + chip].astype(F32)
        summed.append(total)
    unpack(images, ends, jnp.stack(summed))
    stacked = jnp.concatenate(
        [
            jnp.concatenate(summed, axis=0),
            ends[...].reshape(slots * rows, width - main),
        ],
        axis=1,
    )
    stacked_b = stacked.astype(BF16)
    tok_all = tok[...].reshape(images * count, width)
    by_dout = dot(stacked_b, dout[...].reshape(images * count, width), NT)
    by_tok = dot(stacked_b, tok_all, NT)
    grads = []
    for b in range(images):
        span = slice(b * count, (b + 1) * count)
        grad_comb = jnp.concatenate(
            [by_dout[s * rows + b : s * rows + b + 1, span] for s in range(slots)], axis=0
        )
        grad_disp = jnp.concatenate(
            [
                by_tok[s * rows + images + b : s * rows + images + b + 1, span]
                for s in range(slots)
            ],
            axis=0,
        )
        dispatch = disp[b]
        combine = comb[b]
        grads.append(
            dispatch * (grad_disp - jnp.sum(dispatch * grad_disp, axis=1, keepdims=True))
            + combine * (grad_comb - jnp.sum(combine * grad_comb, axis=0, keepdims=True))
        )
    terms = dot(jnp.concatenate(grads, axis=1).astype(BF16), tok_all).astype(BF16)
    terms_out[...] = jnp.broadcast_to(terms[None], terms_out.shape)
    for b in range(images):
        left[b] = jnp.concatenate([disp[b], grads[b]], axis=0)
        right[b] = jnp.concatenate(
            [stacked[s * rows + images + b : s * rows + images + b + 1] for s in range(slots)]
            + [router_t[...].astype(F32)],
            axis=0,
        )


def tokens_kernel(left, right, grad_tokens, buf, sems):
    images, parts = buf.shape[:2]
    step = buf.shape[2]
    copies = []
    for b in range(images):
        rhs = right[b].astype(BF16)
        for i in range(parts):
            lhs = left[b, :, i * step : (i + 1) * step].astype(BF16)
            buf[b, i] = dot(lhs, rhs, TN).astype(BF16)
            copy = pltpu.make_async_copy(
                buf.at[b, i], grad_tokens.at[b, pl.ds(i * step, step)], sems.at[b, i]
            )
            copy.start()
            copies.append(copy)
    for copy in copies:
        copy.wait()


def sum_kernel(terms, total):
    total[...] = jnp.sum(terms[...].astype(F32), axis=0)


def swap_chips(blocks):
    count = lax.axis_size("expert")
    groups = [list(range(core, count, 2)) for core in range(2)]
    return lax.all_to_all(
        blocks, "expert", split_axis=0, concat_axis=0, axis_index_groups=groups, tiled=True
    )


def swap_cores(block):
    count = lax.axis_size("expert")
    return lax.ppermute(block, "expert", [(device, device ^ 1) for device in range(count)])


def per_device(tokens, router, w_in, w_out, d_out):
    devices = lax.axis_size("expert")
    chips = devices // 2
    slots = router.shape[1]
    split_chips = chips // slots
    images, count, width = tokens.shape
    hidden_units = w_in.shape[2]
    rows, main, extra = block_shape(images, width)
    half = chips * rows
    router_t = router.T
    big = images * count * width
    weight = width * hidden_units

    send, tok, dout, disp, comb = call(
        functools.partial(rows_kernel, split_chips),
        (
            vmem_out((chips, rows, main), BF16),
            vmem_out((images, count, width), BF16),
            vmem_out((images, count, width), BF16),
            vmem_out((images, slots, count), F32),
            vmem_out((images, slots, count), F32),
        ),
        (in_hbm(tokens), in_hbm(router_t), in_hbm(d_out)),
        (VMEM,) * 5,
        (HBM,) * 3,
        [
            pltpu.VMEM((slots, width), BF16),
            pltpu.VMEM((slots, rows, main), F32),
            pltpu.SemaphoreType.DMA((2 * images,)),
            pltpu.SemaphoreType.DMA,
        ],
        (6 * slots * big, 4 * big),
    )
    send, w_one, w_two = lax.optimization_barrier((send, w_in, w_out))
    w_one, w_two = in_vmem(w_one[0]), in_vmem(w_two[0])
    near = swap_chips(send)
    far = swap_cores(near)
    other, x, hid, grad = call(
        functools.partial(experts_kernel, images),
        (
            vmem_out((chips, rows, main), BF16),
            vmem_out((2 * half, width), BF16),
            vmem_out((2 * half, hidden_units), BF16),
            vmem_out((2 * half, hidden_units), BF16),
        ),
        (in_vmem(near), in_vmem(far), w_one, w_two),
        (VMEM,) * 4,
        (VMEM,) * 4,
        [
            pltpu.VMEM((2 * chips, rows, extra), F32),
            pltpu.VMEM((chips, rows, main), F32),
        ],
        (12 * half * weight, 4 * weight),
    )
    received = swap_cores(other)
    own = call(
        functools.partial(own_kernel, images),
        vmem_out((chips, rows, main), F32),
        (in_vmem(hid), in_vmem(grad), w_one, w_two),
        VMEM,
        (VMEM,) * 4,
        (),
        (4 * half * weight, 4 * weight),
    )
    total = call(
        add_kernel,
        vmem_out((chips, rows, main), BF16),
        (in_vmem(own), in_vmem(received)),
        VMEM,
        (VMEM,) * 2,
        (),
        (half * main, 8 * half * main),
    )
    shares = swap_chips(total)
    parts = 5
    g_in, g_out = call(
        functools.partial(weights_kernel, images),
        (
            jax.ShapeDtypeStruct((width, hidden_units), BF16),
            jax.ShapeDtypeStruct((hidden_units, width), BF16),
        ),
        (in_vmem(x), in_vmem(hid), in_vmem(grad)),
        (HBM,) * 2,
        (VMEM,) * 3,
        [
            pltpu.VMEM((parts, width // parts, hidden_units), BF16),
            pltpu.VMEM((parts, hidden_units // parts, width), BF16),
            pltpu.SemaphoreType.DMA((parts,)),
            pltpu.SemaphoreType.DMA((parts,)),
        ],
        (8 * half * weight, 4 * weight),
    )
    terms, left, right = call(
        functools.partial(logits_kernel, split_chips),
        (
            vmem_out((devices, slots, width), BF16),
            vmem_out((images, 2 * slots, count), F32),
            vmem_out((images, 2 * slots, width), F32),
        ),
        (
            in_vmem(shares),
            in_vmem(tok),
            in_vmem(dout),
            in_vmem(disp),
            in_vmem(comb),
            router_t,
        ),
        (VMEM,) * 3,
        (VMEM,) * 6,
        [pltpu.VMEM((slots, rows, extra), F32)],
        (6 * slots * big, 4 * big),
    )
    terms = lax.all_to_all(terms, "expert", split_axis=0, concat_axis=0, tiled=True)
    pieces = 2
    grad_tokens = call(
        tokens_kernel,
        jax.ShapeDtypeStruct(tokens.shape, BF16),
        (in_vmem(left), in_vmem(right)),
        HBM,
        (VMEM,) * 2,
        [
            pltpu.VMEM((images, pieces, count // pieces, width), BF16),
            pltpu.SemaphoreType.DMA((images, pieces)),
        ],
        (4 * slots * big, 2 * big),
    )
    grad_router = call(
        sum_kernel,
        jax.ShapeDtypeStruct((slots, width), F32),
        (in_vmem(terms),),
        VMEM,
        (VMEM,),
        (),
        (devices * slots * width, 2 * devices * slots * width),
    )
    return (grad_tokens, g_in[None], g_out[None], grad_router.T)


def solution(mesh):
    in_specs = (
        P(("groups", "expert"), None, None),
        P(None, "groups"),
        P(("groups", "expert"), None, None),
        P(("groups", "expert"), None, None),
        P(("groups", "expert"), None, None),
    )
    out_specs = (
        P(("groups", "expert"), None, None),
        P(("groups", "expert"), None, None),
        P(("groups", "expert"), None, None),
        P(None, "groups"),
    )
    return jax.shard_map(
        per_device, mesh=mesh, in_specs=in_specs, out_specs=out_specs, check_vma=False
    )
```

```python
import functools

import jax
import jax.numpy as jnp
from jax import lax
from jax.experimental import pallas as pl
from jax.experimental.pallas import tpu as pltpu
from jax.sharding import PartitionSpec as P

F32 = jnp.float32
BF16 = jnp.bfloat16
NT = (((1,), (1,)), ((), ()))
TN = (((0,), (0,)), ((), ()))
NN = (((1,), (0,)), ((), ()))

VMEM = pl.BlockSpec(memory_space=pltpu.VMEM)
HBM = pl.BlockSpec(memory_space=pltpu.HBM)
MIB = 1024 * 1024


def dot(left, right, dims=NN):
    return lax.dot_general(left, right, dims, preferred_element_type=F32)


def in_vmem(array):
    return pltpu.with_memory_space_constraint(array, pltpu.VMEM)


def in_hbm(array):
    return pltpu.with_memory_space_constraint(array, pltpu.HBM)


def vmem_out(shape, dtype):
    return pltpu.VMEM(shape, dtype)


def call(kernel, outs, ins, out_specs, in_specs, scratch=(), cost=None, limit=40 * MIB):
    return pl.pallas_call(
        kernel,
        out_shape=outs,
        in_specs=in_specs,
        out_specs=out_specs,
        scratch_shapes=list(scratch),
        compiler_params=pltpu.CompilerParams(vmem_limit_bytes=limit),
        cost_estimate=pl.CostEstimate(flops=cost[0], bytes_accessed=cost[1], transcendentals=0),
    )(*ins)


def block_shape(images, width):
    extra = width // 5
    main = width - extra
    ends = -(-2 * images * extra // main)
    return -(-(2 * images + ends) // 8) * 8, main, extra


def end_place(images, main, extra, row):
    per = main // extra
    return 2 * images + row // per, row % per * extra


def pack(images, scratch, values):
    main = scratch.shape[2]
    extra = values.shape[2] - main
    scratch[...] = values[:, :, :main]
    for row in range(2 * images):
        to, column = end_place(images, main, extra, row)
        scratch[:, to, column : column + extra] = values[:, row, main:]


def unpack(images, scratch, values):
    main = values.shape[2]
    extra = scratch.shape[2]
    scratch[...] = jnp.zeros_like(scratch)
    for row in range(2 * images):
        at, column = end_place(images, main, extra, row)
        scratch[:, row, :] = values[:, at, column : column + extra]


def rows_kernel(
    split_chips,
    tokens,
    router_hbm,
    d_out,
    w_in,
    w_out,
    send,
    tok,
    dout,
    disp_out,
    comb_out,
    w_one,
    w_two,
    router_t,
    block,
    sems,
    other_sems,
):
    images = tok.shape[0]
    slots = router_t.shape[0]
    main = send.shape[2]
    extra = tok.shape[2] - main
    fetch_router = pltpu.make_async_copy(router_hbm, router_t, other_sems.at[0])
    fetch_router.start()
    fetch_tok = [
        pltpu.make_async_copy(tokens.at[b], tok.at[b], sems.at[b]) for b in range(images)
    ]
    fetch_dout = [
        pltpu.make_async_copy(d_out.at[b], dout.at[b], sems.at[images + b]) for b in range(images)
    ]
    fetch_weights = [
        pltpu.make_async_copy(w_in, w_one, other_sems.at[1]),
        pltpu.make_async_copy(w_out, w_two, other_sems.at[2]),
    ]
    for copy in fetch_tok:
        copy.start()
    block[...] = jnp.zeros_like(block)

    def put(row, values):
        to, column = end_place(images, main, extra, row)
        block[:, row, :] = values[:, :main]
        block[:, to, column : column + extra] = values[:, main:]

    fetch_router.wait()
    logits = []
    for b in range(images):
        fetch_tok[b].wait()
        if b == 0:
            for copy in fetch_dout:
                copy.start()
        if b == images - 1:
            for copy in fetch_weights:
                copy.start()
        logits.append(dot(router_t[...], tok[b], NT))
    disps = []
    combs = []
    for b in range(images):
        exps = jnp.exp(logits[b] - jnp.max(logits[b], axis=1, keepdims=True))
        disps.append(exps * (1.0 / jnp.sum(exps, axis=1, keepdims=True)))
        exps = jnp.exp(logits[b] - jnp.max(logits[b], axis=0, keepdims=True))
        combs.append(exps * (1.0 / jnp.sum(exps, axis=0, keepdims=True)))
        disp_out[b] = disps[b]
        comb_out[b] = combs[b]
    for b in range(images):
        put(b, dot(disps[b].astype(BF16), tok[b]))
    for b in range(images):
        fetch_dout[b].wait()
        put(images + b, dot(combs[b].astype(BF16), dout[b]))
    for slot in range(slots):
        rows = block[slot].astype(BF16)
        for chip in range(split_chips):
            send[slot * split_chips + chip] = rows
    for copy in fetch_weights:
        copy.wait()


def experts_kernel(images, near, far, w_in, w_out, other, x_out, hid_out, grad_out, ends, packed):
    chips, rows, main = near.shape
    half = chips * rows
    width = x_out.shape[1]
    for i, blocks in enumerate((near, far)):
        unpack(images, ends.at[pl.ds(i * chips, chips)], blocks[...].astype(F32))
    x = jnp.concatenate(
        [
            jnp.concatenate(
                [near[...].reshape(half, main), far[...].reshape(half, main)], axis=0
            ),
            ends[...].reshape(2 * half, width - main).astype(BF16),
        ],
        axis=1,
    )
    x_out[...] = x
    pre = dot(x, w_in[...])
    grad_hidden = dot(x, w_out[...], NT)
    place = lax.broadcasted_iota(jnp.int32, pre.shape, 0) % rows
    slot_row = place < images
    grad_hidden = pltpu.roll(grad_hidden, 2 * half - images, 0)
    scale = 0.7978845608028654
    square = pre * pre
    tanh = jnp.tanh(scale * pre * (1.0 + 0.044715 * square))
    cdf = 0.5 * (1.0 + tanh)
    slope = cdf + (0.5 * scale) * pre * (1.0 - tanh * tanh) * (1.0 + (3 * 0.044715) * square)
    hidden = jnp.where(slot_row, pre * cdf, 0.0).astype(BF16)
    grad_pre = jnp.where(slot_row, slope * grad_hidden, 0.0)
    grad_low = pltpu.roll(grad_pre, images, 0).astype(BF16)
    hid_out[...] = hidden
    grad_out[...] = grad_low
    shares = dot(hidden[half:], w_out[...]) + dot(grad_low[half:], w_in[...], NT)
    pack(images, packed, shares.reshape(chips, rows, width))
    other[...] = packed[...].astype(BF16)


def own_kernel(images, hid, grad, w_in, w_out, own):
    chips, rows, _ = own.shape
    half = chips * rows
    shares = dot(hid[:half], w_out[...]) + dot(grad[:half], w_in[...], NT)
    pack(images, own, shares.reshape(chips, rows, shares.shape[1]))


def add_kernel(own, received, total):
    total[...] = (own[...] + received[...].astype(F32)).astype(BF16)


def weights_kernel(images, x, hid, grad, g_in, g_out, buf_in, buf_out, sem_in, sem_out):
    parts = buf_in.shape[0]
    step_in = g_in.shape[0] // parts
    step_out = g_out.shape[0] // parts
    count = x.shape[0]
    hid_low = pltpu.roll(hid[...].astype(F32), images, 0).astype(BF16)
    grad_high = pltpu.roll(grad[...].astype(F32), count - images, 0).astype(BF16)
    copies = []
    for i in range(parts):
        buf_out[i] = dot(hid_low[:, i * step_out : (i + 1) * step_out], x[...], TN).astype(BF16)
        copy = pltpu.make_async_copy(
            buf_out.at[i], g_out.at[pl.ds(i * step_out, step_out)], sem_out.at[i]
        )
        copy.start()
        copies.append(copy)
        buf_in[i] = dot(x[:, i * step_in : (i + 1) * step_in], grad_high, TN).astype(BF16)
        copy = pltpu.make_async_copy(
            buf_in.at[i], g_in.at[pl.ds(i * step_in, step_in)], sem_in.at[i]
        )
        copy.start()
        copies.append(copy)
    for copy in copies:
        copy.wait()


def logits_kernel(
    split_chips, shares, tok, dout, disp, comb, router_t, terms_out, left, right, ends
):
    images, slots, count = disp.shape
    chips, rows, main = shares.shape
    width = tok.shape[2]
    summed = []
    for slot in range(slots):
        total = shares[slot * split_chips].astype(F32)
        for chip in range(1, split_chips):
            total = total + shares[slot * split_chips + chip].astype(F32)
        summed.append(total)
    unpack(images, ends, jnp.stack(summed))
    stacked = jnp.concatenate(
        [
            jnp.concatenate(summed, axis=0),
            ends[...].reshape(slots * rows, width - main),
        ],
        axis=1,
    )
    stacked_b = stacked.astype(BF16)
    tok_all = tok[...].reshape(images * count, width)
    by_dout = dot(stacked_b, dout[...].reshape(images * count, width), NT)
    by_tok = dot(stacked_b, tok_all, NT)
    grads = []
    for b in range(images):
        span = slice(b * count, (b + 1) * count)
        grad_comb = jnp.concatenate(
            [by_dout[s * rows + b : s * rows + b + 1, span] for s in range(slots)], axis=0
        )
        grad_disp = jnp.concatenate(
            [
                by_tok[s * rows + images + b : s * rows + images + b + 1, span]
                for s in range(slots)
            ],
            axis=0,
        )
        dispatch = disp[b]
        combine = comb[b]
        grads.append(
            dispatch * (grad_disp - jnp.sum(dispatch * grad_disp, axis=1, keepdims=True))
            + combine * (grad_comb - jnp.sum(combine * grad_comb, axis=0, keepdims=True))
        )
    terms = dot(jnp.concatenate(grads, axis=1).astype(BF16), tok_all).astype(BF16)
    terms_out[...] = jnp.broadcast_to(terms[None], terms_out.shape)
    for b in range(images):
        left[b] = jnp.concatenate([disp[b], grads[b]], axis=0)
        right[b] = jnp.concatenate(
            [stacked[s * rows + images + b : s * rows + images + b + 1] for s in range(slots)]
            + [router_t[...].astype(F32)],
            axis=0,
        )


def tokens_kernel(left, right, grad_tokens, buf, sems):
    images, parts = buf.shape[:2]
    step = buf.shape[2]
    copies = []
    for b in range(images):
        rhs = right[b].astype(BF16)
        for i in range(parts):
            lhs = left[b, :, i * step : (i + 1) * step].astype(BF16)
            buf[b, i] = dot(lhs, rhs, TN).astype(BF16)
            copy = pltpu.make_async_copy(
                buf.at[b, i], grad_tokens.at[b, pl.ds(i * step, step)], sems.at[b, i]
            )
            copy.start()
            copies.append(copy)
    for copy in copies:
        copy.wait()


def sum_kernel(terms, total):
    total[...] = jnp.sum(terms[...].astype(F32), axis=0)


def swap_chips(blocks):
    count = lax.axis_size("expert")
    groups = [list(range(core, count, 2)) for core in range(2)]
    return lax.all_to_all(
        blocks, "expert", split_axis=0, concat_axis=0, axis_index_groups=groups, tiled=True
    )


def swap_cores(block):
    count = lax.axis_size("expert")
    return lax.ppermute(block, "expert", [(device, device ^ 1) for device in range(count)])


def per_device(tokens, router, w_in, w_out, d_out):
    devices = lax.axis_size("expert")
    chips = devices // 2
    slots = router.shape[1]
    split_chips = chips // slots
    images, count, width = tokens.shape
    hidden_units = w_in.shape[2]
    rows, main, extra = block_shape(images, width)
    half = chips * rows
    router_t = router.T
    big = images * count * width
    weight = width * hidden_units

    send, tok, dout, disp, comb, w_one, w_two = call(
        functools.partial(rows_kernel, split_chips),
        (
            vmem_out((chips, rows, main), BF16),
            vmem_out((images, count, width), BF16),
            vmem_out((images, count, width), BF16),
            vmem_out((images, slots, count), F32),
            vmem_out((images, slots, count), F32),
            vmem_out(w_in.shape[1:], BF16),
            vmem_out(w_out.shape[1:], BF16),
        ),
        tuple(in_hbm(array) for array in (tokens, router_t, d_out, w_in[0], w_out[0])),
        (VMEM,) * 7,
        (HBM,) * 5,
        [
            pltpu.VMEM((slots, width), BF16),
            pltpu.VMEM((slots, rows, main), F32),
            pltpu.SemaphoreType.DMA((2 * images,)),
            pltpu.SemaphoreType.DMA((3,)),
        ],
        (6 * slots * big, 4 * big),
    )
    w_one, w_two = in_vmem(w_one), in_vmem(w_two)
    near = swap_chips(send)
    far = swap_cores(near)
    other, x, hid, grad = call(
        functools.partial(experts_kernel, images),
        (
            vmem_out((chips, rows, main), BF16),
            vmem_out((2 * half, width), BF16),
            vmem_out((2 * half, hidden_units), BF16),
            vmem_out((2 * half, hidden_units), BF16),
        ),
        (in_vmem(near), in_vmem(far), w_one, w_two),
        (VMEM,) * 4,
        (VMEM,) * 4,
        [
            pltpu.VMEM((2 * chips, rows, extra), F32),
            pltpu.VMEM((chips, rows, main), F32),
        ],
        (12 * half * weight, 4 * weight),
    )
    received = swap_cores(other)
    own = call(
        functools.partial(own_kernel, images),
        vmem_out((chips, rows, main), F32),
        (in_vmem(hid), in_vmem(grad), w_one, w_two),
        VMEM,
        (VMEM,) * 4,
        (),
        (4 * half * weight, 4 * weight),
    )
    total = call(
        add_kernel,
        vmem_out((chips, rows, main), BF16),
        (in_vmem(own), in_vmem(received)),
        VMEM,
        (VMEM,) * 2,
        (),
        (half * main, 8 * half * main),
    )
    shares = swap_chips(total)
    parts = 5
    g_in, g_out = call(
        functools.partial(weights_kernel, images),
        (
            jax.ShapeDtypeStruct((width, hidden_units), BF16),
            jax.ShapeDtypeStruct((hidden_units, width), BF16),
        ),
        (in_vmem(x), in_vmem(hid), in_vmem(grad)),
        (HBM,) * 2,
        (VMEM,) * 3,
        [
            pltpu.VMEM((parts, width // parts, hidden_units), BF16),
            pltpu.VMEM((parts, hidden_units // parts, width), BF16),
            pltpu.SemaphoreType.DMA((parts,)),
            pltpu.SemaphoreType.DMA((parts,)),
        ],
        (8 * half * weight, 4 * weight),
    )
    terms, left, right = call(
        functools.partial(logits_kernel, split_chips),
        (
            vmem_out((devices, slots, width), BF16),
            vmem_out((images, 2 * slots, count), F32),
            vmem_out((images, 2 * slots, width), F32),
        ),
        (
            in_vmem(shares),
            in_vmem(tok),
            in_vmem(dout),
            in_vmem(disp),
            in_vmem(comb),
            router_t,
        ),
        (VMEM,) * 3,
        (VMEM,) * 6,
        [pltpu.VMEM((slots, rows, extra), F32)],
        (6 * slots * big, 4 * big),
    )
    terms = lax.all_to_all(terms, "expert", split_axis=0, concat_axis=0, tiled=True)
    pieces = 2
    grad_tokens = call(
        tokens_kernel,
        jax.ShapeDtypeStruct(tokens.shape, BF16),
        (in_vmem(left), in_vmem(right)),
        HBM,
        (VMEM,) * 2,
        [
            pltpu.VMEM((images, pieces, count // pieces, width), BF16),
            pltpu.SemaphoreType.DMA((images, pieces)),
        ],
        (4 * slots * big, 2 * big),
    )
    grad_router = call(
        sum_kernel,
        jax.ShapeDtypeStruct((slots, width), F32),
        (in_vmem(terms),),
        VMEM,
        (VMEM,),
        (),
        (devices * slots * width, 2 * devices * slots * width),
    )
    return (grad_tokens, g_in[None], g_out[None], grad_router.T)


def solution(mesh):
    in_specs = (
        P(("groups", "expert"), None, None),
        P(None, "groups"),
        P(("groups", "expert"), None, None),
        P(("groups", "expert"), None, None),
        P(("groups", "expert"), None, None),
    )
    out_specs = (
        P(("groups", "expert"), None, None),
        P(("groups", "expert"), None, None),
        P(("groups", "expert"), None, None),
        P(None, "groups"),
    )
    return jax.shard_map(
        per_device, mesh=mesh, in_specs=in_specs, out_specs=out_specs, check_vma=False
    )
```

```python
import functools

import jax
import jax.numpy as jnp
from jax import lax
from jax.experimental import pallas as pl
from jax.experimental.pallas import tpu as pltpu
from jax.sharding import PartitionSpec as P

F32 = jnp.float32
BF16 = jnp.bfloat16
NT = (((1,), (1,)), ((), ()))
TN = (((0,), (0,)), ((), ()))
NN = (((1,), (0,)), ((), ()))

VMEM = pl.BlockSpec(memory_space=pltpu.VMEM)
HBM = pl.BlockSpec(memory_space=pltpu.HBM)
MIB = 1024 * 1024


def dot(left, right, dims=NN):
    return lax.dot_general(left, right, dims, preferred_element_type=F32)


def in_vmem(array):
    return pltpu.with_memory_space_constraint(array, pltpu.VMEM)


def in_hbm(array):
    return pltpu.with_memory_space_constraint(array, pltpu.HBM)


def vmem_out(shape, dtype):
    return pltpu.VMEM(shape, dtype)


def call(kernel, outs, ins, out_specs, in_specs, scratch=(), cost=None, limit=40 * MIB):
    return pl.pallas_call(
        kernel,
        out_shape=outs,
        in_specs=in_specs,
        out_specs=out_specs,
        scratch_shapes=list(scratch),
        compiler_params=pltpu.CompilerParams(vmem_limit_bytes=limit),
        cost_estimate=pl.CostEstimate(flops=cost[0], bytes_accessed=cost[1], transcendentals=0),
    )(*ins)


def block_shape(images, width):
    extra = width // 5
    main = width - extra
    ends = -(-2 * images * extra // main)
    return -(-(2 * images + ends) // 8) * 8, main, extra


def end_place(images, main, extra, row):
    per = main // extra
    return 2 * images + row // per, row % per * extra


def pack(images, scratch, values):
    main = scratch.shape[2]
    extra = values.shape[2] - main
    scratch[...] = values[:, :, :main]
    for row in range(2 * images):
        to, column = end_place(images, main, extra, row)
        scratch[:, to, column : column + extra] = values[:, row, main:]


def unpack(images, scratch, values):
    main = values.shape[2]
    extra = scratch.shape[2]
    scratch[...] = jnp.zeros_like(scratch)
    for row in range(2 * images):
        at, column = end_place(images, main, extra, row)
        scratch[:, row, :] = values[:, at, column : column + extra]


def rows_kernel(
    split_chips,
    tokens,
    router_hbm,
    d_out,
    send,
    tok,
    dout,
    disp_out,
    comb_out,
    router_t,
    block,
    sems,
    router_sem,
):
    images = tok.shape[0]
    main = send.shape[2]
    extra = tok.shape[2] - main
    fetch_router = pltpu.make_async_copy(router_hbm, router_t, router_sem)
    fetch_router.start()
    fetch_tok = [
        pltpu.make_async_copy(tokens.at[b], tok.at[b], sems.at[b]) for b in range(images)
    ]
    fetch_dout = [
        pltpu.make_async_copy(d_out.at[b], dout.at[b], sems.at[images + b]) for b in range(images)
    ]
    for copy in fetch_tok:
        copy.start()
    block[...] = jnp.zeros_like(block)

    def put(row, values):
        to, column = end_place(images, main, extra, row)
        block[:, row, :] = values[:, :main]
        block[:, to, column : column + extra] = values[:, main:]

    fetch_router.wait()
    logits = []
    for b in range(images):
        fetch_tok[b].wait()
        if b == 0:
            for copy in fetch_dout:
                copy.start()
        logits.append(dot(router_t[...], tok[b], NT))
    disps = []
    combs = []
    for b in range(images):
        exps = jnp.exp(logits[b] - jnp.max(logits[b], axis=1, keepdims=True))
        disps.append(exps * (1.0 / jnp.sum(exps, axis=1, keepdims=True)))
        exps = jnp.exp(logits[b] - jnp.max(logits[b], axis=0, keepdims=True))
        combs.append(exps * (1.0 / jnp.sum(exps, axis=0, keepdims=True)))
        disp_out[b] = disps[b]
        comb_out[b] = combs[b]
    for b in range(images):
        put(b, dot(disps[b].astype(BF16), tok[b]))
    for b in range(images):
        fetch_dout[b].wait()
        put(images + b, dot(combs[b].astype(BF16), dout[b]))
    for slot in range(block.shape[0]):
        rows = block[slot].astype(BF16)
        for chip in range(split_chips):
            send[slot * split_chips + chip] = rows


def fetch_kernel(source, _, target, sems):
    parts = sems.shape[0]
    step = source.shape[0] // parts
    copies = [
        pltpu.make_async_copy(
            source.at[pl.ds(i * step, step)], target.at[pl.ds(i * step, step)], sems.at[i]
        )
        for i in range(parts)
    ]
    for copy in copies:
        copy.start()
    for copy in copies:
        copy.wait()


def experts_kernel(
    images,
    near,
    far,
    w_in,
    w_out_hbm,
    other,
    x_out,
    hid_out,
    grad_out,
    w_out,
    ends,
    packed,
    sems,
):
    parts = sems.shape[0]
    step = w_out.shape[0] // parts
    copies = [
        pltpu.make_async_copy(
            w_out_hbm.at[pl.ds(i * step, step)], w_out.at[pl.ds(i * step, step)], sems.at[i]
        )
        for i in range(parts)
    ]
    for copy in copies:
        copy.start()
    chips, rows, main = near.shape
    half = chips * rows
    width = x_out.shape[1]
    for i, blocks in enumerate((near, far)):
        unpack(images, ends.at[pl.ds(i * chips, chips)], blocks[...].astype(F32))
    x = jnp.concatenate(
        [
            jnp.concatenate(
                [near[...].reshape(half, main), far[...].reshape(half, main)], axis=0
            ),
            ends[...].reshape(2 * half, width - main).astype(BF16),
        ],
        axis=1,
    )
    x_out[...] = x
    pre = dot(x, w_in[...])
    for copy in copies:
        copy.wait()
    grad_hidden = dot(x, w_out[...], NT)
    place = lax.broadcasted_iota(jnp.int32, pre.shape, 0) % rows
    slot_row = place < images
    grad_hidden = pltpu.roll(grad_hidden, 2 * half - images, 0)
    scale = 0.7978845608028654
    square = pre * pre
    tanh = jnp.tanh(scale * pre * (1.0 + 0.044715 * square))
    cdf = 0.5 * (1.0 + tanh)
    slope = cdf + (0.5 * scale) * pre * (1.0 - tanh * tanh) * (1.0 + (3 * 0.044715) * square)
    hidden = jnp.where(slot_row, pre * cdf, 0.0).astype(BF16)
    grad_pre = jnp.where(slot_row, slope * grad_hidden, 0.0)
    grad_low = pltpu.roll(grad_pre, images, 0).astype(BF16)
    hid_out[...] = hidden
    grad_out[...] = grad_low
    shares = dot(hidden[half:], w_out[...]) + dot(grad_low[half:], w_in[...], NT)
    pack(images, packed, shares.reshape(chips, rows, width))
    other[...] = packed[...].astype(BF16)


def own_kernel(images, hid, grad, w_in, w_out, own):
    chips, rows, _ = own.shape
    half = chips * rows
    shares = dot(hid[:half], w_out[...]) + dot(grad[:half], w_in[...], NT)
    pack(images, own, shares.reshape(chips, rows, shares.shape[1]))


def add_kernel(own, received, total):
    total[...] = (own[...] + received[...].astype(F32)).astype(BF16)


def weights_kernel(images, x, hid, grad, g_in, g_out, buf_in, buf_out, sem_in, sem_out):
    parts = buf_in.shape[0]
    step_in = g_in.shape[0] // parts
    step_out = g_out.shape[0] // parts
    count = x.shape[0]
    hid_low = pltpu.roll(hid[...].astype(F32), images, 0).astype(BF16)
    grad_high = pltpu.roll(grad[...].astype(F32), count - images, 0).astype(BF16)
    copies = []
    for i in range(parts):
        buf_out[i] = dot(hid_low[:, i * step_out : (i + 1) * step_out], x[...], TN).astype(BF16)
        copy = pltpu.make_async_copy(
            buf_out.at[i], g_out.at[pl.ds(i * step_out, step_out)], sem_out.at[i]
        )
        copy.start()
        copies.append(copy)
        buf_in[i] = dot(x[:, i * step_in : (i + 1) * step_in], grad_high, TN).astype(BF16)
        copy = pltpu.make_async_copy(
            buf_in.at[i], g_in.at[pl.ds(i * step_in, step_in)], sem_in.at[i]
        )
        copy.start()
        copies.append(copy)
    for copy in copies:
        copy.wait()


def logits_kernel(
    split_chips, shares, tok, dout, disp, comb, router_t, terms_out, left, right, ends
):
    images, slots, count = disp.shape
    chips, rows, main = shares.shape
    width = tok.shape[2]
    summed = []
    for slot in range(slots):
        total = shares[slot * split_chips].astype(F32)
        for chip in range(1, split_chips):
            total = total + shares[slot * split_chips + chip].astype(F32)
        summed.append(total)
    unpack(images, ends, jnp.stack(summed))
    stacked = jnp.concatenate(
        [
            jnp.concatenate(summed, axis=0),
            ends[...].reshape(slots * rows, width - main),
        ],
        axis=1,
    )
    stacked_b = stacked.astype(BF16)
    tok_all = tok[...].reshape(images * count, width)
    by_dout = dot(stacked_b, dout[...].reshape(images * count, width), NT)
    by_tok = dot(stacked_b, tok_all, NT)
    grads = []
    for b in range(images):
        span = slice(b * count, (b + 1) * count)
        grad_comb = jnp.concatenate(
            [by_dout[s * rows + b : s * rows + b + 1, span] for s in range(slots)], axis=0
        )
        grad_disp = jnp.concatenate(
            [
                by_tok[s * rows + images + b : s * rows + images + b + 1, span]
                for s in range(slots)
            ],
            axis=0,
        )
        dispatch = disp[b]
        combine = comb[b]
        grads.append(
            dispatch * (grad_disp - jnp.sum(dispatch * grad_disp, axis=1, keepdims=True))
            + combine * (grad_comb - jnp.sum(combine * grad_comb, axis=0, keepdims=True))
        )
    terms = dot(jnp.concatenate(grads, axis=1).astype(BF16), tok_all).astype(BF16)
    terms_out[...] = jnp.broadcast_to(terms[None], terms_out.shape)
    for b in range(images):
        left[b] = jnp.concatenate([disp[b], grads[b]], axis=0)
        right[b] = jnp.concatenate(
            [stacked[s * rows + images + b : s * rows + images + b + 1] for s in range(slots)]
            + [router_t[...].astype(F32)],
            axis=0,
        )


def tokens_kernel(left, right, grad_tokens, buf, sems):
    images, parts = buf.shape[:2]
    step = buf.shape[2]
    copies = []
    for b in range(images):
        rhs = right[b].astype(BF16)
        for i in range(parts):
            lhs = left[b, :, i * step : (i + 1) * step].astype(BF16)
            buf[b, i] = dot(lhs, rhs, TN).astype(BF16)
            copy = pltpu.make_async_copy(
                buf.at[b, i], grad_tokens.at[b, pl.ds(i * step, step)], sems.at[b, i]
            )
            copy.start()
            copies.append(copy)
    for copy in copies:
        copy.wait()


def sum_kernel(terms, total):
    total[...] = jnp.sum(terms[...].astype(F32), axis=0)


def swap_chips(blocks):
    count = lax.axis_size("expert")
    groups = [list(range(core, count, 2)) for core in range(2)]
    return lax.all_to_all(
        blocks, "expert", split_axis=0, concat_axis=0, axis_index_groups=groups, tiled=True
    )


def swap_cores(block):
    count = lax.axis_size("expert")
    return lax.ppermute(block, "expert", [(device, device ^ 1) for device in range(count)])


def per_device(tokens, router, w_in, w_out, d_out):
    devices = lax.axis_size("expert")
    chips = devices // 2
    slots = router.shape[1]
    split_chips = chips // slots
    images, count, width = tokens.shape
    hidden_units = w_in.shape[2]
    rows, main, extra = block_shape(images, width)
    half = chips * rows
    router_t = router.T
    big = images * count * width
    weight = width * hidden_units

    send, tok, dout, disp, comb = call(
        functools.partial(rows_kernel, split_chips),
        (
            vmem_out((chips, rows, main), BF16),
            vmem_out((images, count, width), BF16),
            vmem_out((images, count, width), BF16),
            vmem_out((images, slots, count), F32),
            vmem_out((images, slots, count), F32),
        ),
        (in_hbm(tokens), in_hbm(router_t), in_hbm(d_out)),
        (VMEM,) * 5,
        (HBM,) * 3,
        [
            pltpu.VMEM((slots, width), BF16),
            pltpu.VMEM((slots, rows, main), F32),
            pltpu.SemaphoreType.DMA((2 * images,)),
            pltpu.SemaphoreType.DMA,
        ],
        (6 * slots * big, 4 * big),
    )
    near = swap_chips(send)
    far = swap_cores(near)
    w_one = call(
        fetch_kernel,
        vmem_out(w_in.shape[1:], BF16),
        (in_hbm(w_in[0]), in_vmem(near)),
        VMEM,
        (HBM, VMEM),
        [pltpu.SemaphoreType.DMA((5,))],
        (0, 4 * weight),
    )
    w_one = in_vmem(w_one)
    other, x, hid, grad, w_two = call(
        functools.partial(experts_kernel, images),
        (
            vmem_out((chips, rows, main), BF16),
            vmem_out((2 * half, width), BF16),
            vmem_out((2 * half, hidden_units), BF16),
            vmem_out((2 * half, hidden_units), BF16),
            vmem_out(w_out.shape[1:], BF16),
        ),
        (in_vmem(near), in_vmem(far), w_one, in_hbm(w_out[0])),
        (VMEM,) * 5,
        (VMEM, VMEM, VMEM, HBM),
        [
            pltpu.VMEM((2 * chips, rows, extra), F32),
            pltpu.VMEM((chips, rows, main), F32),
            pltpu.SemaphoreType.DMA((5,)),
        ],
        (12 * half * weight, 4 * weight),
    )
    w_two = in_vmem(w_two)
    received = swap_cores(other)
    own = call(
        functools.partial(own_kernel, images),
        vmem_out((chips, rows, main), F32),
        (in_vmem(hid), in_vmem(grad), w_one, w_two),
        VMEM,
        (VMEM,) * 4,
        (),
        (4 * half * weight, 4 * weight),
    )
    total = call(
        add_kernel,
        vmem_out((chips, rows, main), BF16),
        (in_vmem(own), in_vmem(received)),
        VMEM,
        (VMEM,) * 2,
        (),
        (half * main, 8 * half * main),
    )
    shares = swap_chips(total)
    parts = 5
    g_in, g_out = call(
        functools.partial(weights_kernel, images),
        (
            jax.ShapeDtypeStruct((width, hidden_units), BF16),
            jax.ShapeDtypeStruct((hidden_units, width), BF16),
        ),
        (in_vmem(x), in_vmem(hid), in_vmem(grad)),
        (HBM,) * 2,
        (VMEM,) * 3,
        [
            pltpu.VMEM((parts, width // parts, hidden_units), BF16),
            pltpu.VMEM((parts, hidden_units // parts, width), BF16),
            pltpu.SemaphoreType.DMA((parts,)),
            pltpu.SemaphoreType.DMA((parts,)),
        ],
        (8 * half * weight, 4 * weight),
    )
    terms, left, right = call(
        functools.partial(logits_kernel, split_chips),
        (
            vmem_out((devices, slots, width), BF16),
            vmem_out((images, 2 * slots, count), F32),
            vmem_out((images, 2 * slots, width), F32),
        ),
        (
            in_vmem(shares),
            in_vmem(tok),
            in_vmem(dout),
            in_vmem(disp),
            in_vmem(comb),
            router_t,
        ),
        (VMEM,) * 3,
        (VMEM,) * 6,
        [pltpu.VMEM((slots, rows, extra), F32)],
        (6 * slots * big, 4 * big),
    )
    terms = lax.all_to_all(terms, "expert", split_axis=0, concat_axis=0, tiled=True)
    pieces = 2
    grad_tokens = call(
        tokens_kernel,
        jax.ShapeDtypeStruct(tokens.shape, BF16),
        (in_vmem(left), in_vmem(right)),
        HBM,
        (VMEM,) * 2,
        [
            pltpu.VMEM((images, pieces, count // pieces, width), BF16),
            pltpu.SemaphoreType.DMA((images, pieces)),
        ],
        (4 * slots * big, 2 * big),
    )
    grad_router = call(
        sum_kernel,
        jax.ShapeDtypeStruct((slots, width), F32),
        (in_vmem(terms),),
        VMEM,
        (VMEM,),
        (),
        (devices * slots * width, 2 * devices * slots * width),
    )
    return (grad_tokens, g_in[None], g_out[None], grad_router.T)


def solution(mesh):
    in_specs = (
        P(("groups", "expert"), None, None),
        P(None, "groups"),
        P(("groups", "expert"), None, None),
        P(("groups", "expert"), None, None),
        P(("groups", "expert"), None, None),
    )
    out_specs = (
        P(("groups", "expert"), None, None),
        P(("groups", "expert"), None, None),
        P(("groups", "expert"), None, None),
        P(None, "groups"),
    )
    return jax.shard_map(
        per_device, mesh=mesh, in_specs=in_specs, out_specs=out_specs, check_vma=False
    )
```

```python
import functools

import jax
import jax.numpy as jnp
from jax import lax
from jax.experimental import pallas as pl
from jax.experimental.pallas import tpu as pltpu
from jax.sharding import PartitionSpec as P

F32 = jnp.float32
BF16 = jnp.bfloat16
NT = (((1,), (1,)), ((), ()))
TN = (((0,), (0,)), ((), ()))
NN = (((1,), (0,)), ((), ()))

VMEM = pl.BlockSpec(memory_space=pltpu.VMEM)
HBM = pl.BlockSpec(memory_space=pltpu.HBM)
MIB = 1024 * 1024


def dot(left, right, dims=NN):
    return lax.dot_general(left, right, dims, preferred_element_type=F32)


def in_vmem(array):
    return pltpu.with_memory_space_constraint(array, pltpu.VMEM)


def in_hbm(array):
    return pltpu.with_memory_space_constraint(array, pltpu.HBM)


def vmem_out(shape, dtype):
    return pltpu.VMEM(shape, dtype)


def call(kernel, outs, ins, out_specs, in_specs, scratch=(), cost=None, limit=40 * MIB):
    return pl.pallas_call(
        kernel,
        out_shape=outs,
        in_specs=in_specs,
        out_specs=out_specs,
        scratch_shapes=list(scratch),
        compiler_params=pltpu.CompilerParams(vmem_limit_bytes=limit),
        cost_estimate=pl.CostEstimate(flops=cost[0], bytes_accessed=cost[1], transcendentals=0),
    )(*ins)


def block_shape(images, width):
    extra = width // 5
    main = width - extra
    ends = -(-2 * images * extra // main)
    return -(-(2 * images + ends) // 8) * 8, main, extra


def end_place(images, main, extra, row):
    per = main // extra
    return 2 * images + row // per, row % per * extra


def pack(images, scratch, values):
    main = scratch.shape[2]
    extra = values.shape[2] - main
    scratch[...] = values[:, :, :main]
    for row in range(2 * images):
        to, column = end_place(images, main, extra, row)
        scratch[:, to, column : column + extra] = values[:, row, main:]


def unpack(images, scratch, values):
    main = values.shape[2]
    extra = scratch.shape[2]
    scratch[...] = jnp.zeros_like(scratch)
    for row in range(2 * images):
        at, column = end_place(images, main, extra, row)
        scratch[:, row, :] = values[:, at, column : column + extra]


def rows_kernel(
    split_chips,
    tokens,
    router_hbm,
    d_out,
    w_in,
    send,
    tok,
    dout,
    disp_out,
    comb_out,
    w_one,
    router_t,
    block,
    sems,
    other_sems,
):
    images = tok.shape[0]
    main = send.shape[2]
    extra = tok.shape[2] - main
    fetch_router = pltpu.make_async_copy(router_hbm, router_t, other_sems.at[0])
    fetch_router.start()
    fetch_tok = [
        pltpu.make_async_copy(tokens.at[b], tok.at[b], sems.at[b]) for b in range(images)
    ]
    fetch_dout = [
        pltpu.make_async_copy(d_out.at[b], dout.at[b], sems.at[images + b]) for b in range(images)
    ]
    fetch_weight = pltpu.make_async_copy(w_in, w_one, other_sems.at[1])
    for copy in fetch_tok:
        copy.start()
    block[...] = jnp.zeros_like(block)

    def put(row, values):
        to, column = end_place(images, main, extra, row)
        block[:, row, :] = values[:, :main]
        block[:, to, column : column + extra] = values[:, main:]

    fetch_router.wait()
    logits = {}
    combs = {}
    disps = {}

    def softmaxes(b):
        exps = jnp.exp(logits[b] - jnp.max(logits[b], axis=1, keepdims=True))
        disp = exps * (1.0 / jnp.sum(exps, axis=1, keepdims=True))
        exps = jnp.exp(logits[b] - jnp.max(logits[b], axis=0, keepdims=True))
        comb = exps * (1.0 / jnp.sum(exps, axis=0, keepdims=True))
        disp_out[b] = disp
        comb_out[b] = comb
        disps[b] = disp.astype(BF16)
        combs[b] = comb.astype(BF16)

    for step in range(images + 2):
        if step < images:
            fetch_tok[step].wait()
            if step == 0:
                for copy in fetch_dout:
                    copy.start()
            if step == min(1, images - 1):
                fetch_weight.start()
            logits[step] = dot(router_t[...], tok[step], NT)
        if 0 <= step - 1 < images:
            softmaxes(step - 1)
        if 0 <= step - 2 < images:
            put(step - 2, dot(disps[step - 2], tok[step - 2]))
    for b in range(images):
        fetch_dout[b].wait()
        put(images + b, dot(combs[b], dout[b]))
    for slot in range(block.shape[0]):
        rows = block[slot].astype(BF16)
        for chip in range(split_chips):
            send[slot * split_chips + chip] = rows
    fetch_weight.wait()


def fetch_kernel(source, _, target, sems):
    parts = sems.shape[0]
    step = source.shape[0] // parts
    copies = [
        pltpu.make_async_copy(
            source.at[pl.ds(i * step, step)], target.at[pl.ds(i * step, step)], sems.at[i]
        )
        for i in range(parts)
    ]
    for copy in copies:
        copy.start()
    for copy in copies:
        copy.wait()


def experts_kernel(images, near, far, w_in, w_out, other, x_out, hid_out, grad_out, ends, packed):
    chips, rows, main = near.shape
    half = chips * rows
    width = x_out.shape[1]
    for i, blocks in enumerate((near, far)):
        unpack(images, ends.at[pl.ds(i * chips, chips)], blocks[...].astype(F32))
    x = jnp.concatenate(
        [
            jnp.concatenate(
                [near[...].reshape(half, main), far[...].reshape(half, main)], axis=0
            ),
            ends[...].reshape(2 * half, width - main).astype(BF16),
        ],
        axis=1,
    )
    x_out[...] = x
    pre = dot(x, w_in[...])
    grad_hidden = dot(x, w_out[...], NT)
    place = lax.broadcasted_iota(jnp.int32, pre.shape, 0) % rows
    slot_row = place < images
    grad_hidden = pltpu.roll(grad_hidden, 2 * half - images, 0)
    scale = 0.7978845608028654
    square = pre * pre
    tanh = jnp.tanh(scale * pre * (1.0 + 0.044715 * square))
    cdf = 0.5 * (1.0 + tanh)
    slope = cdf + (0.5 * scale) * pre * (1.0 - tanh * tanh) * (1.0 + (3 * 0.044715) * square)
    hidden = jnp.where(slot_row, pre * cdf, 0.0).astype(BF16)
    grad_pre = jnp.where(slot_row, slope * grad_hidden, 0.0)
    grad_low = pltpu.roll(grad_pre, images, 0).astype(BF16)
    hid_out[...] = hidden
    grad_out[...] = grad_low
    shares = dot(hidden[half:], w_out[...]) + dot(grad_low[half:], w_in[...], NT)
    pack(images, packed, shares.reshape(chips, rows, width))
    other[...] = packed[...].astype(BF16)


def own_kernel(images, hid, grad, w_in, w_out, own):
    chips, rows, _ = own.shape
    half = chips * rows
    shares = dot(hid[:half], w_out[...]) + dot(grad[:half], w_in[...], NT)
    pack(images, own, shares.reshape(chips, rows, shares.shape[1]))


def add_kernel(own, received, total):
    total[...] = (own[...] + received[...].astype(F32)).astype(BF16)


def weights_kernel(images, x, hid, grad, g_in, g_out, buf_in, buf_out, sem_in, sem_out):
    parts = buf_in.shape[0]
    step_in = g_in.shape[0] // parts
    step_out = g_out.shape[0] // parts
    count = x.shape[0]
    hid_low = pltpu.roll(hid[...].astype(F32), images, 0).astype(BF16)
    grad_high = pltpu.roll(grad[...].astype(F32), count - images, 0).astype(BF16)
    copies = []
    for i in range(parts):
        buf_out[i] = dot(hid_low[:, i * step_out : (i + 1) * step_out], x[...], TN).astype(BF16)
        copy = pltpu.make_async_copy(
            buf_out.at[i], g_out.at[pl.ds(i * step_out, step_out)], sem_out.at[i]
        )
        copy.start()
        copies.append(copy)
        buf_in[i] = dot(x[:, i * step_in : (i + 1) * step_in], grad_high, TN).astype(BF16)
        copy = pltpu.make_async_copy(
            buf_in.at[i], g_in.at[pl.ds(i * step_in, step_in)], sem_in.at[i]
        )
        copy.start()
        copies.append(copy)
    for copy in copies:
        copy.wait()


def logits_kernel(
    split_chips, shares, tok, dout, disp, comb, router_t, terms_out, left, right, ends
):
    images, slots, count = disp.shape
    chips, rows, main = shares.shape
    width = tok.shape[2]
    summed = []
    for slot in range(slots):
        total = shares[slot * split_chips].astype(F32)
        for chip in range(1, split_chips):
            total = total + shares[slot * split_chips + chip].astype(F32)
        summed.append(total)
    unpack(images, ends, jnp.stack(summed))
    stacked = jnp.concatenate(
        [
            jnp.concatenate(summed, axis=0),
            ends[...].reshape(slots * rows, width - main),
        ],
        axis=1,
    )
    stacked_b = stacked.astype(BF16)
    tok_all = tok[...].reshape(images * count, width)
    by_dout = dot(stacked_b, dout[...].reshape(images * count, width), NT)
    by_tok = dot(stacked_b, tok_all, NT)
    grads = []
    for b in range(images):
        span = slice(b * count, (b + 1) * count)
        grad_comb = jnp.concatenate(
            [by_dout[s * rows + b : s * rows + b + 1, span] for s in range(slots)], axis=0
        )
        grad_disp = jnp.concatenate(
            [
                by_tok[s * rows + images + b : s * rows + images + b + 1, span]
                for s in range(slots)
            ],
            axis=0,
        )
        dispatch = disp[b]
        combine = comb[b]
        grads.append(
            dispatch * (grad_disp - jnp.sum(dispatch * grad_disp, axis=1, keepdims=True))
            + combine * (grad_comb - jnp.sum(combine * grad_comb, axis=0, keepdims=True))
        )
    terms = dot(jnp.concatenate(grads, axis=1).astype(BF16), tok_all).astype(BF16)
    terms_out[...] = jnp.broadcast_to(terms[None], terms_out.shape)
    for b in range(images):
        left[b] = jnp.concatenate([disp[b], grads[b]], axis=0)
        right[b] = jnp.concatenate(
            [stacked[s * rows + images + b : s * rows + images + b + 1] for s in range(slots)]
            + [router_t[...].astype(F32)],
            axis=0,
        )


def tokens_kernel(left, right, grad_tokens, buf, sems):
    images, parts = buf.shape[:2]
    step = buf.shape[2]
    copies = []
    for b in range(images):
        rhs = right[b].astype(BF16)
        for i in range(parts):
            lhs = left[b, :, i * step : (i + 1) * step].astype(BF16)
            buf[b, i] = dot(lhs, rhs, TN).astype(BF16)
            copy = pltpu.make_async_copy(
                buf.at[b, i], grad_tokens.at[b, pl.ds(i * step, step)], sems.at[b, i]
            )
            copy.start()
            copies.append(copy)
    for copy in copies:
        copy.wait()


def sum_kernel(terms, total):
    total[...] = jnp.sum(terms[...].astype(F32), axis=0)


def swap_chips(blocks):
    count = lax.axis_size("expert")
    groups = [list(range(core, count, 2)) for core in range(2)]
    return lax.all_to_all(
        blocks, "expert", split_axis=0, concat_axis=0, axis_index_groups=groups, tiled=True
    )


def swap_cores(block):
    count = lax.axis_size("expert")
    return lax.ppermute(block, "expert", [(device, device ^ 1) for device in range(count)])


def per_device(tokens, router, w_in, w_out, d_out):
    devices = lax.axis_size("expert")
    chips = devices // 2
    slots = router.shape[1]
    split_chips = chips // slots
    images, count, width = tokens.shape
    hidden_units = w_in.shape[2]
    rows, main, extra = block_shape(images, width)
    half = chips * rows
    router_t = router.T
    big = images * count * width
    weight = width * hidden_units

    send, tok, dout, disp, comb, w_one = call(
        functools.partial(rows_kernel, split_chips),
        (
            vmem_out((chips, rows, main), BF16),
            vmem_out((images, count, width), BF16),
            vmem_out((images, count, width), BF16),
            vmem_out((images, slots, count), F32),
            vmem_out((images, slots, count), F32),
            vmem_out(w_in.shape[1:], BF16),
        ),
        tuple(in_hbm(array) for array in (tokens, router_t, d_out, w_in[0])),
        (VMEM,) * 6,
        (HBM,) * 4,
        [
            pltpu.VMEM((slots, width), BF16),
            pltpu.VMEM((slots, rows, main), F32),
            pltpu.SemaphoreType.DMA((2 * images,)),
            pltpu.SemaphoreType.DMA((2,)),
        ],
        (6 * slots * big, 4 * big),
    )
    near = swap_chips(send)
    far = swap_cores(near)
    w_two = call(
        fetch_kernel,
        vmem_out(w_out.shape[1:], BF16),
        (in_hbm(w_out[0]), in_vmem(near)),
        VMEM,
        (HBM, VMEM),
        [pltpu.SemaphoreType.DMA((5,))],
        (0, 4 * weight),
    )
    w_one, w_two = in_vmem(w_one), in_vmem(w_two)
    other, x, hid, grad = call(
        functools.partial(experts_kernel, images),
        (
            vmem_out((chips, rows, main), BF16),
            vmem_out((2 * half, width), BF16),
            vmem_out((2 * half, hidden_units), BF16),
            vmem_out((2 * half, hidden_units), BF16),
        ),
        (in_vmem(near), in_vmem(far), w_one, w_two),
        (VMEM,) * 4,
        (VMEM,) * 4,
        [
            pltpu.VMEM((2 * chips, rows, extra), F32),
            pltpu.VMEM((chips, rows, main), F32),
        ],
        (12 * half * weight, 4 * weight),
    )
    received = swap_cores(other)
    own = call(
        functools.partial(own_kernel, images),
        vmem_out((chips, rows, main), F32),
        (in_vmem(hid), in_vmem(grad), w_one, w_two),
        VMEM,
        (VMEM,) * 4,
        (),
        (4 * half * weight, 4 * weight),
    )
    total = call(
        add_kernel,
        vmem_out((chips, rows, main), BF16),
        (in_vmem(own), in_vmem(received)),
        VMEM,
        (VMEM,) * 2,
        (),
        (half * main, 8 * half * main),
    )
    shares = swap_chips(total)
    parts = 5
    g_in, g_out = call(
        functools.partial(weights_kernel, images),
        (
            jax.ShapeDtypeStruct((width, hidden_units), BF16),
            jax.ShapeDtypeStruct((hidden_units, width), BF16),
        ),
        (in_vmem(x), in_vmem(hid), in_vmem(grad)),
        (HBM,) * 2,
        (VMEM,) * 3,
        [
            pltpu.VMEM((parts, width // parts, hidden_units), BF16),
            pltpu.VMEM((parts, hidden_units // parts, width), BF16),
            pltpu.SemaphoreType.DMA((parts,)),
            pltpu.SemaphoreType.DMA((parts,)),
        ],
        (8 * half * weight, 4 * weight),
    )
    terms, left, right = call(
        functools.partial(logits_kernel, split_chips),
        (
            vmem_out((devices, slots, width), BF16),
            vmem_out((images, 2 * slots, count), F32),
            vmem_out((images, 2 * slots, width), F32),
        ),
        (
            in_vmem(shares),
            in_vmem(tok),
            in_vmem(dout),
            in_vmem(disp),
            in_vmem(comb),
            router_t,
        ),
        (VMEM,) * 3,
        (VMEM,) * 6,
        [pltpu.VMEM((slots, rows, extra), F32)],
        (6 * slots * big, 4 * big),
    )
    terms = lax.all_to_all(terms, "expert", split_axis=0, concat_axis=0, tiled=True)
    pieces = 2
    grad_tokens = call(
        tokens_kernel,
        jax.ShapeDtypeStruct(tokens.shape, BF16),
        (in_vmem(left), in_vmem(right)),
        HBM,
        (VMEM,) * 2,
        [
            pltpu.VMEM((images, pieces, count // pieces, width), BF16),
            pltpu.SemaphoreType.DMA((images, pieces)),
        ],
        (4 * slots * big, 2 * big),
    )
    grad_router = call(
        sum_kernel,
        jax.ShapeDtypeStruct((slots, width), F32),
        (in_vmem(terms),),
        VMEM,
        (VMEM,),
        (),
        (devices * slots * width, 2 * devices * slots * width),
    )
    return (grad_tokens, g_in[None], g_out[None], grad_router.T)


def solution(mesh):
    in_specs = (
        P(("groups", "expert"), None, None),
        P(None, "groups"),
        P(("groups", "expert"), None, None),
        P(("groups", "expert"), None, None),
        P(("groups", "expert"), None, None),
    )
    out_specs = (
        P(("groups", "expert"), None, None),
        P(("groups", "expert"), None, None),
        P(("groups", "expert"), None, None),
        P(None, "groups"),
    )
    return jax.shard_map(
        per_device, mesh=mesh, in_specs=in_specs, out_specs=out_specs, check_vma=False
    )
```

```python
import functools

import jax
import jax.numpy as jnp
from jax import lax
from jax.experimental import pallas as pl
from jax.experimental.pallas import tpu as pltpu
from jax.sharding import PartitionSpec as P

F32 = jnp.float32
BF16 = jnp.bfloat16
NT = (((1,), (1,)), ((), ()))
TN = (((0,), (0,)), ((), ()))
NN = (((1,), (0,)), ((), ()))

VMEM = pl.BlockSpec(memory_space=pltpu.VMEM)
HBM = pl.BlockSpec(memory_space=pltpu.HBM)
MIB = 1024 * 1024


def dot(left, right, dims=NN):
    return lax.dot_general(left, right, dims, preferred_element_type=F32)


def in_vmem(array):
    return pltpu.with_memory_space_constraint(array, pltpu.VMEM)


def in_hbm(array):
    return pltpu.with_memory_space_constraint(array, pltpu.HBM)


def vmem_out(shape, dtype):
    return pltpu.VMEM(shape, dtype)


def call(kernel, outs, ins, out_specs, in_specs, scratch=(), cost=None, limit=40 * MIB):
    return pl.pallas_call(
        kernel,
        out_shape=outs,
        in_specs=in_specs,
        out_specs=out_specs,
        scratch_shapes=list(scratch),
        compiler_params=pltpu.CompilerParams(vmem_limit_bytes=limit),
        cost_estimate=pl.CostEstimate(flops=cost[0], bytes_accessed=cost[1], transcendentals=0),
    )(*ins)


def block_shape(images, width):
    extra = width // 5
    main = width - extra
    ends = -(-2 * images * extra // main)
    return -(-(2 * images + ends) // 8) * 8, main, extra


def end_place(images, main, extra, row):
    per = main // extra
    return 2 * images + row // per, row % per * extra


def pack(images, scratch, values):
    main = scratch.shape[2]
    extra = values.shape[2] - main
    scratch[...] = values[:, :, :main]
    for row in range(2 * images):
        to, column = end_place(images, main, extra, row)
        scratch[:, to, column : column + extra] = values[:, row, main:]


def unpack(images, scratch, values):
    main = values.shape[2]
    extra = scratch.shape[2]
    scratch[...] = jnp.zeros_like(scratch)
    for row in range(2 * images):
        at, column = end_place(images, main, extra, row)
        scratch[:, row, :] = values[:, at, column : column + extra]


def rows_kernel(
    tokens,
    router_hbm,
    d_out,
    rows_out,
    tok,
    dout,
    disp_out,
    comb_out,
    router_t,
    block,
    sems,
    other_sems,
):
    images = tok.shape[0]
    main = rows_out.shape[2]
    extra = tok.shape[2] - main
    fetch_router = pltpu.make_async_copy(router_hbm, router_t, other_sems.at[0])
    fetch_router.start()
    fetch_tok = [
        pltpu.make_async_copy(tokens.at[b], tok.at[b], sems.at[b]) for b in range(images)
    ]
    fetch_dout = [
        pltpu.make_async_copy(d_out.at[b], dout.at[b], sems.at[images + b]) for b in range(images)
    ]
    for copy in fetch_tok:
        copy.start()
    block[...] = jnp.zeros_like(block)

    def put(row, values):
        to, column = end_place(images, main, extra, row)
        block[:, row, :] = values[:, :main]
        block[:, to, column : column + extra] = values[:, main:]

    fetch_router.wait()
    logits = {}
    combs = {}
    disps = {}

    def softmaxes(b):
        exps = jnp.exp(logits[b] - jnp.max(logits[b], axis=1, keepdims=True))
        disp = exps * (1.0 / jnp.sum(exps, axis=1, keepdims=True))
        exps = jnp.exp(logits[b] - jnp.max(logits[b], axis=0, keepdims=True))
        comb = exps * (1.0 / jnp.sum(exps, axis=0, keepdims=True))
        disp_out[b] = disp
        comb_out[b] = comb
        disps[b] = disp.astype(BF16)
        combs[b] = comb.astype(BF16)

    for step in range(images + 2):
        if step < images:
            fetch_tok[step].wait()
            if step == 0:
                for copy in fetch_dout:
                    copy.start()
            logits[step] = dot(router_t[...], tok[step], NT)
        if 0 <= step - 1 < images:
            softmaxes(step - 1)
        if 0 <= step - 2 < images:
            put(step - 2, dot(disps[step - 2], tok[step - 2]))
    for b in range(images):
        fetch_dout[b].wait()
        put(images + b, dot(combs[b], dout[b]))
    rows_out[...] = block[...].astype(BF16)


def repeat_kernel(split_chips, rows, tok, dout, send):
    for slot in range(rows.shape[0]):
        for chip in range(split_chips):
            send[slot * split_chips + chip] = rows[slot]


def hidden_rows(images, blocks, w_in, w_out, x_out, hid_out, grad_out, ends):
    chips, rows, main = blocks.shape
    half = chips * rows
    width = x_out.shape[1]
    unpack(images, ends, blocks[...].astype(F32))
    x = jnp.concatenate(
        [
            blocks[...].reshape(half, main),
            ends[...].reshape(half, width - main).astype(BF16),
        ],
        axis=1,
    )
    x_out[...] = x
    pre = dot(x, w_in[...])
    grad_hidden = dot(x, w_out[...], NT)
    place = lax.broadcasted_iota(jnp.int32, pre.shape, 0) % rows
    slot_row = place < images
    grad_hidden = pltpu.roll(grad_hidden, half - images, 0)
    scale = 0.7978845608028654
    square = pre * pre
    tanh = jnp.tanh(scale * pre * (1.0 + 0.044715 * square))
    cdf = 0.5 * (1.0 + tanh)
    slope = cdf + (0.5 * scale) * pre * (1.0 - tanh * tanh) * (1.0 + (3 * 0.044715) * square)
    hidden = jnp.where(slot_row, pre * cdf, 0.0).astype(BF16)
    grad_pre = jnp.where(slot_row, slope * grad_hidden, 0.0)
    grad_low = pltpu.roll(grad_pre, images, 0).astype(BF16)
    hid_out[...] = hidden
    grad_out[...] = grad_low
    return hidden, grad_low


def near_kernel(images, blocks, w_in, w_out, x_out, hid_out, grad_out, ends):
    hidden_rows(images, blocks, w_in, w_out, x_out, hid_out, grad_out, ends)


def far_kernel(images, blocks, w_in, w_out, _, other, x_out, hid_out, grad_out, ends, packed):
    hidden, grad_low = hidden_rows(images, blocks, w_in, w_out, x_out, hid_out, grad_out, ends)
    shares = dot(hidden, w_out[...]) + dot(grad_low, w_in[...], NT)
    pack(images, packed, shares.reshape(blocks.shape[:2] + (shares.shape[1],)))
    other[...] = packed[...].astype(BF16)


def own_kernel(images, hid, grad, w_in, w_out, own):
    chips, rows, _ = own.shape
    shares = dot(hid[...], w_out[...]) + dot(grad[...], w_in[...], NT)
    pack(images, own, shares.reshape(chips, rows, shares.shape[1]))


def add_kernel(own, received, total):
    total[...] = (own[...] + received[...].astype(F32)).astype(BF16)


def weights_kernel(
    images,
    x_near,
    hid_near,
    grad_near,
    x_far,
    hid_far,
    grad_far,
    g_in,
    g_out,
    buf_in,
    buf_out,
    sem_in,
    sem_out,
):
    parts = buf_in.shape[0]
    step_in = g_in.shape[0] // parts
    step_out = g_out.shape[0] // parts
    x = jnp.concatenate([x_near[...], x_far[...]], axis=0)
    hid = jnp.concatenate([hid_near[...], hid_far[...]], axis=0)
    grad = jnp.concatenate([grad_near[...], grad_far[...]], axis=0)
    hid_low = pltpu.roll(hid.astype(F32), images, 0).astype(BF16)
    grad_high = pltpu.roll(grad.astype(F32), x.shape[0] - images, 0).astype(BF16)
    copies = []
    for i in range(parts):
        buf_out[i] = dot(hid_low[:, i * step_out : (i + 1) * step_out], x, TN).astype(BF16)
        copy = pltpu.make_async_copy(
            buf_out.at[i], g_out.at[pl.ds(i * step_out, step_out)], sem_out.at[i]
        )
        copy.start()
        copies.append(copy)
        buf_in[i] = dot(x[:, i * step_in : (i + 1) * step_in], grad_high, TN).astype(BF16)
        copy = pltpu.make_async_copy(
            buf_in.at[i], g_in.at[pl.ds(i * step_in, step_in)], sem_in.at[i]
        )
        copy.start()
        copies.append(copy)
    for copy in copies:
        copy.wait()


def logits_kernel(
    split_chips, shares, tok, dout, disp, comb, router_t, terms_out, left, right, ends
):
    images, slots, count = disp.shape
    chips, rows, main = shares.shape
    width = tok.shape[2]
    summed = []
    for slot in range(slots):
        total = shares[slot * split_chips].astype(F32)
        for chip in range(1, split_chips):
            total = total + shares[slot * split_chips + chip].astype(F32)
        summed.append(total)
    unpack(images, ends, jnp.stack(summed))
    stacked = jnp.concatenate(
        [
            jnp.concatenate(summed, axis=0),
            ends[...].reshape(slots * rows, width - main),
        ],
        axis=1,
    )
    stacked_b = stacked.astype(BF16)
    tok_all = tok[...].reshape(images * count, width)
    by_dout = dot(stacked_b, dout[...].reshape(images * count, width), NT)
    by_tok = dot(stacked_b, tok_all, NT)
    grads = []
    for b in range(images):
        span = slice(b * count, (b + 1) * count)
        grad_comb = jnp.concatenate(
            [by_dout[s * rows + b : s * rows + b + 1, span] for s in range(slots)], axis=0
        )
        grad_disp = jnp.concatenate(
            [
                by_tok[s * rows + images + b : s * rows + images + b + 1, span]
                for s in range(slots)
            ],
            axis=0,
        )
        dispatch = disp[b]
        combine = comb[b]
        grads.append(
            dispatch * (grad_disp - jnp.sum(dispatch * grad_disp, axis=1, keepdims=True))
            + combine * (grad_comb - jnp.sum(combine * grad_comb, axis=0, keepdims=True))
        )
    terms = dot(jnp.concatenate(grads, axis=1).astype(BF16), tok_all).astype(BF16)
    terms_out[...] = jnp.broadcast_to(terms[None], terms_out.shape)
    for b in range(images):
        left[b] = jnp.concatenate([disp[b], grads[b]], axis=0)
        right[b] = jnp.concatenate(
            [stacked[s * rows + images + b : s * rows + images + b + 1] for s in range(slots)]
            + [router_t[...].astype(F32)],
            axis=0,
        )


def tokens_kernel(left, right, grad_tokens, buf, sems):
    images, parts = buf.shape[:2]
    step = buf.shape[2]
    copies = []
    for b in range(images):
        rhs = right[b].astype(BF16)
        for i in range(parts):
            lhs = left[b, :, i * step : (i + 1) * step].astype(BF16)
            buf[b, i] = dot(lhs, rhs, TN).astype(BF16)
            copy = pltpu.make_async_copy(
                buf.at[b, i], grad_tokens.at[b, pl.ds(i * step, step)], sems.at[b, i]
            )
            copy.start()
            copies.append(copy)
    for copy in copies:
        copy.wait()


def sum_kernel(terms, total):
    total[...] = jnp.sum(terms[...].astype(F32), axis=0)


def swap_chips(blocks):
    count = lax.axis_size("expert")
    groups = [list(range(core, count, 2)) for core in range(2)]
    return lax.all_to_all(
        blocks, "expert", split_axis=0, concat_axis=0, axis_index_groups=groups, tiled=True
    )


def swap_cores(block):
    count = lax.axis_size("expert")
    return lax.ppermute(block, "expert", [(device, device ^ 1) for device in range(count)])


def per_device(tokens, router, w_in, w_out, d_out):
    devices = lax.axis_size("expert")
    chips = devices // 2
    slots = router.shape[1]
    split_chips = chips // slots
    images, count, width = tokens.shape
    hidden_units = w_in.shape[2]
    rows, main, extra = block_shape(images, width)
    half = chips * rows
    router_t = router.T
    big = images * count * width
    weight = width * hidden_units

    blocks, tok, dout, disp, comb = call(
        rows_kernel,
        (
            vmem_out((slots, rows, main), BF16),
            vmem_out((images, count, width), BF16),
            vmem_out((images, count, width), BF16),
            vmem_out((images, slots, count), F32),
            vmem_out((images, slots, count), F32),
        ),
        tuple(in_hbm(array) for array in (tokens, router_t, d_out)),
        (VMEM,) * 5,
        (HBM,) * 3,
        [
            pltpu.VMEM((slots, width), BF16),
            pltpu.VMEM((slots, rows, main), F32),
            pltpu.SemaphoreType.DMA((2 * images,)),
            pltpu.SemaphoreType.DMA((2,)),
        ],
        (6 * slots * big, 4 * big),
        limit=56 * MIB,
    )
    send = call(
        functools.partial(repeat_kernel, split_chips),
        vmem_out((chips, rows, main), BF16),
        (in_vmem(blocks), in_vmem(tok), in_vmem(dout)),
        VMEM,
        (VMEM,) * 3,
        (),
        (4 * half * weight, 40 * weight),
    )
    near = swap_chips(send)
    far = swap_cores(near)
    w_one, w_two = in_vmem(w_in[0]), in_vmem(w_out[0])
    inner = (
        vmem_out((half, width), BF16),
        vmem_out((half, hidden_units), BF16),
        vmem_out((half, hidden_units), BF16),
    )
    hidden_near = call(
        functools.partial(near_kernel, images),
        inner,
        (in_vmem(near), w_one, w_two),
        (VMEM,) * 3,
        (VMEM,) * 3,
        [pltpu.VMEM((chips, rows, extra), F32)],
        (4 * half * weight, 4 * weight),
    )
    hidden_near = [in_vmem(array) for array in hidden_near]
    other, *hidden_far = call(
        functools.partial(far_kernel, images),
        (vmem_out((chips, rows, main), BF16),) + inner,
        (in_vmem(far), w_one, w_two, hidden_near[1]),
        (VMEM,) * 4,
        (VMEM,) * 4,
        [
            pltpu.VMEM((chips, rows, extra), F32),
            pltpu.VMEM((chips, rows, main), F32),
        ],
        (8 * half * weight, 4 * weight),
    )
    hidden_far = [in_vmem(array) for array in hidden_far]
    received = swap_cores(other)
    own = call(
        functools.partial(own_kernel, images),
        vmem_out((chips, rows, main), F32),
        (hidden_near[1], hidden_near[2], w_one, w_two),
        VMEM,
        (VMEM,) * 4,
        (),
        (4 * half * weight, 4 * weight),
    )
    total = call(
        add_kernel,
        vmem_out((chips, rows, main), BF16),
        (in_vmem(own), in_vmem(received)),
        VMEM,
        (VMEM,) * 2,
        (),
        (half * main, 8 * half * main),
    )
    shares = swap_chips(total)
    parts = 5
    g_in, g_out = call(
        functools.partial(weights_kernel, images),
        (
            jax.ShapeDtypeStruct((width, hidden_units), BF16),
            jax.ShapeDtypeStruct((hidden_units, width), BF16),
        ),
        (*hidden_near, *hidden_far),
        (HBM,) * 2,
        (VMEM,) * 6,
        [
            pltpu.VMEM((parts, width // parts, hidden_units), BF16),
            pltpu.VMEM((parts, hidden_units // parts, width), BF16),
            pltpu.SemaphoreType.DMA((parts,)),
            pltpu.SemaphoreType.DMA((parts,)),
        ],
        (8 * half * weight, 4 * weight),
    )
    terms, left, right = call(
        functools.partial(logits_kernel, split_chips),
        (
            vmem_out((devices, slots, width), BF16),
            vmem_out((images, 2 * slots, count), F32),
            vmem_out((images, 2 * slots, width), F32),
        ),
        (
            in_vmem(shares),
            in_vmem(tok),
            in_vmem(dout),
            in_vmem(disp),
            in_vmem(comb),
            router_t,
        ),
        (VMEM,) * 3,
        (VMEM,) * 6,
        [pltpu.VMEM((slots, rows, extra), F32)],
        (6 * slots * big, 4 * big),
    )
    terms = lax.all_to_all(terms, "expert", split_axis=0, concat_axis=0, tiled=True)
    pieces = 2
    grad_tokens = call(
        tokens_kernel,
        jax.ShapeDtypeStruct(tokens.shape, BF16),
        (in_vmem(left), in_vmem(right)),
        HBM,
        (VMEM,) * 2,
        [
            pltpu.VMEM((images, pieces, count // pieces, width), BF16),
            pltpu.SemaphoreType.DMA((images, pieces)),
        ],
        (4 * slots * big, 2 * big),
    )
    grad_router = call(
        sum_kernel,
        jax.ShapeDtypeStruct((slots, width), F32),
        (in_vmem(terms),),
        VMEM,
        (VMEM,),
        (),
        (devices * slots * width, 2 * devices * slots * width),
    )
    return (grad_tokens, g_in[None], g_out[None], grad_router.T)


def solution(mesh):
    in_specs = (
        P(("groups", "expert"), None, None),
        P(None, "groups"),
        P(("groups", "expert"), None, None),
        P(("groups", "expert"), None, None),
        P(("groups", "expert"), None, None),
    )
    out_specs = (
        P(("groups", "expert"), None, None),
        P(("groups", "expert"), None, None),
        P(("groups", "expert"), None, None),
        P(None, "groups"),
    )
    return jax.shard_map(
        per_device, mesh=mesh, in_specs=in_specs, out_specs=out_specs, check_vma=False
    )
```

```python
import functools

import jax
import jax.numpy as jnp
from jax import lax
from jax.experimental import pallas as pl
from jax.experimental.pallas import tpu as pltpu
from jax.sharding import PartitionSpec as P

F32 = jnp.float32
BF16 = jnp.bfloat16
NT = (((1,), (1,)), ((), ()))
TN = (((0,), (0,)), ((), ()))
NN = (((1,), (0,)), ((), ()))

VMEM = pl.BlockSpec(memory_space=pltpu.VMEM)
HBM = pl.BlockSpec(memory_space=pltpu.HBM)
MIB = 1024 * 1024


def dot(left, right, dims=NN):
    return lax.dot_general(left, right, dims, preferred_element_type=F32)


def in_vmem(array):
    return pltpu.with_memory_space_constraint(array, pltpu.VMEM)


def in_hbm(array):
    return pltpu.with_memory_space_constraint(array, pltpu.HBM)


def vmem_out(shape, dtype):
    return pltpu.VMEM(shape, dtype)


def call(kernel, outs, ins, out_specs, in_specs, scratch=(), cost=None, limit=40 * MIB):
    return pl.pallas_call(
        kernel,
        out_shape=outs,
        in_specs=in_specs,
        out_specs=out_specs,
        scratch_shapes=list(scratch),
        compiler_params=pltpu.CompilerParams(vmem_limit_bytes=limit),
        cost_estimate=pl.CostEstimate(flops=cost[0], bytes_accessed=cost[1], transcendentals=0),
    )(*ins)


def block_shape(images, width):
    extra = width // 5
    main = width - extra
    ends = -(-2 * images * extra // main)
    return -(-(2 * images + ends) // 8) * 8, main, extra


def end_place(images, main, extra, row):
    per = main // extra
    return 2 * images + row // per, row % per * extra


def pack(images, scratch, values):
    main = scratch.shape[2]
    extra = values.shape[2] - main
    scratch[...] = values[:, :, :main]
    for row in range(2 * images):
        to, column = end_place(images, main, extra, row)
        scratch[:, to, column : column + extra] = values[:, row, main:]


def unpack(images, scratch, values):
    main = values.shape[2]
    extra = scratch.shape[2]
    scratch[...] = jnp.zeros_like(scratch)
    for row in range(2 * images):
        at, column = end_place(images, main, extra, row)
        scratch[:, row, :] = values[:, at, column : column + extra]


def rows_kernel(
    tokens,
    router_hbm,
    d_out,
    rows_out,
    tok,
    dout,
    disp_out,
    comb_out,
    router_t,
    block,
    sems,
    other_sems,
):
    images = tok.shape[0]
    main = rows_out.shape[2]
    extra = tok.shape[2] - main
    fetch_router = pltpu.make_async_copy(router_hbm, router_t, other_sems.at[0])
    fetch_router.start()
    fetch_tok = [
        pltpu.make_async_copy(tokens.at[b], tok.at[b], sems.at[b]) for b in range(images)
    ]
    fetch_dout = [
        pltpu.make_async_copy(d_out.at[b], dout.at[b], sems.at[images + b]) for b in range(images)
    ]
    for copy in fetch_tok:
        copy.start()
    block[...] = jnp.zeros_like(block)

    def put(row, values):
        to, column = end_place(images, main, extra, row)
        block[:, row, :] = values[:, :main]
        block[:, to, column : column + extra] = values[:, main:]

    fetch_router.wait()
    logits = {}
    combs = {}
    disps = {}

    def softmaxes(b):
        exps = jnp.exp(logits[b] - jnp.max(logits[b], axis=1, keepdims=True))
        disp = exps * (1.0 / jnp.sum(exps, axis=1, keepdims=True))
        exps = jnp.exp(logits[b] - jnp.max(logits[b], axis=0, keepdims=True))
        comb = exps * (1.0 / jnp.sum(exps, axis=0, keepdims=True))
        disp_out[b] = disp
        comb_out[b] = comb
        disps[b] = disp.astype(BF16)
        combs[b] = comb.astype(BF16)

    for step in range(2 * images):
        if step < images:
            fetch_tok[step].wait()
            if step == 0:
                for copy in fetch_dout:
                    copy.start()
            logits[step] = dot(router_t[...], tok[step], NT)
        else:
            fetch_dout[step - images].wait()
        if 0 <= step - 1 < images:
            softmaxes(step - 1)
        if step >= images:
            put(step, dot(combs[step - images], dout[step - images]))
        if 0 <= step - 2 < images:
            put(step - 2, dot(disps[step - 2], tok[step - 2]))
    for b in range(max(2 * images - 2, 0), images):
        put(b, dot(disps[b], tok[b]))
    rows_out[...] = block[...].astype(BF16)


def repeat_kernel(split_chips, rows, tok, dout, send):
    for slot in range(rows.shape[0]):
        for chip in range(split_chips):
            send[slot * split_chips + chip] = rows[slot]


def hidden_rows(images, blocks, w_in, w_out, x_out, hid_out, grad_out, ends):
    chips, rows, main = blocks.shape
    half = chips * rows
    width = x_out.shape[1]
    unpack(images, ends, blocks[...].astype(F32))
    x = jnp.concatenate(
        [
            blocks[...].reshape(half, main),
            ends[...].reshape(half, width - main).astype(BF16),
        ],
        axis=1,
    )
    x_out[...] = x
    pre = dot(x, w_in[...])
    grad_hidden = dot(x, w_out[...], NT)
    place = lax.broadcasted_iota(jnp.int32, pre.shape, 0) % rows
    slot_row = place < images
    grad_hidden = pltpu.roll(grad_hidden, half - images, 0)
    scale = 0.7978845608028654
    square = pre * pre
    tanh = jnp.tanh(scale * pre * (1.0 + 0.044715 * square))
    cdf = 0.5 * (1.0 + tanh)
    slope = cdf + (0.5 * scale) * pre * (1.0 - tanh * tanh) * (1.0 + (3 * 0.044715) * square)
    hidden = jnp.where(slot_row, pre * cdf, 0.0).astype(BF16)
    grad_pre = jnp.where(slot_row, slope * grad_hidden, 0.0)
    grad_low = pltpu.roll(grad_pre, images, 0).astype(BF16)
    hid_out[...] = hidden
    grad_out[...] = grad_low
    return hidden, grad_low


def near_kernel(images, blocks, w_in, w_out, x_out, hid_out, grad_out, ends):
    hidden_rows(images, blocks, w_in, w_out, x_out, hid_out, grad_out, ends)


def far_kernel(images, blocks, w_in, w_out, _, other, x_out, hid_out, grad_out, ends, packed):
    hidden, grad_low = hidden_rows(images, blocks, w_in, w_out, x_out, hid_out, grad_out, ends)
    shares = dot(hidden, w_out[...]) + dot(grad_low, w_in[...], NT)
    pack(images, packed, shares.reshape(blocks.shape[:2] + (shares.shape[1],)))
    other[...] = packed[...].astype(BF16)


def own_kernel(images, hid, grad, w_in, w_out, own):
    chips, rows, _ = own.shape
    shares = dot(hid[...], w_out[...]) + dot(grad[...], w_in[...], NT)
    pack(images, own, shares.reshape(chips, rows, shares.shape[1]))


def add_kernel(own, received, total):
    total[...] = (own[...] + received[...].astype(F32)).astype(BF16)


def weights_kernel(
    images,
    x_near,
    hid_near,
    grad_near,
    x_far,
    hid_far,
    grad_far,
    g_in,
    g_out,
    buf_in,
    buf_out,
    sem_in,
    sem_out,
):
    parts = buf_in.shape[0]
    step_in = g_in.shape[0] // parts
    step_out = g_out.shape[0] // parts
    x = jnp.concatenate([x_near[...], x_far[...]], axis=0)
    hid = jnp.concatenate([hid_near[...], hid_far[...]], axis=0)
    grad = jnp.concatenate([grad_near[...], grad_far[...]], axis=0)
    hid_low = pltpu.roll(hid.astype(F32), images, 0).astype(BF16)
    grad_high = pltpu.roll(grad.astype(F32), x.shape[0] - images, 0).astype(BF16)
    copies = []
    for i in range(parts):
        buf_out[i] = dot(hid_low[:, i * step_out : (i + 1) * step_out], x, TN).astype(BF16)
        copy = pltpu.make_async_copy(
            buf_out.at[i], g_out.at[pl.ds(i * step_out, step_out)], sem_out.at[i]
        )
        copy.start()
        copies.append(copy)
        buf_in[i] = dot(x[:, i * step_in : (i + 1) * step_in], grad_high, TN).astype(BF16)
        copy = pltpu.make_async_copy(
            buf_in.at[i], g_in.at[pl.ds(i * step_in, step_in)], sem_in.at[i]
        )
        copy.start()
        copies.append(copy)
    for copy in copies:
        copy.wait()


def logits_kernel(
    split_chips, shares, tok, dout, disp, comb, router_t, terms_out, left, right, ends
):
    images, slots, count = disp.shape
    chips, rows, main = shares.shape
    width = tok.shape[2]
    summed = []
    for slot in range(slots):
        total = shares[slot * split_chips].astype(F32)
        for chip in range(1, split_chips):
            total = total + shares[slot * split_chips + chip].astype(F32)
        summed.append(total)
    unpack(images, ends, jnp.stack(summed))
    stacked = jnp.concatenate(
        [
            jnp.concatenate(summed, axis=0),
            ends[...].reshape(slots * rows, width - main),
        ],
        axis=1,
    )
    stacked_b = stacked.astype(BF16)
    by_dout = {}
    by_tok = {}
    grads = {}

    def products(b):
        by_dout[b] = dot(stacked_b, dout[b], NT)
        by_tok[b] = dot(stacked_b, tok[b], NT)

    def logits_grad(b):
        grad_comb = jnp.concatenate(
            [by_dout[b][s * rows + b : s * rows + b + 1] for s in range(slots)], axis=0
        )
        at = images + b
        grad_disp = jnp.concatenate(
            [by_tok[b][s * rows + at : s * rows + at + 1] for s in range(slots)], axis=0
        )
        dispatch = disp[b]
        combine = comb[b]
        grads[b] = dispatch * (
            grad_disp - jnp.sum(dispatch * grad_disp, axis=1, keepdims=True)
        ) + combine * (grad_comb - jnp.sum(combine * grad_comb, axis=0, keepdims=True))

    terms = jnp.zeros((slots, width), F32)
    for step in range(images + 2):
        if step < images:
            products(step)
        if 0 <= step - 1 < images:
            logits_grad(step - 1)
        if 0 <= step - 2 < images:
            terms = terms + dot(grads[step - 2].astype(BF16), tok[step - 2])
    terms = terms.astype(BF16)
    terms_out[...] = jnp.broadcast_to(terms[None], terms_out.shape)
    for b in range(images):
        left[b] = jnp.concatenate([disp[b], grads[b]], axis=0)
        right[b] = jnp.concatenate(
            [stacked[s * rows + images + b : s * rows + images + b + 1] for s in range(slots)]
            + [router_t[...].astype(F32)],
            axis=0,
        )


def tokens_kernel(left, right, grad_tokens, buf, sems):
    images, parts = buf.shape[:2]
    step = buf.shape[2]
    copies = []
    for b in range(images):
        rhs = right[b].astype(BF16)
        for i in range(parts):
            lhs = left[b, :, i * step : (i + 1) * step].astype(BF16)
            buf[b, i] = dot(lhs, rhs, TN).astype(BF16)
            copy = pltpu.make_async_copy(
                buf.at[b, i], grad_tokens.at[b, pl.ds(i * step, step)], sems.at[b, i]
            )
            copy.start()
            copies.append(copy)
    for copy in copies:
        copy.wait()


def sum_kernel(terms, total):
    total[...] = jnp.sum(terms[...].astype(F32), axis=0)


def swap_chips(blocks):
    count = lax.axis_size("expert")
    groups = [list(range(core, count, 2)) for core in range(2)]
    return lax.all_to_all(
        blocks, "expert", split_axis=0, concat_axis=0, axis_index_groups=groups, tiled=True
    )


def swap_cores(block):
    count = lax.axis_size("expert")
    return lax.ppermute(block, "expert", [(device, device ^ 1) for device in range(count)])


def per_device(tokens, router, w_in, w_out, d_out):
    devices = lax.axis_size("expert")
    chips = devices // 2
    slots = router.shape[1]
    split_chips = chips // slots
    images, count, width = tokens.shape
    hidden_units = w_in.shape[2]
    rows, main, extra = block_shape(images, width)
    half = chips * rows
    router_t = router.T
    big = images * count * width
    weight = width * hidden_units

    blocks, tok, dout, disp, comb = call(
        rows_kernel,
        (
            vmem_out((slots, rows, main), BF16),
            vmem_out((images, count, width), BF16),
            vmem_out((images, count, width), BF16),
            vmem_out((images, slots, count), F32),
            vmem_out((images, slots, count), F32),
        ),
        tuple(in_hbm(array) for array in (tokens, router_t, d_out)),
        (VMEM,) * 5,
        (HBM,) * 3,
        [
            pltpu.VMEM((slots, width), BF16),
            pltpu.VMEM((slots, rows, main), F32),
            pltpu.SemaphoreType.DMA((2 * images,)),
            pltpu.SemaphoreType.DMA((2,)),
        ],
        (6 * slots * big, 4 * big),
        limit=56 * MIB,
    )
    send = call(
        functools.partial(repeat_kernel, split_chips),
        vmem_out((chips, rows, main), BF16),
        (in_vmem(blocks), in_vmem(tok), in_vmem(dout)),
        VMEM,
        (VMEM,) * 3,
        (),
        (4 * half * weight, 40 * weight),
    )
    near = swap_chips(send)
    far = swap_cores(near)
    w_one, w_two = in_vmem(w_in[0]), in_vmem(w_out[0])
    inner = (
        vmem_out((half, width), BF16),
        vmem_out((half, hidden_units), BF16),
        vmem_out((half, hidden_units), BF16),
    )
    hidden_near = call(
        functools.partial(near_kernel, images),
        inner,
        (in_vmem(near), w_one, w_two),
        (VMEM,) * 3,
        (VMEM,) * 3,
        [pltpu.VMEM((chips, rows, extra), F32)],
        (4 * half * weight, 4 * weight),
    )
    hidden_near = [in_vmem(array) for array in hidden_near]
    other, *hidden_far = call(
        functools.partial(far_kernel, images),
        (vmem_out((chips, rows, main), BF16),) + inner,
        (in_vmem(far), w_one, w_two, hidden_near[1]),
        (VMEM,) * 4,
        (VMEM,) * 4,
        [
            pltpu.VMEM((chips, rows, extra), F32),
            pltpu.VMEM((chips, rows, main), F32),
        ],
        (8 * half * weight, 4 * weight),
    )
    hidden_far = [in_vmem(array) for array in hidden_far]
    received = swap_cores(other)
    own = call(
        functools.partial(own_kernel, images),
        vmem_out((chips, rows, main), F32),
        (hidden_near[1], hidden_near[2], w_one, w_two),
        VMEM,
        (VMEM,) * 4,
        (),
        (4 * half * weight, 4 * weight),
    )
    total = call(
        add_kernel,
        vmem_out((chips, rows, main), BF16),
        (in_vmem(own), in_vmem(received)),
        VMEM,
        (VMEM,) * 2,
        (),
        (half * main, 8 * half * main),
    )
    shares = swap_chips(total)
    parts = 5
    g_in, g_out = call(
        functools.partial(weights_kernel, images),
        (
            jax.ShapeDtypeStruct((width, hidden_units), BF16),
            jax.ShapeDtypeStruct((hidden_units, width), BF16),
        ),
        (*hidden_near, *hidden_far),
        (HBM,) * 2,
        (VMEM,) * 6,
        [
            pltpu.VMEM((parts, width // parts, hidden_units), BF16),
            pltpu.VMEM((parts, hidden_units // parts, width), BF16),
            pltpu.SemaphoreType.DMA((parts,)),
            pltpu.SemaphoreType.DMA((parts,)),
        ],
        (8 * half * weight, 4 * weight),
    )
    terms, left, right = call(
        functools.partial(logits_kernel, split_chips),
        (
            vmem_out((devices, slots, width), BF16),
            vmem_out((images, 2 * slots, count), F32),
            vmem_out((images, 2 * slots, width), F32),
        ),
        (
            in_vmem(shares),
            in_vmem(tok),
            in_vmem(dout),
            in_vmem(disp),
            in_vmem(comb),
            router_t,
        ),
        (VMEM,) * 3,
        (VMEM,) * 6,
        [pltpu.VMEM((slots, rows, extra), F32)],
        (6 * slots * big, 4 * big),
    )
    terms = lax.all_to_all(terms, "expert", split_axis=0, concat_axis=0, tiled=True)
    pieces = 2
    grad_tokens = call(
        tokens_kernel,
        jax.ShapeDtypeStruct(tokens.shape, BF16),
        (in_vmem(left), in_vmem(right)),
        HBM,
        (VMEM,) * 2,
        [
            pltpu.VMEM((images, pieces, count // pieces, width), BF16),
            pltpu.SemaphoreType.DMA((images, pieces)),
        ],
        (4 * slots * big, 2 * big),
    )
    grad_router = call(
        sum_kernel,
        jax.ShapeDtypeStruct((slots, width), F32),
        (in_vmem(terms),),
        VMEM,
        (VMEM,),
        (),
        (devices * slots * width, 2 * devices * slots * width),
    )
    return (grad_tokens, g_in[None], g_out[None], grad_router.T)


def solution(mesh):
    in_specs = (
        P(("groups", "expert"), None, None),
        P(None, "groups"),
        P(("groups", "expert"), None, None),
        P(("groups", "expert"), None, None),
        P(("groups", "expert"), None, None),
    )
    out_specs = (
        P(("groups", "expert"), None, None),
        P(("groups", "expert"), None, None),
        P(("groups", "expert"), None, None),
        P(None, "groups"),
    )
    return jax.shard_map(
        per_device, mesh=mesh, in_specs=in_specs, out_specs=out_specs, check_vma=False
    )
```

```python
import functools

import jax
import jax.numpy as jnp
from jax import lax
from jax.experimental import pallas as pl
from jax.experimental.pallas import tpu as pltpu
from jax.sharding import PartitionSpec as P

F32 = jnp.float32
BF16 = jnp.bfloat16
NT = (((1,), (1,)), ((), ()))
TN = (((0,), (0,)), ((), ()))
NN = (((1,), (0,)), ((), ()))

VMEM = pl.BlockSpec(memory_space=pltpu.VMEM)
HBM = pl.BlockSpec(memory_space=pltpu.HBM)
MIB = 1024 * 1024


def dot(left, right, dims=NN):
    return lax.dot_general(left, right, dims, preferred_element_type=F32)


def in_vmem(array):
    return pltpu.with_memory_space_constraint(array, pltpu.VMEM)


def in_hbm(array):
    return pltpu.with_memory_space_constraint(array, pltpu.HBM)


def vmem_out(shape, dtype):
    return pltpu.VMEM(shape, dtype)


def call(kernel, outs, ins, out_specs, in_specs, scratch=(), cost=None, limit=40 * MIB):
    return pl.pallas_call(
        kernel,
        out_shape=outs,
        in_specs=in_specs,
        out_specs=out_specs,
        scratch_shapes=list(scratch),
        compiler_params=pltpu.CompilerParams(vmem_limit_bytes=limit),
        cost_estimate=pl.CostEstimate(flops=cost[0], bytes_accessed=cost[1], transcendentals=0),
    )(*ins)


def block_shape(images, width):
    extra = width // 5
    main = width - extra
    ends = -(-2 * images * extra // main)
    return -(-(2 * images + ends) // 8) * 8, main, extra


def end_place(images, main, extra, row):
    per = main // extra
    return 2 * images + row // per, row % per * extra


def pack(images, scratch, values):
    main = scratch.shape[2]
    extra = values.shape[2] - main
    scratch[...] = values[:, :, :main]
    for row in range(2 * images):
        to, column = end_place(images, main, extra, row)
        scratch[:, to, column : column + extra] = values[:, row, main:]


def unpack(images, scratch, values):
    main = values.shape[2]
    extra = scratch.shape[2]
    scratch[...] = jnp.zeros_like(scratch)
    for row in range(2 * images):
        at, column = end_place(images, main, extra, row)
        scratch[:, row, :] = values[:, at, column : column + extra]


def rows_kernel(
    tokens,
    router_hbm,
    d_out,
    w_in,
    rows_out,
    tok,
    dout,
    disp_out,
    comb_out,
    w_one,
    router_t,
    block,
    sems,
    other_sems,
):
    images = tok.shape[0]
    main = rows_out.shape[2]
    extra = tok.shape[2] - main
    fetch_router = pltpu.make_async_copy(router_hbm, router_t, other_sems.at[0])
    fetch_router.start()
    fetch_tok = [
        pltpu.make_async_copy(tokens.at[b], tok.at[b], sems.at[b]) for b in range(images)
    ]
    fetch_dout = [
        pltpu.make_async_copy(d_out.at[b], dout.at[b], sems.at[images + b]) for b in range(images)
    ]
    fetch_weight = pltpu.make_async_copy(w_in, w_one, other_sems.at[1])
    for copy in fetch_tok:
        copy.start()
    block[...] = jnp.zeros_like(block)

    def put(row, values):
        to, column = end_place(images, main, extra, row)
        block[:, row, :] = values[:, :main]
        block[:, to, column : column + extra] = values[:, main:]

    fetch_router.wait()
    logits = {}
    combs = {}
    disps = {}

    def softmaxes(b):
        exps = jnp.exp(logits[b] - jnp.max(logits[b], axis=1, keepdims=True))
        disp = exps * (1.0 / jnp.sum(exps, axis=1, keepdims=True))
        exps = jnp.exp(logits[b] - jnp.max(logits[b], axis=0, keepdims=True))
        comb = exps * (1.0 / jnp.sum(exps, axis=0, keepdims=True))
        disp_out[b] = disp
        comb_out[b] = comb
        disps[b] = disp.astype(BF16)
        combs[b] = comb.astype(BF16)

    for step in range(2 * images):
        if step < images:
            fetch_tok[step].wait()
            if step == 0:
                for copy in fetch_dout:
                    copy.start()
            logits[step] = dot(router_t[...], tok[step], NT)
        else:
            fetch_dout[step - images].wait()
            if step == images:
                fetch_weight.start()
        if 0 <= step - 1 < images:
            softmaxes(step - 1)
        if step >= images:
            put(step, dot(combs[step - images], dout[step - images]))
        if 0 <= step - 2 < images:
            put(step - 2, dot(disps[step - 2], tok[step - 2]))
    for b in range(max(2 * images - 2, 0), images):
        put(b, dot(disps[b], tok[b]))
    rows_out[...] = block[...].astype(BF16)
    fetch_weight.wait()


def repeat_kernel(split_chips, rows, tok, dout, send):
    for slot in range(rows.shape[0]):
        for chip in range(split_chips):
            send[slot * split_chips + chip] = rows[slot]


def hidden_rows(images, blocks, w_in, w_out, x_out, hid_out, grad_out, ends):
    chips, rows, main = blocks.shape
    half = chips * rows
    width = x_out.shape[1]
    unpack(images, ends, blocks[...].astype(F32))
    x = jnp.concatenate(
        [
            blocks[...].reshape(half, main),
            ends[...].reshape(half, width - main).astype(BF16),
        ],
        axis=1,
    )
    x_out[...] = x
    pre = dot(x, w_in[...])
    grad_hidden = dot(x, w_out[...], NT)
    place = lax.broadcasted_iota(jnp.int32, pre.shape, 0) % rows
    slot_row = place < images
    grad_hidden = pltpu.roll(grad_hidden, half - images, 0)
    scale = 0.7978845608028654
    square = pre * pre
    tanh = jnp.tanh(scale * pre * (1.0 + 0.044715 * square))
    cdf = 0.5 * (1.0 + tanh)
    slope = cdf + (0.5 * scale) * pre * (1.0 - tanh * tanh) * (1.0 + (3 * 0.044715) * square)
    hidden = jnp.where(slot_row, pre * cdf, 0.0).astype(BF16)
    grad_pre = jnp.where(slot_row, slope * grad_hidden, 0.0)
    grad_low = pltpu.roll(grad_pre, images, 0).astype(BF16)
    hid_out[...] = hidden
    grad_out[...] = grad_low
    return hidden, grad_low


def near_kernel(images, blocks, w_in, w_out, x_out, hid_out, grad_out, ends):
    hidden_rows(images, blocks, w_in, w_out, x_out, hid_out, grad_out, ends)


def far_kernel(images, blocks, w_in, w_out, _, other, x_out, hid_out, grad_out, ends, packed):
    hidden, grad_low = hidden_rows(images, blocks, w_in, w_out, x_out, hid_out, grad_out, ends)
    shares = dot(hidden, w_out[...]) + dot(grad_low, w_in[...], NT)
    pack(images, packed, shares.reshape(blocks.shape[:2] + (shares.shape[1],)))
    other[...] = packed[...].astype(BF16)


def own_kernel(images, hid, grad, w_in, w_out, own):
    chips, rows, _ = own.shape
    shares = dot(hid[...], w_out[...]) + dot(grad[...], w_in[...], NT)
    pack(images, own, shares.reshape(chips, rows, shares.shape[1]))


def add_kernel(own, received, total):
    total[...] = (own[...] + received[...].astype(F32)).astype(BF16)


def weights_kernel(
    images,
    x_near,
    hid_near,
    grad_near,
    x_far,
    hid_far,
    grad_far,
    g_in,
    g_out,
    buf_in,
    buf_out,
    sem_in,
    sem_out,
):
    parts = buf_in.shape[0]
    step_in = g_in.shape[0] // parts
    step_out = g_out.shape[0] // parts
    x = jnp.concatenate([x_near[...], x_far[...]], axis=0)
    hid = jnp.concatenate([hid_near[...], hid_far[...]], axis=0)
    grad = jnp.concatenate([grad_near[...], grad_far[...]], axis=0)
    hid_low = pltpu.roll(hid.astype(F32), images, 0).astype(BF16)
    grad_high = pltpu.roll(grad.astype(F32), x.shape[0] - images, 0).astype(BF16)
    copies = []
    for i in range(parts):
        buf_out[i] = dot(hid_low[:, i * step_out : (i + 1) * step_out], x, TN).astype(BF16)
        copy = pltpu.make_async_copy(
            buf_out.at[i], g_out.at[pl.ds(i * step_out, step_out)], sem_out.at[i]
        )
        copy.start()
        copies.append(copy)
        buf_in[i] = dot(x[:, i * step_in : (i + 1) * step_in], grad_high, TN).astype(BF16)
        copy = pltpu.make_async_copy(
            buf_in.at[i], g_in.at[pl.ds(i * step_in, step_in)], sem_in.at[i]
        )
        copy.start()
        copies.append(copy)
    for copy in copies:
        copy.wait()


def logits_kernel(
    split_chips, shares, tok, dout, disp, comb, router_t, terms_out, left, right, ends
):
    images, slots, count = disp.shape
    chips, rows, main = shares.shape
    width = tok.shape[2]
    summed = []
    for slot in range(slots):
        total = shares[slot * split_chips].astype(F32)
        for chip in range(1, split_chips):
            total = total + shares[slot * split_chips + chip].astype(F32)
        summed.append(total)
    unpack(images, ends, jnp.stack(summed))
    stacked = jnp.concatenate(
        [
            jnp.concatenate(summed, axis=0),
            ends[...].reshape(slots * rows, width - main),
        ],
        axis=1,
    )
    stacked_b = stacked.astype(BF16)
    by_dout = {}
    by_tok = {}
    grads = {}

    def products(b):
        by_dout[b] = dot(stacked_b, dout[b], NT)
        by_tok[b] = dot(stacked_b, tok[b], NT)

    def logits_grad(b):
        grad_comb = jnp.concatenate(
            [by_dout[b][s * rows + b : s * rows + b + 1] for s in range(slots)], axis=0
        )
        at = images + b
        grad_disp = jnp.concatenate(
            [by_tok[b][s * rows + at : s * rows + at + 1] for s in range(slots)], axis=0
        )
        dispatch = disp[b]
        combine = comb[b]
        grads[b] = dispatch * (
            grad_disp - jnp.sum(dispatch * grad_disp, axis=1, keepdims=True)
        ) + combine * (grad_comb - jnp.sum(combine * grad_comb, axis=0, keepdims=True))

    terms = jnp.zeros((slots, width), F32)
    for step in range(images + 2):
        if step < images:
            products(step)
        if 0 <= step - 1 < images:
            logits_grad(step - 1)
        if 0 <= step - 2 < images:
            terms = terms + dot(grads[step - 2].astype(BF16), tok[step - 2])
    terms = terms.astype(BF16)
    terms_out[...] = jnp.broadcast_to(terms[None], terms_out.shape)
    for b in range(images):
        left[b] = jnp.concatenate([disp[b], grads[b]], axis=0)
        right[b] = jnp.concatenate(
            [stacked[s * rows + images + b : s * rows + images + b + 1] for s in range(slots)]
            + [router_t[...].astype(F32)],
            axis=0,
        )


def tokens_kernel(left, right, grad_tokens, buf, sems):
    images, parts = buf.shape[:2]
    step = buf.shape[2]
    copies = []
    for b in range(images):
        rhs = right[b].astype(BF16)
        for i in range(parts):
            lhs = left[b, :, i * step : (i + 1) * step].astype(BF16)
            buf[b, i] = dot(lhs, rhs, TN).astype(BF16)
            copy = pltpu.make_async_copy(
                buf.at[b, i], grad_tokens.at[b, pl.ds(i * step, step)], sems.at[b, i]
            )
            copy.start()
            copies.append(copy)
    for copy in copies:
        copy.wait()


def sum_kernel(terms, total):
    total[...] = jnp.sum(terms[...].astype(F32), axis=0)


def swap_chips(blocks):
    count = lax.axis_size("expert")
    groups = [list(range(core, count, 2)) for core in range(2)]
    return lax.all_to_all(
        blocks, "expert", split_axis=0, concat_axis=0, axis_index_groups=groups, tiled=True
    )


def swap_cores(block):
    count = lax.axis_size("expert")
    return lax.ppermute(block, "expert", [(device, device ^ 1) for device in range(count)])


def per_device(tokens, router, w_in, w_out, d_out):
    devices = lax.axis_size("expert")
    chips = devices // 2
    slots = router.shape[1]
    split_chips = chips // slots
    images, count, width = tokens.shape
    hidden_units = w_in.shape[2]
    rows, main, extra = block_shape(images, width)
    half = chips * rows
    router_t = router.T
    big = images * count * width
    weight = width * hidden_units

    blocks, tok, dout, disp, comb, w_one = call(
        rows_kernel,
        (
            vmem_out((slots, rows, main), BF16),
            vmem_out((images, count, width), BF16),
            vmem_out((images, count, width), BF16),
            vmem_out((images, slots, count), F32),
            vmem_out((images, slots, count), F32),
            vmem_out(w_in.shape[1:], BF16),
        ),
        tuple(in_hbm(array) for array in (tokens, router_t, d_out, w_in[0])),
        (VMEM,) * 6,
        (HBM,) * 4,
        [
            pltpu.VMEM((slots, width), BF16),
            pltpu.VMEM((slots, rows, main), F32),
            pltpu.SemaphoreType.DMA((2 * images,)),
            pltpu.SemaphoreType.DMA((2,)),
        ],
        (6 * slots * big, 4 * big),
        limit=58 * MIB,
    )
    send = call(
        functools.partial(repeat_kernel, split_chips),
        vmem_out((chips, rows, main), BF16),
        (in_vmem(blocks), in_vmem(tok), in_vmem(dout)),
        VMEM,
        (VMEM,) * 3,
        (),
        (4 * half * weight, 40 * weight),
    )
    near = swap_chips(send)
    far = swap_cores(near)
    w_one, w_two = in_vmem(w_one), in_vmem(w_out[0])
    inner = (
        vmem_out((half, width), BF16),
        vmem_out((half, hidden_units), BF16),
        vmem_out((half, hidden_units), BF16),
    )
    hidden_near = call(
        functools.partial(near_kernel, images),
        inner,
        (in_vmem(near), w_one, w_two),
        (VMEM,) * 3,
        (VMEM,) * 3,
        [pltpu.VMEM((chips, rows, extra), F32)],
        (4 * half * weight, 4 * weight),
    )
    hidden_near = [in_vmem(array) for array in hidden_near]
    other, *hidden_far = call(
        functools.partial(far_kernel, images),
        (vmem_out((chips, rows, main), BF16),) + inner,
        (in_vmem(far), w_one, w_two, hidden_near[1]),
        (VMEM,) * 4,
        (VMEM,) * 4,
        [
            pltpu.VMEM((chips, rows, extra), F32),
            pltpu.VMEM((chips, rows, main), F32),
        ],
        (8 * half * weight, 4 * weight),
    )
    hidden_far = [in_vmem(array) for array in hidden_far]
    received = swap_cores(other)
    own = call(
        functools.partial(own_kernel, images),
        vmem_out((chips, rows, main), F32),
        (hidden_near[1], hidden_near[2], w_one, w_two),
        VMEM,
        (VMEM,) * 4,
        (),
        (4 * half * weight, 4 * weight),
    )
    total = call(
        add_kernel,
        vmem_out((chips, rows, main), BF16),
        (in_vmem(own), in_vmem(received)),
        VMEM,
        (VMEM,) * 2,
        (),
        (half * main, 8 * half * main),
    )
    shares = swap_chips(total)
    parts = 5
    g_in, g_out = call(
        functools.partial(weights_kernel, images),
        (
            jax.ShapeDtypeStruct((width, hidden_units), BF16),
            jax.ShapeDtypeStruct((hidden_units, width), BF16),
        ),
        (*hidden_near, *hidden_far),
        (HBM,) * 2,
        (VMEM,) * 6,
        [
            pltpu.VMEM((parts, width // parts, hidden_units), BF16),
            pltpu.VMEM((parts, hidden_units // parts, width), BF16),
            pltpu.SemaphoreType.DMA((parts,)),
            pltpu.SemaphoreType.DMA((parts,)),
        ],
        (8 * half * weight, 4 * weight),
    )
    terms, left, right = call(
        functools.partial(logits_kernel, split_chips),
        (
            vmem_out((devices, slots, width), BF16),
            vmem_out((images, 2 * slots, count), F32),
            vmem_out((images, 2 * slots, width), F32),
        ),
        (
            in_vmem(shares),
            in_vmem(tok),
            in_vmem(dout),
            in_vmem(disp),
            in_vmem(comb),
            router_t,
        ),
        (VMEM,) * 3,
        (VMEM,) * 6,
        [pltpu.VMEM((slots, rows, extra), F32)],
        (6 * slots * big, 4 * big),
    )
    terms = lax.all_to_all(terms, "expert", split_axis=0, concat_axis=0, tiled=True)
    pieces = 2
    grad_tokens = call(
        tokens_kernel,
        jax.ShapeDtypeStruct(tokens.shape, BF16),
        (in_vmem(left), in_vmem(right)),
        HBM,
        (VMEM,) * 2,
        [
            pltpu.VMEM((images, pieces, count // pieces, width), BF16),
            pltpu.SemaphoreType.DMA((images, pieces)),
        ],
        (4 * slots * big, 2 * big),
    )
    grad_router = call(
        sum_kernel,
        jax.ShapeDtypeStruct((slots, width), F32),
        (in_vmem(terms),),
        VMEM,
        (VMEM,),
        (),
        (devices * slots * width, 2 * devices * slots * width),
    )
    return (grad_tokens, g_in[None], g_out[None], grad_router.T)


def solution(mesh):
    in_specs = (
        P(("groups", "expert"), None, None),
        P(None, "groups"),
        P(("groups", "expert"), None, None),
        P(("groups", "expert"), None, None),
        P(("groups", "expert"), None, None),
    )
    out_specs = (
        P(("groups", "expert"), None, None),
        P(("groups", "expert"), None, None),
        P(("groups", "expert"), None, None),
        P(None, "groups"),
    )
    return jax.shard_map(
        per_device, mesh=mesh, in_specs=in_specs, out_specs=out_specs, check_vma=False
    )
```

```python
import functools

import jax
import jax.numpy as jnp
from jax import lax
from jax.experimental import pallas as pl
from jax.experimental.pallas import tpu as pltpu
from jax.sharding import PartitionSpec as P

F32 = jnp.float32
BF16 = jnp.bfloat16
NT = (((1,), (1,)), ((), ()))
TN = (((0,), (0,)), ((), ()))
NN = (((1,), (0,)), ((), ()))

VMEM = pl.BlockSpec(memory_space=pltpu.VMEM)
HBM = pl.BlockSpec(memory_space=pltpu.HBM)
MIB = 1024 * 1024


def dot(left, right, dims=NN):
    return lax.dot_general(left, right, dims, preferred_element_type=F32)


def in_vmem(array):
    return pltpu.with_memory_space_constraint(array, pltpu.VMEM)


def in_hbm(array):
    return pltpu.with_memory_space_constraint(array, pltpu.HBM)


def vmem_out(shape, dtype):
    return pltpu.VMEM(shape, dtype)


def call(kernel, outs, ins, out_specs, in_specs, scratch=(), cost=None, limit=40 * MIB):
    return pl.pallas_call(
        kernel,
        out_shape=outs,
        in_specs=in_specs,
        out_specs=out_specs,
        scratch_shapes=list(scratch),
        compiler_params=pltpu.CompilerParams(vmem_limit_bytes=limit),
        cost_estimate=pl.CostEstimate(flops=cost[0], bytes_accessed=cost[1], transcendentals=0),
    )(*ins)


def block_shape(images, width):
    extra = width // 5
    main = width - extra
    ends = -(-2 * images * extra // main)
    return -(-(2 * images + ends) // 8) * 8, main, extra


def end_place(images, main, extra, row):
    per = main // extra
    return 2 * images + row // per, row % per * extra


def pack(images, scratch, values):
    main = scratch.shape[2]
    extra = values.shape[2] - main
    scratch[...] = values[:, :, :main]
    for row in range(2 * images):
        to, column = end_place(images, main, extra, row)
        scratch[:, to, column : column + extra] = values[:, row, main:]


def unpack(images, scratch, values):
    main = values.shape[2]
    extra = scratch.shape[2]
    scratch[...] = jnp.zeros_like(scratch)
    for row in range(2 * images):
        at, column = end_place(images, main, extra, row)
        scratch[:, row, :] = values[:, at, column : column + extra]


def rows_kernel(
    tokens,
    router_hbm,
    d_out,
    rows_out,
    tok,
    dout,
    disp_out,
    comb_out,
    router_t,
    block,
    sems,
    other_sems,
):
    images = tok.shape[0]
    main = rows_out.shape[2]
    extra = tok.shape[2] - main
    fetch_router = pltpu.make_async_copy(router_hbm, router_t, other_sems.at[0])
    fetch_router.start()
    fetch_tok = [
        pltpu.make_async_copy(tokens.at[b], tok.at[b], sems.at[b]) for b in range(images)
    ]
    fetch_dout = [
        pltpu.make_async_copy(d_out.at[b], dout.at[b], sems.at[images + b]) for b in range(images)
    ]
    for copy in fetch_tok + fetch_dout:
        copy.start()
    block[...] = jnp.zeros_like(block)

    def put(row, values):
        to, column = end_place(images, main, extra, row)
        block[:, row, :] = values[:, :main]
        block[:, to, column : column + extra] = values[:, main:]

    fetch_router.wait()
    logits = {}
    combs = {}
    disps = {}

    def softmaxes(b):
        exps = jnp.exp(logits[b] - jnp.max(logits[b], axis=1, keepdims=True))
        disp = exps * (1.0 / jnp.sum(exps, axis=1, keepdims=True))
        exps = jnp.exp(logits[b] - jnp.max(logits[b], axis=0, keepdims=True))
        comb = exps * (1.0 / jnp.sum(exps, axis=0, keepdims=True))
        disp_out[b] = disp
        comb_out[b] = comb
        disps[b] = disp.astype(BF16)
        combs[b] = comb.astype(BF16)

    for step in range(2 * images):
        if step < images:
            fetch_tok[step].wait()
            logits[step] = dot(router_t[...], tok[step], NT)
        if 0 <= step - 1 < images:
            softmaxes(step - 1)
        if 0 <= step - 2 < images:
            put(step - 2, dot(disps[step - 2], tok[step - 2]))
        if step >= images:
            fetch_dout[step - images].wait()
            put(step, dot(combs[step - images], dout[step - images]))
    for b in range(max(2 * images - 2, 0), images):
        put(b, dot(disps[b], tok[b]))
    rows_out[...] = block[...].astype(BF16)


def repeat_kernel(split_chips, rows, tok, dout, send):
    for slot in range(rows.shape[0]):
        for chip in range(split_chips):
            send[slot * split_chips + chip] = rows[slot]


def hidden_rows(images, blocks, w_in, w_out, x_out, hid_out, grad_out, ends):
    chips, rows, main = blocks.shape
    half = chips * rows
    width = x_out.shape[1]
    unpack(images, ends, blocks[...].astype(F32))
    x = jnp.concatenate(
        [
            blocks[...].reshape(half, main),
            ends[...].reshape(half, width - main).astype(BF16),
        ],
        axis=1,
    )
    x_out[...] = x
    pre = dot(x, w_in[...])
    grad_hidden = dot(x, w_out[...], NT)
    place = lax.broadcasted_iota(jnp.int32, pre.shape, 0) % rows
    slot_row = place < images
    grad_hidden = pltpu.roll(grad_hidden, half - images, 0)
    scale = 0.7978845608028654
    square = pre * pre
    tanh = jnp.tanh(scale * pre * (1.0 + 0.044715 * square))
    cdf = 0.5 * (1.0 + tanh)
    slope = cdf + (0.5 * scale) * pre * (1.0 - tanh * tanh) * (1.0 + (3 * 0.044715) * square)
    hidden = jnp.where(slot_row, pre * cdf, 0.0).astype(BF16)
    grad_pre = jnp.where(slot_row, slope * grad_hidden, 0.0)
    grad_low = pltpu.roll(grad_pre, images, 0).astype(BF16)
    hid_out[...] = hidden
    grad_out[...] = grad_low
    return hidden, grad_low


def near_kernel(images, blocks, w_in, w_out, x_out, hid_out, grad_out, ends):
    hidden_rows(images, blocks, w_in, w_out, x_out, hid_out, grad_out, ends)


def far_kernel(images, blocks, w_in, w_out, _, other, x_out, hid_out, grad_out, ends, packed):
    hidden, grad_low = hidden_rows(images, blocks, w_in, w_out, x_out, hid_out, grad_out, ends)
    shares = dot(hidden, w_out[...]) + dot(grad_low, w_in[...], NT)
    pack(images, packed, shares.reshape(blocks.shape[:2] + (shares.shape[1],)))
    other[...] = packed[...].astype(BF16)


def own_kernel(images, hid, grad, w_in, w_out, own):
    chips, rows, _ = own.shape
    shares = dot(hid[...], w_out[...]) + dot(grad[...], w_in[...], NT)
    pack(images, own, shares.reshape(chips, rows, shares.shape[1]))


def add_kernel(own, received, total):
    total[...] = (own[...] + received[...].astype(F32)).astype(BF16)


def weights_kernel(
    images,
    x_near,
    hid_near,
    grad_near,
    x_far,
    hid_far,
    grad_far,
    g_in,
    g_out,
    buf_in,
    buf_out,
    sem_in,
    sem_out,
):
    parts = buf_in.shape[0]
    step_in = g_in.shape[0] // parts
    step_out = g_out.shape[0] // parts
    x = jnp.concatenate([x_near[...], x_far[...]], axis=0)
    hid = jnp.concatenate([hid_near[...], hid_far[...]], axis=0)
    grad = jnp.concatenate([grad_near[...], grad_far[...]], axis=0)
    hid_low = pltpu.roll(hid.astype(F32), images, 0).astype(BF16)
    grad_high = pltpu.roll(grad.astype(F32), x.shape[0] - images, 0).astype(BF16)
    copies = []
    for i in range(parts):
        buf_out[i] = dot(hid_low[:, i * step_out : (i + 1) * step_out], x, TN).astype(BF16)
        copy = pltpu.make_async_copy(
            buf_out.at[i], g_out.at[pl.ds(i * step_out, step_out)], sem_out.at[i]
        )
        copy.start()
        copies.append(copy)
        buf_in[i] = dot(x[:, i * step_in : (i + 1) * step_in], grad_high, TN).astype(BF16)
        copy = pltpu.make_async_copy(
            buf_in.at[i], g_in.at[pl.ds(i * step_in, step_in)], sem_in.at[i]
        )
        copy.start()
        copies.append(copy)
    for copy in copies:
        copy.wait()


def logits_kernel(
    split_chips, shares, tok, dout, disp, comb, router_t, terms_out, left, right, ends
):
    images, slots, count = disp.shape
    chips, rows, main = shares.shape
    width = tok.shape[2]
    summed = []
    for slot in range(slots):
        total = shares[slot * split_chips].astype(F32)
        for chip in range(1, split_chips):
            total = total + shares[slot * split_chips + chip].astype(F32)
        summed.append(total)
    unpack(images, ends, jnp.stack(summed))
    stacked = jnp.concatenate(
        [
            jnp.concatenate(summed, axis=0),
            ends[...].reshape(slots * rows, width - main),
        ],
        axis=1,
    )
    stacked_b = stacked.astype(BF16)
    by_dout = {}
    by_tok = {}
    grads = {}

    def products(b):
        by_dout[b] = dot(stacked_b, dout[b], NT)
        by_tok[b] = dot(stacked_b, tok[b], NT)

    def logits_grad(b):
        grad_comb = jnp.concatenate(
            [by_dout[b][s * rows + b : s * rows + b + 1] for s in range(slots)], axis=0
        )
        at = images + b
        grad_disp = jnp.concatenate(
            [by_tok[b][s * rows + at : s * rows + at + 1] for s in range(slots)], axis=0
        )
        dispatch = disp[b]
        combine = comb[b]
        grads[b] = dispatch * (
            grad_disp - jnp.sum(dispatch * grad_disp, axis=1, keepdims=True)
        ) + combine * (grad_comb - jnp.sum(combine * grad_comb, axis=0, keepdims=True))

    terms = jnp.zeros((slots, width), F32)
    for step in range(images + 2):
        if step < images:
            products(step)
        if 0 <= step - 1 < images:
            logits_grad(step - 1)
        if 0 <= step - 2 < images:
            terms = terms + dot(grads[step - 2].astype(BF16), tok[step - 2])
    terms = terms.astype(BF16)
    terms_out[...] = jnp.broadcast_to(terms[None], terms_out.shape)
    for b in range(images):
        left[b] = jnp.concatenate([disp[b], grads[b]], axis=0)
        right[b] = jnp.concatenate(
            [stacked[s * rows + images + b : s * rows + images + b + 1] for s in range(slots)]
            + [router_t[...].astype(F32)],
            axis=0,
        )


def tokens_kernel(left, right, grad_tokens, buf, sems):
    images, parts = buf.shape[:2]
    step = buf.shape[2]
    copies = []
    for b in range(images):
        rhs = right[b].astype(BF16)
        for i in range(parts):
            lhs = left[b, :, i * step : (i + 1) * step].astype(BF16)
            buf[b, i] = dot(lhs, rhs, TN).astype(BF16)
            copy = pltpu.make_async_copy(
                buf.at[b, i], grad_tokens.at[b, pl.ds(i * step, step)], sems.at[b, i]
            )
            copy.start()
            copies.append(copy)
    for copy in copies:
        copy.wait()


def sum_kernel(terms, total):
    total[...] = jnp.sum(terms[...].astype(F32), axis=0)


def swap_chips(blocks):
    count = lax.axis_size("expert")
    groups = [list(range(core, count, 2)) for core in range(2)]
    return lax.all_to_all(
        blocks, "expert", split_axis=0, concat_axis=0, axis_index_groups=groups, tiled=True
    )


def swap_cores(block):
    count = lax.axis_size("expert")
    return lax.ppermute(block, "expert", [(device, device ^ 1) for device in range(count)])


def per_device(tokens, router, w_in, w_out, d_out):
    devices = lax.axis_size("expert")
    chips = devices // 2
    slots = router.shape[1]
    split_chips = chips // slots
    images, count, width = tokens.shape
    hidden_units = w_in.shape[2]
    rows, main, extra = block_shape(images, width)
    half = chips * rows
    router_t = router.T
    big = images * count * width
    weight = width * hidden_units

    blocks, tok, dout, disp, comb = call(
        rows_kernel,
        (
            vmem_out((slots, rows, main), BF16),
            vmem_out((images, count, width), BF16),
            vmem_out((images, count, width), BF16),
            vmem_out((images, slots, count), F32),
            vmem_out((images, slots, count), F32),
        ),
        tuple(in_hbm(array) for array in (tokens, router_t, d_out)),
        (VMEM,) * 5,
        (HBM,) * 3,
        [
            pltpu.VMEM((slots, width), BF16),
            pltpu.VMEM((slots, rows, main), F32),
            pltpu.SemaphoreType.DMA((2 * images,)),
            pltpu.SemaphoreType.DMA((2,)),
        ],
        (6 * slots * big, 4 * big),
        limit=56 * MIB,
    )
    send = call(
        functools.partial(repeat_kernel, split_chips),
        vmem_out((chips, rows, main), BF16),
        (in_vmem(blocks), in_vmem(tok), in_vmem(dout)),
        VMEM,
        (VMEM,) * 3,
        (),
        (4 * half * weight, 40 * weight),
    )
    near = swap_chips(send)
    far = swap_cores(near)
    w_one, w_two = in_vmem(w_in[0]), in_vmem(w_out[0])
    inner = (
        vmem_out((half, width), BF16),
        vmem_out((half, hidden_units), BF16),
        vmem_out((half, hidden_units), BF16),
    )
    hidden_near = call(
        functools.partial(near_kernel, images),
        inner,
        (in_vmem(near), w_one, w_two),
        (VMEM,) * 3,
        (VMEM,) * 3,
        [pltpu.VMEM((chips, rows, extra), F32)],
        (4 * half * weight, 4 * weight),
    )
    hidden_near = [in_vmem(array) for array in hidden_near]
    other, *hidden_far = call(
        functools.partial(far_kernel, images),
        (vmem_out((chips, rows, main), BF16),) + inner,
        (in_vmem(far), w_one, w_two, hidden_near[1]),
        (VMEM,) * 4,
        (VMEM,) * 4,
        [
            pltpu.VMEM((chips, rows, extra), F32),
            pltpu.VMEM((chips, rows, main), F32),
        ],
        (8 * half * weight, 4 * weight),
    )
    hidden_far = [in_vmem(array) for array in hidden_far]
    received = swap_cores(other)
    own = call(
        functools.partial(own_kernel, images),
        vmem_out((chips, rows, main), F32),
        (hidden_near[1], hidden_near[2], w_one, w_two),
        VMEM,
        (VMEM,) * 4,
        (),
        (4 * half * weight, 4 * weight),
    )
    total = call(
        add_kernel,
        vmem_out((chips, rows, main), BF16),
        (in_vmem(own), in_vmem(received)),
        VMEM,
        (VMEM,) * 2,
        (),
        (half * main, 8 * half * main),
    )
    shares = swap_chips(total)
    parts = 5
    g_in, g_out = call(
        functools.partial(weights_kernel, images),
        (
            jax.ShapeDtypeStruct((width, hidden_units), BF16),
            jax.ShapeDtypeStruct((hidden_units, width), BF16),
        ),
        (*hidden_near, *hidden_far),
        (HBM,) * 2,
        (VMEM,) * 6,
        [
            pltpu.VMEM((parts, width // parts, hidden_units), BF16),
            pltpu.VMEM((parts, hidden_units // parts, width), BF16),
            pltpu.SemaphoreType.DMA((parts,)),
            pltpu.SemaphoreType.DMA((parts,)),
        ],
        (8 * half * weight, 4 * weight),
    )
    terms, left, right = call(
        functools.partial(logits_kernel, split_chips),
        (
            vmem_out((devices, slots, width), BF16),
            vmem_out((images, 2 * slots, count), F32),
            vmem_out((images, 2 * slots, width), F32),
        ),
        (
            in_vmem(shares),
            in_vmem(tok),
            in_vmem(dout),
            in_vmem(disp),
            in_vmem(comb),
            router_t,
        ),
        (VMEM,) * 3,
        (VMEM,) * 6,
        [pltpu.VMEM((slots, rows, extra), F32)],
        (6 * slots * big, 4 * big),
    )
    terms = lax.all_to_all(terms, "expert", split_axis=0, concat_axis=0, tiled=True)
    pieces = 2
    grad_tokens = call(
        tokens_kernel,
        jax.ShapeDtypeStruct(tokens.shape, BF16),
        (in_vmem(left), in_vmem(right)),
        HBM,
        (VMEM,) * 2,
        [
            pltpu.VMEM((images, pieces, count // pieces, width), BF16),
            pltpu.SemaphoreType.DMA((images, pieces)),
        ],
        (4 * slots * big, 2 * big),
    )
    grad_router = call(
        sum_kernel,
        jax.ShapeDtypeStruct((slots, width), F32),
        (in_vmem(terms),),
        VMEM,
        (VMEM,),
        (),
        (devices * slots * width, 2 * devices * slots * width),
    )
    return (grad_tokens, g_in[None], g_out[None], grad_router.T)


def solution(mesh):
    in_specs = (
        P(("groups", "expert"), None, None),
        P(None, "groups"),
        P(("groups", "expert"), None, None),
        P(("groups", "expert"), None, None),
        P(("groups", "expert"), None, None),
    )
    out_specs = (
        P(("groups", "expert"), None, None),
        P(("groups", "expert"), None, None),
        P(("groups", "expert"), None, None),
        P(None, "groups"),
    )
    return jax.shard_map(
        per_device, mesh=mesh, in_specs=in_specs, out_specs=out_specs, check_vma=False
    )
```

```python
import functools

import jax
import jax.numpy as jnp
from jax import lax
from jax.experimental import pallas as pl
from jax.experimental.pallas import tpu as pltpu
from jax.sharding import PartitionSpec as P

F32 = jnp.float32
BF16 = jnp.bfloat16
NT = (((1,), (1,)), ((), ()))
TN = (((0,), (0,)), ((), ()))
NN = (((1,), (0,)), ((), ()))

VMEM = pl.BlockSpec(memory_space=pltpu.VMEM)
HBM = pl.BlockSpec(memory_space=pltpu.HBM)
MIB = 1024 * 1024


def dot(left, right, dims=NN):
    return lax.dot_general(left, right, dims, preferred_element_type=F32)


def in_vmem(array):
    return pltpu.with_memory_space_constraint(array, pltpu.VMEM)


def in_hbm(array):
    return pltpu.with_memory_space_constraint(array, pltpu.HBM)


def vmem_out(shape, dtype):
    return pltpu.VMEM(shape, dtype)


def call(kernel, outs, ins, out_specs, in_specs, scratch=(), cost=None, limit=40 * MIB):
    return pl.pallas_call(
        kernel,
        out_shape=outs,
        in_specs=in_specs,
        out_specs=out_specs,
        scratch_shapes=list(scratch),
        compiler_params=pltpu.CompilerParams(vmem_limit_bytes=limit),
        cost_estimate=pl.CostEstimate(flops=cost[0], bytes_accessed=cost[1], transcendentals=0),
    )(*ins)


def block_shape(images, width):
    extra = width // 5
    main = width - extra
    ends = -(-2 * images * extra // main)
    return -(-(2 * images + ends) // 8) * 8, main, extra


def end_place(images, main, extra, row):
    per = main // extra
    return 2 * images + row // per, row % per * extra


def pack(images, scratch, values):
    main = scratch.shape[2]
    extra = values.shape[2] - main
    scratch[...] = values[:, :, :main]
    for row in range(2 * images):
        to, column = end_place(images, main, extra, row)
        scratch[:, to, column : column + extra] = values[:, row, main:]


def unpack(images, scratch, values):
    main = values.shape[2]
    extra = scratch.shape[2]
    scratch[...] = jnp.zeros_like(scratch)
    for row in range(2 * images):
        at, column = end_place(images, main, extra, row)
        scratch[:, row, :] = values[:, at, column : column + extra]


def rows_kernel(
    tokens,
    router_hbm,
    d_out,
    rows_out,
    tok,
    dout,
    disp_out,
    comb_out,
    router_t,
    block,
    sems,
    other_sems,
):
    images = tok.shape[0]
    main = rows_out.shape[2]
    extra = tok.shape[2] - main
    fetch_router = pltpu.make_async_copy(router_hbm, router_t, other_sems.at[0])
    fetch_router.start()
    fetch_tok = [
        pltpu.make_async_copy(tokens.at[b], tok.at[b], sems.at[b]) for b in range(images)
    ]
    fetch_dout = [
        pltpu.make_async_copy(d_out.at[b], dout.at[b], sems.at[images + b]) for b in range(images)
    ]
    for copy in fetch_tok:
        copy.start()
    block[...] = jnp.zeros_like(block)

    def put(row, values):
        to, column = end_place(images, main, extra, row)
        block[:, row, :] = values[:, :main]
        block[:, to, column : column + extra] = values[:, main:]

    fetch_router.wait()
    for copy in fetch_dout:
        copy.start()
    logits = {}
    combs = {}
    disps = {}

    def softmaxes(b):
        exps = jnp.exp(logits[b] - jnp.max(logits[b], axis=1, keepdims=True))
        disp = exps * (1.0 / jnp.sum(exps, axis=1, keepdims=True))
        exps = jnp.exp(logits[b] - jnp.max(logits[b], axis=0, keepdims=True))
        comb = exps * (1.0 / jnp.sum(exps, axis=0, keepdims=True))
        disp_out[b] = disp
        comb_out[b] = comb
        disps[b] = disp.astype(BF16)
        combs[b] = comb.astype(BF16)

    for step in range(2 * images):
        if step < images:
            fetch_tok[step].wait()
            logits[step] = dot(router_t[...], tok[step], NT)
        else:
            fetch_dout[step - images].wait()
        if 0 <= step - 1 < images:
            softmaxes(step - 1)
        if step >= images:
            put(step, dot(combs[step - images], dout[step - images]))
        if 0 <= step - 2 < images:
            put(step - 2, dot(disps[step - 2], tok[step - 2]))
    for b in range(max(2 * images - 2, 0), images):
        put(b, dot(disps[b], tok[b]))
    rows_out[...] = block[...].astype(BF16)


def repeat_kernel(split_chips, rows, tok, dout, send):
    for slot in range(rows.shape[0]):
        for chip in range(split_chips):
            send[slot * split_chips + chip] = rows[slot]


def hidden_rows(images, blocks, w_in, w_out, x_out, hid_out, grad_out, ends):
    chips, rows, main = blocks.shape
    half = chips * rows
    width = x_out.shape[1]
    unpack(images, ends, blocks[...].astype(F32))
    x = jnp.concatenate(
        [
            blocks[...].reshape(half, main),
            ends[...].reshape(half, width - main).astype(BF16),
        ],
        axis=1,
    )
    x_out[...] = x
    pre = dot(x, w_in[...])
    grad_hidden = dot(x, w_out[...], NT)
    place = lax.broadcasted_iota(jnp.int32, pre.shape, 0) % rows
    slot_row = place < images
    grad_hidden = pltpu.roll(grad_hidden, half - images, 0)
    scale = 0.7978845608028654
    square = pre * pre
    tanh = jnp.tanh(scale * pre * (1.0 + 0.044715 * square))
    cdf = 0.5 * (1.0 + tanh)
    slope = cdf + (0.5 * scale) * pre * (1.0 - tanh * tanh) * (1.0 + (3 * 0.044715) * square)
    hidden = jnp.where(slot_row, pre * cdf, 0.0).astype(BF16)
    grad_pre = jnp.where(slot_row, slope * grad_hidden, 0.0)
    grad_low = pltpu.roll(grad_pre, images, 0).astype(BF16)
    hid_out[...] = hidden
    grad_out[...] = grad_low
    return hidden, grad_low


def near_kernel(images, blocks, w_in, w_out, x_out, hid_out, grad_out, ends):
    hidden_rows(images, blocks, w_in, w_out, x_out, hid_out, grad_out, ends)


def far_kernel(images, blocks, w_in, w_out, _, other, x_out, hid_out, grad_out, ends, packed):
    hidden, grad_low = hidden_rows(images, blocks, w_in, w_out, x_out, hid_out, grad_out, ends)
    shares = dot(hidden, w_out[...]) + dot(grad_low, w_in[...], NT)
    pack(images, packed, shares.reshape(blocks.shape[:2] + (shares.shape[1],)))
    other[...] = packed[...].astype(BF16)


def own_kernel(images, hid, grad, w_in, w_out, own):
    chips, rows, _ = own.shape
    shares = dot(hid[...], w_out[...]) + dot(grad[...], w_in[...], NT)
    pack(images, own, shares.reshape(chips, rows, shares.shape[1]))


def add_kernel(own, received, total):
    total[...] = (own[...] + received[...].astype(F32)).astype(BF16)


def weights_kernel(
    images,
    x_near,
    hid_near,
    grad_near,
    x_far,
    hid_far,
    grad_far,
    g_in,
    g_out,
    buf_in,
    buf_out,
    sem_in,
    sem_out,
):
    parts = buf_in.shape[0]
    step_in = g_in.shape[0] // parts
    step_out = g_out.shape[0] // parts
    x = jnp.concatenate([x_near[...], x_far[...]], axis=0)
    hid = jnp.concatenate([hid_near[...], hid_far[...]], axis=0)
    grad = jnp.concatenate([grad_near[...], grad_far[...]], axis=0)
    hid_low = pltpu.roll(hid.astype(F32), images, 0).astype(BF16)
    grad_high = pltpu.roll(grad.astype(F32), x.shape[0] - images, 0).astype(BF16)
    copies = []
    for i in range(parts):
        buf_out[i] = dot(hid_low[:, i * step_out : (i + 1) * step_out], x, TN).astype(BF16)
        copy = pltpu.make_async_copy(
            buf_out.at[i], g_out.at[pl.ds(i * step_out, step_out)], sem_out.at[i]
        )
        copy.start()
        copies.append(copy)
        buf_in[i] = dot(x[:, i * step_in : (i + 1) * step_in], grad_high, TN).astype(BF16)
        copy = pltpu.make_async_copy(
            buf_in.at[i], g_in.at[pl.ds(i * step_in, step_in)], sem_in.at[i]
        )
        copy.start()
        copies.append(copy)
    for copy in copies:
        copy.wait()


def logits_kernel(
    split_chips, shares, tok, dout, disp, comb, router_t, terms_out, left, right, ends
):
    images, slots, count = disp.shape
    chips, rows, main = shares.shape
    width = tok.shape[2]
    summed = []
    for slot in range(slots):
        total = shares[slot * split_chips].astype(F32)
        for chip in range(1, split_chips):
            total = total + shares[slot * split_chips + chip].astype(F32)
        summed.append(total)
    unpack(images, ends, jnp.stack(summed))
    stacked = jnp.concatenate(
        [
            jnp.concatenate(summed, axis=0),
            ends[...].reshape(slots * rows, width - main),
        ],
        axis=1,
    )
    stacked_b = stacked.astype(BF16)
    by_dout = {}
    by_tok = {}
    grads = {}

    def products(b):
        by_dout[b] = dot(stacked_b, dout[b], NT)
        by_tok[b] = dot(stacked_b, tok[b], NT)

    def logits_grad(b):
        grad_comb = jnp.concatenate(
            [by_dout[b][s * rows + b : s * rows + b + 1] for s in range(slots)], axis=0
        )
        at = images + b
        grad_disp = jnp.concatenate(
            [by_tok[b][s * rows + at : s * rows + at + 1] for s in range(slots)], axis=0
        )
        dispatch = disp[b]
        combine = comb[b]
        grads[b] = dispatch * (
            grad_disp - jnp.sum(dispatch * grad_disp, axis=1, keepdims=True)
        ) + combine * (grad_comb - jnp.sum(combine * grad_comb, axis=0, keepdims=True))

    terms = jnp.zeros((slots, width), F32)
    for step in range(images + 2):
        if step < images:
            products(step)
        if 0 <= step - 1 < images:
            logits_grad(step - 1)
        if 0 <= step - 2 < images:
            terms = terms + dot(grads[step - 2].astype(BF16), tok[step - 2])
    terms = terms.astype(BF16)
    terms_out[...] = jnp.broadcast_to(terms[None], terms_out.shape)
    for b in range(images):
        left[b] = jnp.concatenate([disp[b], grads[b]], axis=0)
        right[b] = jnp.concatenate(
            [stacked[s * rows + images + b : s * rows + images + b + 1] for s in range(slots)]
            + [router_t[...].astype(F32)],
            axis=0,
        )


def tokens_kernel(left, right, grad_tokens, buf, sems):
    images, parts = buf.shape[:2]
    step = buf.shape[2]
    copies = []
    for b in range(images):
        rhs = right[b].astype(BF16)
        for i in range(parts):
            lhs = left[b, :, i * step : (i + 1) * step].astype(BF16)
            buf[b, i] = dot(lhs, rhs, TN).astype(BF16)
            copy = pltpu.make_async_copy(
                buf.at[b, i], grad_tokens.at[b, pl.ds(i * step, step)], sems.at[b, i]
            )
            copy.start()
            copies.append(copy)
    for copy in copies:
        copy.wait()


def sum_kernel(terms, total):
    total[...] = jnp.sum(terms[...].astype(F32), axis=0)


def swap_chips(blocks):
    count = lax.axis_size("expert")
    groups = [list(range(core, count, 2)) for core in range(2)]
    return lax.all_to_all(
        blocks, "expert", split_axis=0, concat_axis=0, axis_index_groups=groups, tiled=True
    )


def swap_cores(block):
    count = lax.axis_size("expert")
    return lax.ppermute(block, "expert", [(device, device ^ 1) for device in range(count)])


def per_device(tokens, router, w_in, w_out, d_out):
    devices = lax.axis_size("expert")
    chips = devices // 2
    slots = router.shape[1]
    split_chips = chips // slots
    images, count, width = tokens.shape
    hidden_units = w_in.shape[2]
    rows, main, extra = block_shape(images, width)
    half = chips * rows
    router_t = router.T
    big = images * count * width
    weight = width * hidden_units

    blocks, tok, dout, disp, comb = call(
        rows_kernel,
        (
            vmem_out((slots, rows, main), BF16),
            vmem_out((images, count, width), BF16),
            vmem_out((images, count, width), BF16),
            vmem_out((images, slots, count), F32),
            vmem_out((images, slots, count), F32),
        ),
        tuple(in_hbm(array) for array in (tokens, router_t, d_out)),
        (VMEM,) * 5,
        (HBM,) * 3,
        [
            pltpu.VMEM((slots, width), BF16),
            pltpu.VMEM((slots, rows, main), F32),
            pltpu.SemaphoreType.DMA((2 * images,)),
            pltpu.SemaphoreType.DMA((2,)),
        ],
        (6 * slots * big, 4 * big),
        limit=56 * MIB,
    )
    send = call(
        functools.partial(repeat_kernel, split_chips),
        vmem_out((chips, rows, main), BF16),
        (in_vmem(blocks), in_vmem(tok), in_vmem(dout)),
        VMEM,
        (VMEM,) * 3,
        (),
        (4 * half * weight, 40 * weight),
    )
    near = swap_chips(send)
    far = swap_cores(near)
    w_one, w_two = in_vmem(w_in[0]), in_vmem(w_out[0])
    inner = (
        vmem_out((half, width), BF16),
        vmem_out((half, hidden_units), BF16),
        vmem_out((half, hidden_units), BF16),
    )
    hidden_near = call(
        functools.partial(near_kernel, images),
        inner,
        (in_vmem(near), w_one, w_two),
        (VMEM,) * 3,
        (VMEM,) * 3,
        [pltpu.VMEM((chips, rows, extra), F32)],
        (4 * half * weight, 4 * weight),
    )
    hidden_near = [in_vmem(array) for array in hidden_near]
    other, *hidden_far = call(
        functools.partial(far_kernel, images),
        (vmem_out((chips, rows, main), BF16),) + inner,
        (in_vmem(far), w_one, w_two, hidden_near[1]),
        (VMEM,) * 4,
        (VMEM,) * 4,
        [
            pltpu.VMEM((chips, rows, extra), F32),
            pltpu.VMEM((chips, rows, main), F32),
        ],
        (8 * half * weight, 4 * weight),
    )
    hidden_far = [in_vmem(array) for array in hidden_far]
    received = swap_cores(other)
    own = call(
        functools.partial(own_kernel, images),
        vmem_out((chips, rows, main), F32),
        (hidden_near[1], hidden_near[2], w_one, w_two),
        VMEM,
        (VMEM,) * 4,
        (),
        (4 * half * weight, 4 * weight),
    )
    total = call(
        add_kernel,
        vmem_out((chips, rows, main), BF16),
        (in_vmem(own), in_vmem(received)),
        VMEM,
        (VMEM,) * 2,
        (),
        (half * main, 8 * half * main),
    )
    shares = swap_chips(total)
    parts = 5
    g_in, g_out = call(
        functools.partial(weights_kernel, images),
        (
            jax.ShapeDtypeStruct((width, hidden_units), BF16),
            jax.ShapeDtypeStruct((hidden_units, width), BF16),
        ),
        (*hidden_near, *hidden_far),
        (HBM,) * 2,
        (VMEM,) * 6,
        [
            pltpu.VMEM((parts, width // parts, hidden_units), BF16),
            pltpu.VMEM((parts, hidden_units // parts, width), BF16),
            pltpu.SemaphoreType.DMA((parts,)),
            pltpu.SemaphoreType.DMA((parts,)),
        ],
        (8 * half * weight, 4 * weight),
    )
    terms, left, right = call(
        functools.partial(logits_kernel, split_chips),
        (
            vmem_out((devices, slots, width), BF16),
            vmem_out((images, 2 * slots, count), F32),
            vmem_out((images, 2 * slots, width), F32),
        ),
        (
            in_vmem(shares),
            in_vmem(tok),
            in_vmem(dout),
            in_vmem(disp),
            in_vmem(comb),
            router_t,
        ),
        (VMEM,) * 3,
        (VMEM,) * 6,
        [pltpu.VMEM((slots, rows, extra), F32)],
        (6 * slots * big, 4 * big),
    )
    terms = lax.all_to_all(terms, "expert", split_axis=0, concat_axis=0, tiled=True)
    pieces = 2
    grad_tokens = call(
        tokens_kernel,
        jax.ShapeDtypeStruct(tokens.shape, BF16),
        (in_vmem(left), in_vmem(right)),
        HBM,
        (VMEM,) * 2,
        [
            pltpu.VMEM((images, pieces, count // pieces, width), BF16),
            pltpu.SemaphoreType.DMA((images, pieces)),
        ],
        (4 * slots * big, 2 * big),
    )
    grad_router = call(
        sum_kernel,
        jax.ShapeDtypeStruct((slots, width), F32),
        (in_vmem(terms),),
        VMEM,
        (VMEM,),
        (),
        (devices * slots * width, 2 * devices * slots * width),
    )
    return (grad_tokens, g_in[None], g_out[None], grad_router.T)


def solution(mesh):
    in_specs = (
        P(("groups", "expert"), None, None),
        P(None, "groups"),
        P(("groups", "expert"), None, None),
        P(("groups", "expert"), None, None),
        P(("groups", "expert"), None, None),
    )
    out_specs = (
        P(("groups", "expert"), None, None),
        P(("groups", "expert"), None, None),
        P(("groups", "expert"), None, None),
        P(None, "groups"),
    )
    return jax.shard_map(
        per_device, mesh=mesh, in_specs=in_specs, out_specs=out_specs, check_vma=False
    )
```

```python
import functools

import jax
import jax.numpy as jnp
from jax import lax
from jax.experimental import pallas as pl
from jax.experimental.pallas import tpu as pltpu
from jax.sharding import PartitionSpec as P

F32 = jnp.float32
BF16 = jnp.bfloat16
NT = (((1,), (1,)), ((), ()))
TN = (((0,), (0,)), ((), ()))
NN = (((1,), (0,)), ((), ()))

VMEM = pl.BlockSpec(memory_space=pltpu.VMEM)
HBM = pl.BlockSpec(memory_space=pltpu.HBM)
MIB = 1024 * 1024


def dot(left, right, dims=NN):
    return lax.dot_general(left, right, dims, preferred_element_type=F32)


def in_vmem(array):
    return pltpu.with_memory_space_constraint(array, pltpu.VMEM)


def in_hbm(array):
    return pltpu.with_memory_space_constraint(array, pltpu.HBM)


def vmem_out(shape, dtype):
    return pltpu.VMEM(shape, dtype)


def call(kernel, outs, ins, out_specs, in_specs, scratch=(), cost=None, limit=40 * MIB):
    return pl.pallas_call(
        kernel,
        out_shape=outs,
        in_specs=in_specs,
        out_specs=out_specs,
        scratch_shapes=list(scratch),
        compiler_params=pltpu.CompilerParams(vmem_limit_bytes=limit),
        cost_estimate=pl.CostEstimate(flops=cost[0], bytes_accessed=cost[1], transcendentals=0),
    )(*ins)


def block_shape(images, width):
    extra = width // 5
    main = width - extra
    ends = -(-2 * images * extra // main)
    return -(-(2 * images + ends) // 8) * 8, main, extra


def end_place(images, main, extra, row):
    per = main // extra
    return 2 * images + row // per, row % per * extra


def pack(images, scratch, values):
    main = scratch.shape[2]
    extra = values.shape[2] - main
    scratch[...] = values[:, :, :main]
    for row in range(2 * images):
        to, column = end_place(images, main, extra, row)
        scratch[:, to, column : column + extra] = values[:, row, main:]


def unpack(images, scratch, values):
    main = values.shape[2]
    extra = scratch.shape[2]
    scratch[...] = jnp.zeros_like(scratch)
    for row in range(2 * images):
        at, column = end_place(images, main, extra, row)
        scratch[:, row, :] = values[:, at, column : column + extra]


def rows_kernel(
    tokens,
    router_hbm,
    d_out,
    w_in,
    rows_out,
    tok,
    dout,
    disp_out,
    comb_out,
    w_one,
    router_t,
    block,
    sems,
    other_sems,
):
    images = tok.shape[0]
    main = rows_out.shape[2]
    extra = tok.shape[2] - main
    fetch_router = pltpu.make_async_copy(router_hbm, router_t, other_sems.at[0])
    fetch_router.start()
    fetch_tok = [
        pltpu.make_async_copy(tokens.at[b], tok.at[b], sems.at[b]) for b in range(images)
    ]
    fetch_dout = [
        pltpu.make_async_copy(d_out.at[b], dout.at[b], sems.at[images + b]) for b in range(images)
    ]
    fetch_weight = pltpu.make_async_copy(w_in, w_one, other_sems.at[1])
    for copy in fetch_tok:
        copy.start()
    block[...] = jnp.zeros_like(block)

    def put(row, values):
        to, column = end_place(images, main, extra, row)
        block[:, row, :] = values[:, :main]
        block[:, to, column : column + extra] = values[:, main:]

    fetch_router.wait()
    for copy in fetch_dout:
        copy.start()
    logits = {}
    combs = {}
    disps = {}

    def softmaxes(b):
        exps = jnp.exp(logits[b] - jnp.max(logits[b], axis=1, keepdims=True))
        disp = exps * (1.0 / jnp.sum(exps, axis=1, keepdims=True))
        exps = jnp.exp(logits[b] - jnp.max(logits[b], axis=0, keepdims=True))
        comb = exps * (1.0 / jnp.sum(exps, axis=0, keepdims=True))
        disp_out[b] = disp
        comb_out[b] = comb
        disps[b] = disp.astype(BF16)
        combs[b] = comb.astype(BF16)

    for step in range(2 * images):
        if step < images:
            fetch_tok[step].wait()
            if step == 0:
                fetch_weight.start()
            logits[step] = dot(router_t[...], tok[step], NT)
        else:
            fetch_dout[step - images].wait()
        if 0 <= step - 1 < images:
            softmaxes(step - 1)
        if step >= images:
            put(step, dot(combs[step - images], dout[step - images]))
        if 0 <= step - 2 < images:
            put(step - 2, dot(disps[step - 2], tok[step - 2]))
    for b in range(max(2 * images - 2, 0), images):
        put(b, dot(disps[b], tok[b]))
    rows_out[...] = block[...].astype(BF16)
    fetch_weight.wait()


def repeat_kernel(split_chips, rows, tok, dout, send):
    for slot in range(rows.shape[0]):
        for chip in range(split_chips):
            send[slot * split_chips + chip] = rows[slot]


def hidden_rows(images, blocks, w_in, w_out, x_out, hid_out, grad_out, ends):
    chips, rows, main = blocks.shape
    half = chips * rows
    width = x_out.shape[1]
    unpack(images, ends, blocks[...].astype(F32))
    x = jnp.concatenate(
        [
            blocks[...].reshape(half, main),
            ends[...].reshape(half, width - main).astype(BF16),
        ],
        axis=1,
    )
    x_out[...] = x
    pre = dot(x, w_in[...])
    grad_hidden = dot(x, w_out[...], NT)
    place = lax.broadcasted_iota(jnp.int32, pre.shape, 0) % rows
    slot_row = place < images
    grad_hidden = pltpu.roll(grad_hidden, half - images, 0)
    scale = 0.7978845608028654
    square = pre * pre
    tanh = jnp.tanh(scale * pre * (1.0 + 0.044715 * square))
    cdf = 0.5 * (1.0 + tanh)
    slope = cdf + (0.5 * scale) * pre * (1.0 - tanh * tanh) * (1.0 + (3 * 0.044715) * square)
    hidden = jnp.where(slot_row, pre * cdf, 0.0).astype(BF16)
    grad_pre = jnp.where(slot_row, slope * grad_hidden, 0.0)
    grad_low = pltpu.roll(grad_pre, images, 0).astype(BF16)
    hid_out[...] = hidden
    grad_out[...] = grad_low
    return hidden, grad_low


def near_kernel(images, blocks, w_in, w_out, x_out, hid_out, grad_out, ends):
    hidden_rows(images, blocks, w_in, w_out, x_out, hid_out, grad_out, ends)


def far_kernel(images, blocks, w_in, w_out, _, other, x_out, hid_out, grad_out, ends, packed):
    hidden, grad_low = hidden_rows(images, blocks, w_in, w_out, x_out, hid_out, grad_out, ends)
    shares = dot(hidden, w_out[...]) + dot(grad_low, w_in[...], NT)
    pack(images, packed, shares.reshape(blocks.shape[:2] + (shares.shape[1],)))
    other[...] = packed[...].astype(BF16)


def own_kernel(images, hid, grad, w_in, w_out, own):
    chips, rows, _ = own.shape
    shares = dot(hid[...], w_out[...]) + dot(grad[...], w_in[...], NT)
    pack(images, own, shares.reshape(chips, rows, shares.shape[1]))


def add_kernel(own, received, total):
    total[...] = (own[...] + received[...].astype(F32)).astype(BF16)


def weights_kernel(
    images,
    x_near,
    hid_near,
    grad_near,
    x_far,
    hid_far,
    grad_far,
    g_in,
    g_out,
    buf_in,
    buf_out,
    sem_in,
    sem_out,
):
    parts = buf_in.shape[0]
    step_in = g_in.shape[0] // parts
    step_out = g_out.shape[0] // parts
    x = jnp.concatenate([x_near[...], x_far[...]], axis=0)
    hid = jnp.concatenate([hid_near[...], hid_far[...]], axis=0)
    grad = jnp.concatenate([grad_near[...], grad_far[...]], axis=0)
    hid_low = pltpu.roll(hid.astype(F32), images, 0).astype(BF16)
    grad_high = pltpu.roll(grad.astype(F32), x.shape[0] - images, 0).astype(BF16)
    copies = []
    for i in range(parts):
        buf_out[i] = dot(hid_low[:, i * step_out : (i + 1) * step_out], x, TN).astype(BF16)
        copy = pltpu.make_async_copy(
            buf_out.at[i], g_out.at[pl.ds(i * step_out, step_out)], sem_out.at[i]
        )
        copy.start()
        copies.append(copy)
        buf_in[i] = dot(x[:, i * step_in : (i + 1) * step_in], grad_high, TN).astype(BF16)
        copy = pltpu.make_async_copy(
            buf_in.at[i], g_in.at[pl.ds(i * step_in, step_in)], sem_in.at[i]
        )
        copy.start()
        copies.append(copy)
    for copy in copies:
        copy.wait()


def logits_kernel(
    split_chips, shares, tok, dout, disp, comb, router_t, terms_out, left, right, ends
):
    images, slots, count = disp.shape
    chips, rows, main = shares.shape
    width = tok.shape[2]
    summed = []
    for slot in range(slots):
        total = shares[slot * split_chips].astype(F32)
        for chip in range(1, split_chips):
            total = total + shares[slot * split_chips + chip].astype(F32)
        summed.append(total)
    unpack(images, ends, jnp.stack(summed))
    stacked = jnp.concatenate(
        [
            jnp.concatenate(summed, axis=0),
            ends[...].reshape(slots * rows, width - main),
        ],
        axis=1,
    )
    stacked_b = stacked.astype(BF16)
    by_dout = {}
    by_tok = {}
    grads = {}

    def products(b):
        by_dout[b] = dot(stacked_b, dout[b], NT)
        by_tok[b] = dot(stacked_b, tok[b], NT)

    def logits_grad(b):
        grad_comb = jnp.concatenate(
            [by_dout[b][s * rows + b : s * rows + b + 1] for s in range(slots)], axis=0
        )
        at = images + b
        grad_disp = jnp.concatenate(
            [by_tok[b][s * rows + at : s * rows + at + 1] for s in range(slots)], axis=0
        )
        dispatch = disp[b]
        combine = comb[b]
        grads[b] = dispatch * (
            grad_disp - jnp.sum(dispatch * grad_disp, axis=1, keepdims=True)
        ) + combine * (grad_comb - jnp.sum(combine * grad_comb, axis=0, keepdims=True))

    terms = jnp.zeros((slots, width), F32)
    for step in range(images + 2):
        if step < images:
            products(step)
        if 0 <= step - 1 < images:
            logits_grad(step - 1)
        if 0 <= step - 2 < images:
            terms = terms + dot(grads[step - 2].astype(BF16), tok[step - 2])
    terms = terms.astype(BF16)
    terms_out[...] = jnp.broadcast_to(terms[None], terms_out.shape)
    for b in range(images):
        left[b] = jnp.concatenate([disp[b], grads[b]], axis=0)
        right[b] = jnp.concatenate(
            [stacked[s * rows + images + b : s * rows + images + b + 1] for s in range(slots)]
            + [router_t[...].astype(F32)],
            axis=0,
        )


def tokens_kernel(left, right, grad_tokens, buf, sems):
    images, parts = buf.shape[:2]
    step = buf.shape[2]
    copies = []
    for b in range(images):
        rhs = right[b].astype(BF16)
        for i in range(parts):
            lhs = left[b, :, i * step : (i + 1) * step].astype(BF16)
            buf[b, i] = dot(lhs, rhs, TN).astype(BF16)
            copy = pltpu.make_async_copy(
                buf.at[b, i], grad_tokens.at[b, pl.ds(i * step, step)], sems.at[b, i]
            )
            copy.start()
            copies.append(copy)
    for copy in copies:
        copy.wait()


def sum_kernel(terms, total):
    total[...] = jnp.sum(terms[...].astype(F32), axis=0)


def swap_chips(blocks):
    count = lax.axis_size("expert")
    groups = [list(range(core, count, 2)) for core in range(2)]
    return lax.all_to_all(
        blocks, "expert", split_axis=0, concat_axis=0, axis_index_groups=groups, tiled=True
    )


def swap_cores(block):
    count = lax.axis_size("expert")
    return lax.ppermute(block, "expert", [(device, device ^ 1) for device in range(count)])


def per_device(tokens, router, w_in, w_out, d_out):
    devices = lax.axis_size("expert")
    chips = devices // 2
    slots = router.shape[1]
    split_chips = chips // slots
    images, count, width = tokens.shape
    hidden_units = w_in.shape[2]
    rows, main, extra = block_shape(images, width)
    half = chips * rows
    router_t = router.T
    big = images * count * width
    weight = width * hidden_units

    blocks, tok, dout, disp, comb, w_one = call(
        rows_kernel,
        (
            vmem_out((slots, rows, main), BF16),
            vmem_out((images, count, width), BF16),
            vmem_out((images, count, width), BF16),
            vmem_out((images, slots, count), F32),
            vmem_out((images, slots, count), F32),
            vmem_out(w_in.shape[1:], BF16),
        ),
        tuple(in_hbm(array) for array in (tokens, router_t, d_out, w_in[0])),
        (VMEM,) * 6,
        (HBM,) * 4,
        [
            pltpu.VMEM((slots, width), BF16),
            pltpu.VMEM((slots, rows, main), F32),
            pltpu.SemaphoreType.DMA((2 * images,)),
            pltpu.SemaphoreType.DMA((2,)),
        ],
        (6 * slots * big, 4 * big),
        limit=58 * MIB,
    )
    send = call(
        functools.partial(repeat_kernel, split_chips),
        vmem_out((chips, rows, main), BF16),
        (in_vmem(blocks), in_vmem(tok), in_vmem(dout)),
        VMEM,
        (VMEM,) * 3,
        (),
        (4 * half * weight, 40 * weight),
    )
    near = swap_chips(send)
    far = swap_cores(near)
    w_one, w_two = in_vmem(w_one), in_vmem(w_out[0])
    inner = (
        vmem_out((half, width), BF16),
        vmem_out((half, hidden_units), BF16),
        vmem_out((half, hidden_units), BF16),
    )
    hidden_near = call(
        functools.partial(near_kernel, images),
        inner,
        (in_vmem(near), w_one, w_two),
        (VMEM,) * 3,
        (VMEM,) * 3,
        [pltpu.VMEM((chips, rows, extra), F32)],
        (4 * half * weight, 4 * weight),
    )
    hidden_near = [in_vmem(array) for array in hidden_near]
    other, *hidden_far = call(
        functools.partial(far_kernel, images),
        (vmem_out((chips, rows, main), BF16),) + inner,
        (in_vmem(far), w_one, w_two, hidden_near[1]),
        (VMEM,) * 4,
        (VMEM,) * 4,
        [
            pltpu.VMEM((chips, rows, extra), F32),
            pltpu.VMEM((chips, rows, main), F32),
        ],
        (8 * half * weight, 4 * weight),
    )
    hidden_far = [in_vmem(array) for array in hidden_far]
    received = swap_cores(other)
    own = call(
        functools.partial(own_kernel, images),
        vmem_out((chips, rows, main), F32),
        (hidden_near[1], hidden_near[2], w_one, w_two),
        VMEM,
        (VMEM,) * 4,
        (),
        (4 * half * weight, 4 * weight),
    )
    total = call(
        add_kernel,
        vmem_out((chips, rows, main), BF16),
        (in_vmem(own), in_vmem(received)),
        VMEM,
        (VMEM,) * 2,
        (),
        (half * main, 8 * half * main),
    )
    shares = swap_chips(total)
    parts = 5
    g_in, g_out = call(
        functools.partial(weights_kernel, images),
        (
            jax.ShapeDtypeStruct((width, hidden_units), BF16),
            jax.ShapeDtypeStruct((hidden_units, width), BF16),
        ),
        (*hidden_near, *hidden_far),
        (HBM,) * 2,
        (VMEM,) * 6,
        [
            pltpu.VMEM((parts, width // parts, hidden_units), BF16),
            pltpu.VMEM((parts, hidden_units // parts, width), BF16),
            pltpu.SemaphoreType.DMA((parts,)),
            pltpu.SemaphoreType.DMA((parts,)),
        ],
        (8 * half * weight, 4 * weight),
    )
    terms, left, right = call(
        functools.partial(logits_kernel, split_chips),
        (
            vmem_out((devices, slots, width), BF16),
            vmem_out((images, 2 * slots, count), F32),
            vmem_out((images, 2 * slots, width), F32),
        ),
        (
            in_vmem(shares),
            in_vmem(tok),
            in_vmem(dout),
            in_vmem(disp),
            in_vmem(comb),
            router_t,
        ),
        (VMEM,) * 3,
        (VMEM,) * 6,
        [pltpu.VMEM((slots, rows, extra), F32)],
        (6 * slots * big, 4 * big),
    )
    terms = lax.all_to_all(terms, "expert", split_axis=0, concat_axis=0, tiled=True)
    pieces = 2
    grad_tokens = call(
        tokens_kernel,
        jax.ShapeDtypeStruct(tokens.shape, BF16),
        (in_vmem(left), in_vmem(right)),
        HBM,
        (VMEM,) * 2,
        [
            pltpu.VMEM((images, pieces, count // pieces, width), BF16),
            pltpu.SemaphoreType.DMA((images, pieces)),
        ],
        (4 * slots * big, 2 * big),
    )
    grad_router = call(
        sum_kernel,
        jax.ShapeDtypeStruct((slots, width), F32),
        (in_vmem(terms),),
        VMEM,
        (VMEM,),
        (),
        (devices * slots * width, 2 * devices * slots * width),
    )
    return (grad_tokens, g_in[None], g_out[None], grad_router.T)


def solution(mesh):
    in_specs = (
        P(("groups", "expert"), None, None),
        P(None, "groups"),
        P(("groups", "expert"), None, None),
        P(("groups", "expert"), None, None),
        P(("groups", "expert"), None, None),
    )
    out_specs = (
        P(("groups", "expert"), None, None),
        P(("groups", "expert"), None, None),
        P(("groups", "expert"), None, None),
        P(None, "groups"),
    )
    return jax.shard_map(
        per_device, mesh=mesh, in_specs=in_specs, out_specs=out_specs, check_vma=False
    )
```

```python
import functools

import jax
import jax.numpy as jnp
from jax import lax
from jax.experimental import pallas as pl
from jax.experimental.pallas import tpu as pltpu
from jax.sharding import PartitionSpec as P

F32 = jnp.float32
BF16 = jnp.bfloat16
NT = (((1,), (1,)), ((), ()))
TN = (((0,), (0,)), ((), ()))
NN = (((1,), (0,)), ((), ()))

VMEM = pl.BlockSpec(memory_space=pltpu.VMEM)
HBM = pl.BlockSpec(memory_space=pltpu.HBM)
MIB = 1024 * 1024


def dot(left, right, dims=NN):
    return lax.dot_general(left, right, dims, preferred_element_type=F32)


def in_vmem(array):
    return pltpu.with_memory_space_constraint(array, pltpu.VMEM)


def in_hbm(array):
    return pltpu.with_memory_space_constraint(array, pltpu.HBM)


def vmem_out(shape, dtype):
    return pltpu.VMEM(shape, dtype)


def call(kernel, outs, ins, out_specs, in_specs, scratch=(), cost=None, limit=40 * MIB):
    return pl.pallas_call(
        kernel,
        out_shape=outs,
        in_specs=in_specs,
        out_specs=out_specs,
        scratch_shapes=list(scratch),
        compiler_params=pltpu.CompilerParams(vmem_limit_bytes=limit),
        cost_estimate=pl.CostEstimate(flops=cost[0], bytes_accessed=cost[1], transcendentals=0),
    )(*ins)


def block_shape(images, width):
    extra = width // 5
    main = width - extra
    ends = -(-2 * images * extra // main)
    return -(-(2 * images + ends) // 8) * 8, main, extra


def end_place(images, main, extra, row):
    per = main // extra
    return 2 * images + row // per, row % per * extra


def pack(images, scratch, values):
    main = scratch.shape[2]
    extra = values.shape[2] - main
    scratch[...] = values[:, :, :main]
    for row in range(2 * images):
        to, column = end_place(images, main, extra, row)
        scratch[:, to, column : column + extra] = values[:, row, main:]


def unpack(images, scratch, values):
    main = values.shape[2]
    extra = scratch.shape[2]
    scratch[...] = jnp.zeros_like(scratch)
    for row in range(2 * images):
        at, column = end_place(images, main, extra, row)
        scratch[:, row, :] = values[:, at, column : column + extra]


def rows_kernel(
    tokens,
    router_hbm,
    d_out,
    rows_out,
    tok,
    dout,
    disp_out,
    comb_out,
    router_t,
    block,
    sems,
    other_sems,
):
    images = tok.shape[0]
    main = rows_out.shape[2]
    extra = tok.shape[2] - main
    fetch_router = pltpu.make_async_copy(router_hbm, router_t, other_sems.at[0])
    fetch_router.start()
    fetch_tok = [
        pltpu.make_async_copy(tokens.at[b], tok.at[b], sems.at[b]) for b in range(images)
    ]
    fetch_dout = [
        pltpu.make_async_copy(d_out.at[b], dout.at[b], sems.at[images + b]) for b in range(images)
    ]
    for copy in fetch_tok:
        copy.start()
    block[...] = jnp.zeros_like(block)

    def put(row, values):
        to, column = end_place(images, main, extra, row)
        block[:, row, :] = values[:, :main]
        block[:, to, column : column + extra] = values[:, main:]

    fetch_router.wait()
    for copy in fetch_dout:
        copy.start()
    logits = {}
    combs = {}
    disps = {}

    def softmaxes(b):
        exps = jnp.exp(logits[b] - jnp.max(logits[b], axis=1, keepdims=True))
        disp = exps * (1.0 / jnp.sum(exps, axis=1, keepdims=True))
        exps = jnp.exp(logits[b] - jnp.max(logits[b], axis=0, keepdims=True))
        comb = exps * (1.0 / jnp.sum(exps, axis=0, keepdims=True))
        disp_out[b] = disp
        comb_out[b] = comb
        disps[b] = disp.astype(BF16)
        combs[b] = comb.astype(BF16)

    for step in range(2 * images):
        if step < images:
            fetch_tok[step].wait()
            logits[step] = dot(tok[step], router_t[...], NT).T
        else:
            fetch_dout[step - images].wait()
        if 0 <= step - 1 < images:
            softmaxes(step - 1)
        if step >= images:
            put(step, dot(combs[step - images], dout[step - images]))
        if 0 <= step - 2 < images:
            put(step - 2, dot(disps[step - 2], tok[step - 2]))
    for b in range(max(2 * images - 2, 0), images):
        put(b, dot(disps[b], tok[b]))
    rows_out[...] = block[...].astype(BF16)


def repeat_kernel(split_chips, rows, tok, dout, send):
    for slot in range(rows.shape[0]):
        for chip in range(split_chips):
            send[slot * split_chips + chip] = rows[slot]


def hidden_rows(images, blocks, w_in, w_out, x_out, hid_out, grad_out, ends):
    chips, rows, main = blocks.shape
    half = chips * rows
    width = x_out.shape[1]
    unpack(images, ends, blocks[...].astype(F32))
    x = jnp.concatenate(
        [
            blocks[...].reshape(half, main),
            ends[...].reshape(half, width - main).astype(BF16),
        ],
        axis=1,
    )
    x_out[...] = x
    pre = dot(x, w_in[...])
    grad_hidden = dot(x, w_out[...], NT)
    place = lax.broadcasted_iota(jnp.int32, pre.shape, 0) % rows
    slot_row = place < images
    grad_hidden = pltpu.roll(grad_hidden, half - images, 0)
    scale = 0.7978845608028654
    square = pre * pre
    tanh = jnp.tanh(scale * pre * (1.0 + 0.044715 * square))
    cdf = 0.5 * (1.0 + tanh)
    slope = cdf + (0.5 * scale) * pre * (1.0 - tanh * tanh) * (1.0 + (3 * 0.044715) * square)
    hidden = jnp.where(slot_row, pre * cdf, 0.0).astype(BF16)
    grad_pre = jnp.where(slot_row, slope * grad_hidden, 0.0)
    grad_low = pltpu.roll(grad_pre, images, 0).astype(BF16)
    hid_out[...] = hidden
    grad_out[...] = grad_low
    return hidden, grad_low


def near_kernel(images, blocks, w_in, w_out, x_out, hid_out, grad_out, ends):
    hidden_rows(images, blocks, w_in, w_out, x_out, hid_out, grad_out, ends)


def far_kernel(images, blocks, w_in, w_out, _, other, x_out, hid_out, grad_out, ends, packed):
    hidden, grad_low = hidden_rows(images, blocks, w_in, w_out, x_out, hid_out, grad_out, ends)
    shares = dot(hidden, w_out[...]) + dot(grad_low, w_in[...], NT)
    pack(images, packed, shares.reshape(blocks.shape[:2] + (shares.shape[1],)))
    other[...] = packed[...].astype(BF16)


def own_kernel(images, hid, grad, w_in, w_out, own):
    chips, rows, _ = own.shape
    shares = dot(hid[...], w_out[...]) + dot(grad[...], w_in[...], NT)
    pack(images, own, shares.reshape(chips, rows, shares.shape[1]))


def add_kernel(own, received, total):
    total[...] = (own[...] + received[...].astype(F32)).astype(BF16)


def weights_kernel(
    images,
    x_near,
    hid_near,
    grad_near,
    x_far,
    hid_far,
    grad_far,
    g_in,
    g_out,
    buf_in,
    buf_out,
    sem_in,
    sem_out,
):
    parts = buf_in.shape[0]
    step_in = g_in.shape[0] // parts
    step_out = g_out.shape[0] // parts
    x = jnp.concatenate([x_near[...], x_far[...]], axis=0)
    hid = jnp.concatenate([hid_near[...], hid_far[...]], axis=0)
    grad = jnp.concatenate([grad_near[...], grad_far[...]], axis=0)
    hid_low = pltpu.roll(hid.astype(F32), images, 0).astype(BF16)
    grad_high = pltpu.roll(grad.astype(F32), x.shape[0] - images, 0).astype(BF16)
    copies = []
    for i in range(parts):
        buf_out[i] = dot(hid_low[:, i * step_out : (i + 1) * step_out], x, TN).astype(BF16)
        copy = pltpu.make_async_copy(
            buf_out.at[i], g_out.at[pl.ds(i * step_out, step_out)], sem_out.at[i]
        )
        copy.start()
        copies.append(copy)
        buf_in[i] = dot(x[:, i * step_in : (i + 1) * step_in], grad_high, TN).astype(BF16)
        copy = pltpu.make_async_copy(
            buf_in.at[i], g_in.at[pl.ds(i * step_in, step_in)], sem_in.at[i]
        )
        copy.start()
        copies.append(copy)
    for copy in copies:
        copy.wait()


def logits_kernel(
    split_chips, shares, tok, dout, disp, comb, router_t, terms_out, left, right, ends
):
    images, slots, count = disp.shape
    chips, rows, main = shares.shape
    width = tok.shape[2]
    summed = []
    for slot in range(slots):
        total = shares[slot * split_chips].astype(F32)
        for chip in range(1, split_chips):
            total = total + shares[slot * split_chips + chip].astype(F32)
        summed.append(total)
    unpack(images, ends, jnp.stack(summed))
    stacked = jnp.concatenate(
        [
            jnp.concatenate(summed, axis=0),
            ends[...].reshape(slots * rows, width - main),
        ],
        axis=1,
    )
    stacked_b = stacked.astype(BF16)
    by_dout = {}
    by_tok = {}
    grads = {}

    def products(b):
        by_dout[b] = dot(dout[b], stacked_b, NT).T
        by_tok[b] = dot(tok[b], stacked_b, NT).T

    def logits_grad(b):
        grad_comb = jnp.concatenate(
            [by_dout[b][s * rows + b : s * rows + b + 1] for s in range(slots)], axis=0
        )
        at = images + b
        grad_disp = jnp.concatenate(
            [by_tok[b][s * rows + at : s * rows + at + 1] for s in range(slots)], axis=0
        )
        dispatch = disp[b]
        combine = comb[b]
        grads[b] = dispatch * (
            grad_disp - jnp.sum(dispatch * grad_disp, axis=1, keepdims=True)
        ) + combine * (grad_comb - jnp.sum(combine * grad_comb, axis=0, keepdims=True))

    terms = jnp.zeros((slots, width), F32)
    for step in range(images + 2):
        if step < images:
            products(step)
        if 0 <= step - 1 < images:
            logits_grad(step - 1)
        if 0 <= step - 2 < images:
            terms = terms + dot(grads[step - 2].astype(BF16), tok[step - 2])
    terms = terms.astype(BF16)
    terms_out[...] = jnp.broadcast_to(terms[None], terms_out.shape)
    for b in range(images):
        left[b] = jnp.concatenate([disp[b], grads[b]], axis=0)
        right[b] = jnp.concatenate(
            [stacked[s * rows + images + b : s * rows + images + b + 1] for s in range(slots)]
            + [router_t[...].astype(F32)],
            axis=0,
        )


def tokens_kernel(left, right, grad_tokens, buf, sems):
    images, parts = buf.shape[:2]
    step = buf.shape[2]
    copies = []
    for b in range(images):
        rhs = right[b].astype(BF16)
        for i in range(parts):
            lhs = left[b, :, i * step : (i + 1) * step].astype(BF16)
            buf[b, i] = dot(lhs, rhs, TN).astype(BF16)
            copy = pltpu.make_async_copy(
                buf.at[b, i], grad_tokens.at[b, pl.ds(i * step, step)], sems.at[b, i]
            )
            copy.start()
            copies.append(copy)
    for copy in copies:
        copy.wait()


def sum_kernel(terms, total):
    total[...] = jnp.sum(terms[...].astype(F32), axis=0)


def swap_chips(blocks):
    count = lax.axis_size("expert")
    groups = [list(range(core, count, 2)) for core in range(2)]
    return lax.all_to_all(
        blocks, "expert", split_axis=0, concat_axis=0, axis_index_groups=groups, tiled=True
    )


def swap_cores(block):
    count = lax.axis_size("expert")
    return lax.ppermute(block, "expert", [(device, device ^ 1) for device in range(count)])


def per_device(tokens, router, w_in, w_out, d_out):
    devices = lax.axis_size("expert")
    chips = devices // 2
    slots = router.shape[1]
    split_chips = chips // slots
    images, count, width = tokens.shape
    hidden_units = w_in.shape[2]
    rows, main, extra = block_shape(images, width)
    half = chips * rows
    router_t = router.T
    big = images * count * width
    weight = width * hidden_units

    blocks, tok, dout, disp, comb = call(
        rows_kernel,
        (
            vmem_out((slots, rows, main), BF16),
            vmem_out((images, count, width), BF16),
            vmem_out((images, count, width), BF16),
            vmem_out((images, slots, count), F32),
            vmem_out((images, slots, count), F32),
        ),
        tuple(in_hbm(array) for array in (tokens, router_t, d_out)),
        (VMEM,) * 5,
        (HBM,) * 3,
        [
            pltpu.VMEM((slots, width), BF16),
            pltpu.VMEM((slots, rows, main), F32),
            pltpu.SemaphoreType.DMA((2 * images,)),
            pltpu.SemaphoreType.DMA((2,)),
        ],
        (6 * slots * big, 4 * big),
        limit=56 * MIB,
    )
    send = call(
        functools.partial(repeat_kernel, split_chips),
        vmem_out((chips, rows, main), BF16),
        (in_vmem(blocks), in_vmem(tok), in_vmem(dout)),
        VMEM,
        (VMEM,) * 3,
        (),
        (4 * half * weight, 40 * weight),
    )
    near = swap_chips(send)
    far = swap_cores(near)
    w_one, w_two = in_vmem(w_in[0]), in_vmem(w_out[0])
    inner = (
        vmem_out((half, width), BF16),
        vmem_out((half, hidden_units), BF16),
        vmem_out((half, hidden_units), BF16),
    )
    hidden_near = call(
        functools.partial(near_kernel, images),
        inner,
        (in_vmem(near), w_one, w_two),
        (VMEM,) * 3,
        (VMEM,) * 3,
        [pltpu.VMEM((chips, rows, extra), F32)],
        (4 * half * weight, 4 * weight),
    )
    hidden_near = [in_vmem(array) for array in hidden_near]
    other, *hidden_far = call(
        functools.partial(far_kernel, images),
        (vmem_out((chips, rows, main), BF16),) + inner,
        (in_vmem(far), w_one, w_two, hidden_near[1]),
        (VMEM,) * 4,
        (VMEM,) * 4,
        [
            pltpu.VMEM((chips, rows, extra), F32),
            pltpu.VMEM((chips, rows, main), F32),
        ],
        (8 * half * weight, 4 * weight),
    )
    hidden_far = [in_vmem(array) for array in hidden_far]
    received = swap_cores(other)
    own = call(
        functools.partial(own_kernel, images),
        vmem_out((chips, rows, main), F32),
        (hidden_near[1], hidden_near[2], w_one, w_two),
        VMEM,
        (VMEM,) * 4,
        (),
        (4 * half * weight, 4 * weight),
    )
    total = call(
        add_kernel,
        vmem_out((chips, rows, main), BF16),
        (in_vmem(own), in_vmem(received)),
        VMEM,
        (VMEM,) * 2,
        (),
        (half * main, 8 * half * main),
    )
    shares = swap_chips(total)
    parts = 5
    g_in, g_out = call(
        functools.partial(weights_kernel, images),
        (
            jax.ShapeDtypeStruct((width, hidden_units), BF16),
            jax.ShapeDtypeStruct((hidden_units, width), BF16),
        ),
        (*hidden_near, *hidden_far),
        (HBM,) * 2,
        (VMEM,) * 6,
        [
            pltpu.VMEM((parts, width // parts, hidden_units), BF16),
            pltpu.VMEM((parts, hidden_units // parts, width), BF16),
            pltpu.SemaphoreType.DMA((parts,)),
            pltpu.SemaphoreType.DMA((parts,)),
        ],
        (8 * half * weight, 4 * weight),
    )
    terms, left, right = call(
        functools.partial(logits_kernel, split_chips),
        (
            vmem_out((devices, slots, width), BF16),
            vmem_out((images, 2 * slots, count), F32),
            vmem_out((images, 2 * slots, width), F32),
        ),
        (
            in_vmem(shares),
            in_vmem(tok),
            in_vmem(dout),
            in_vmem(disp),
            in_vmem(comb),
            router_t,
        ),
        (VMEM,) * 3,
        (VMEM,) * 6,
        [pltpu.VMEM((slots, rows, extra), F32)],
        (6 * slots * big, 4 * big),
    )
    terms = lax.all_to_all(terms, "expert", split_axis=0, concat_axis=0, tiled=True)
    pieces = 2
    grad_tokens = call(
        tokens_kernel,
        jax.ShapeDtypeStruct(tokens.shape, BF16),
        (in_vmem(left), in_vmem(right)),
        HBM,
        (VMEM,) * 2,
        [
            pltpu.VMEM((images, pieces, count // pieces, width), BF16),
            pltpu.SemaphoreType.DMA((images, pieces)),
        ],
        (4 * slots * big, 2 * big),
    )
    grad_router = call(
        sum_kernel,
        jax.ShapeDtypeStruct((slots, width), F32),
        (in_vmem(terms),),
        VMEM,
        (VMEM,),
        (),
        (devices * slots * width, 2 * devices * slots * width),
    )
    return (grad_tokens, g_in[None], g_out[None], grad_router.T)


def solution(mesh):
    in_specs = (
        P(("groups", "expert"), None, None),
        P(None, "groups"),
        P(("groups", "expert"), None, None),
        P(("groups", "expert"), None, None),
        P(("groups", "expert"), None, None),
    )
    out_specs = (
        P(("groups", "expert"), None, None),
        P(("groups", "expert"), None, None),
        P(("groups", "expert"), None, None),
        P(None, "groups"),
    )
    return jax.shard_map(
        per_device, mesh=mesh, in_specs=in_specs, out_specs=out_specs, check_vma=False
    )
```

```python
import functools

import jax
import jax.numpy as jnp
from jax import lax
from jax.experimental import pallas as pl
from jax.experimental.pallas import tpu as pltpu
from jax.sharding import PartitionSpec as P

F32 = jnp.float32
BF16 = jnp.bfloat16
NT = (((1,), (1,)), ((), ()))
TN = (((0,), (0,)), ((), ()))
NN = (((1,), (0,)), ((), ()))

VMEM = pl.BlockSpec(memory_space=pltpu.VMEM)
HBM = pl.BlockSpec(memory_space=pltpu.HBM)
MIB = 1024 * 1024


def dot(left, right, dims=NN):
    return lax.dot_general(left, right, dims, preferred_element_type=F32)


def in_vmem(array):
    return pltpu.with_memory_space_constraint(array, pltpu.VMEM)


def in_hbm(array):
    return pltpu.with_memory_space_constraint(array, pltpu.HBM)


def vmem_out(shape, dtype):
    return pltpu.VMEM(shape, dtype)


def call(kernel, outs, ins, out_specs, in_specs, scratch=(), cost=None, limit=40 * MIB):
    return pl.pallas_call(
        kernel,
        out_shape=outs,
        in_specs=in_specs,
        out_specs=out_specs,
        scratch_shapes=list(scratch),
        compiler_params=pltpu.CompilerParams(vmem_limit_bytes=limit),
        cost_estimate=pl.CostEstimate(flops=cost[0], bytes_accessed=cost[1], transcendentals=0),
    )(*ins)


def block_shape(images, width):
    extra = width // 5
    main = width - extra
    ends = -(-2 * images * extra // main)
    return -(-(2 * images + ends) // 8) * 8, main, extra


def end_place(images, main, extra, row):
    per = main // extra
    return 2 * images + row // per, row % per * extra


def pack(images, scratch, values):
    main = scratch.shape[2]
    extra = values.shape[2] - main
    scratch[...] = values[:, :, :main]
    for row in range(2 * images):
        to, column = end_place(images, main, extra, row)
        scratch[:, to, column : column + extra] = values[:, row, main:]


def unpack(images, scratch, values):
    main = values.shape[2]
    extra = scratch.shape[2]
    scratch[...] = jnp.zeros_like(scratch)
    for row in range(2 * images):
        at, column = end_place(images, main, extra, row)
        scratch[:, row, :] = values[:, at, column : column + extra]


def rows_kernel(
    tokens,
    router_hbm,
    d_out,
    rows_out,
    tok,
    dout,
    disp_out,
    comb_out,
    router_t,
    block,
    tok_sems,
    sems,
    other_sems,
):
    images = tok.shape[0]
    main = rows_out.shape[2]
    extra = tok.shape[2] - main
    fetch_router = pltpu.make_async_copy(router_hbm, router_t, other_sems.at[0])
    fetch_router.start()
    fetch_tok = []
    for b in range(images):
        parts = max(4 >> b, 1)
        step = tok.shape[1] // parts
        fetch_tok.append(
            [
                pltpu.make_async_copy(
                    tokens.at[b, pl.ds(i * step, step)],
                    tok.at[b, pl.ds(i * step, step)],
                    tok_sems.at[b, i],
                )
                for i in range(parts)
            ]
        )
    fetch_dout = [
        pltpu.make_async_copy(d_out.at[b], dout.at[b], sems.at[b]) for b in range(images)
    ]
    for copies in fetch_tok:
        for copy in copies:
            copy.start()
    block[...] = jnp.zeros_like(block)

    def put(row, values):
        to, column = end_place(images, main, extra, row)
        block[:, row, :] = values[:, :main]
        block[:, to, column : column + extra] = values[:, main:]

    fetch_router.wait()
    for copy in fetch_dout:
        copy.start()
    logits = {}
    combs = {}
    disps = {}

    def softmaxes(b):
        exps = jnp.exp(logits[b] - jnp.max(logits[b], axis=1, keepdims=True))
        disp = exps * (1.0 / jnp.sum(exps, axis=1, keepdims=True))
        exps = jnp.exp(logits[b] - jnp.max(logits[b], axis=0, keepdims=True))
        comb = exps * (1.0 / jnp.sum(exps, axis=0, keepdims=True))
        disp_out[b] = disp
        comb_out[b] = comb
        disps[b] = disp.astype(BF16)
        combs[b] = comb.astype(BF16)

    for step in range(2 * images):
        if step < images:
            for copy in fetch_tok[step]:
                copy.wait()
            logits[step] = dot(router_t[...], tok[step], NT)
        else:
            fetch_dout[step - images].wait()
        if 0 <= step - 1 < images:
            softmaxes(step - 1)
        if step >= images:
            put(step, dot(combs[step - images], dout[step - images]))
        if 0 <= step - 2 < images:
            put(step - 2, dot(disps[step - 2], tok[step - 2]))
    for b in range(max(2 * images - 2, 0), images):
        put(b, dot(disps[b], tok[b]))
    rows_out[...] = block[...].astype(BF16)


def repeat_kernel(split_chips, rows, tok, dout, send):
    for slot in range(rows.shape[0]):
        for chip in range(split_chips):
            send[slot * split_chips + chip] = rows[slot]


def hidden_rows(images, blocks, w_in, w_out, x_out, hid_out, grad_out, ends):
    chips, rows, main = blocks.shape
    half = chips * rows
    width = x_out.shape[1]
    unpack(images, ends, blocks[...].astype(F32))
    x = jnp.concatenate(
        [
            blocks[...].reshape(half, main),
            ends[...].reshape(half, width - main).astype(BF16),
        ],
        axis=1,
    )
    x_out[...] = x
    pre = dot(x, w_in[...])
    grad_hidden = dot(x, w_out[...], NT)
    place = lax.broadcasted_iota(jnp.int32, pre.shape, 0) % rows
    slot_row = place < images
    grad_hidden = pltpu.roll(grad_hidden, half - images, 0)
    scale = 0.7978845608028654
    square = pre * pre
    tanh = jnp.tanh(scale * pre * (1.0 + 0.044715 * square))
    cdf = 0.5 * (1.0 + tanh)
    slope = cdf + (0.5 * scale) * pre * (1.0 - tanh * tanh) * (1.0 + (3 * 0.044715) * square)
    hidden = jnp.where(slot_row, pre * cdf, 0.0).astype(BF16)
    grad_pre = jnp.where(slot_row, slope * grad_hidden, 0.0)
    grad_low = pltpu.roll(grad_pre, images, 0).astype(BF16)
    hid_out[...] = hidden
    grad_out[...] = grad_low
    return hidden, grad_low


def near_kernel(images, blocks, w_in, w_out, x_out, hid_out, grad_out, ends):
    hidden_rows(images, blocks, w_in, w_out, x_out, hid_out, grad_out, ends)


def far_kernel(images, blocks, w_in, w_out, _, other, x_out, hid_out, grad_out, ends, packed):
    hidden, grad_low = hidden_rows(images, blocks, w_in, w_out, x_out, hid_out, grad_out, ends)
    shares = dot(hidden, w_out[...]) + dot(grad_low, w_in[...], NT)
    pack(images, packed, shares.reshape(blocks.shape[:2] + (shares.shape[1],)))
    other[...] = packed[...].astype(BF16)


def own_kernel(images, hid, grad, w_in, w_out, own):
    chips, rows, _ = own.shape
    shares = dot(hid[...], w_out[...]) + dot(grad[...], w_in[...], NT)
    pack(images, own, shares.reshape(chips, rows, shares.shape[1]))


def add_kernel(own, received, total):
    total[...] = (own[...] + received[...].astype(F32)).astype(BF16)


def weights_kernel(
    images,
    x_near,
    hid_near,
    grad_near,
    x_far,
    hid_far,
    grad_far,
    g_in,
    g_out,
    buf_in,
    buf_out,
    sem_in,
    sem_out,
):
    parts = buf_in.shape[0]
    step_in = g_in.shape[0] // parts
    step_out = g_out.shape[0] // parts
    x = jnp.concatenate([x_near[...], x_far[...]], axis=0)
    hid = jnp.concatenate([hid_near[...], hid_far[...]], axis=0)
    grad = jnp.concatenate([grad_near[...], grad_far[...]], axis=0)
    hid_low = pltpu.roll(hid.astype(F32), images, 0).astype(BF16)
    grad_high = pltpu.roll(grad.astype(F32), x.shape[0] - images, 0).astype(BF16)
    copies = []
    for i in range(parts):
        buf_out[i] = dot(hid_low[:, i * step_out : (i + 1) * step_out], x, TN).astype(BF16)
        copy = pltpu.make_async_copy(
            buf_out.at[i], g_out.at[pl.ds(i * step_out, step_out)], sem_out.at[i]
        )
        copy.start()
        copies.append(copy)
        buf_in[i] = dot(x[:, i * step_in : (i + 1) * step_in], grad_high, TN).astype(BF16)
        copy = pltpu.make_async_copy(
            buf_in.at[i], g_in.at[pl.ds(i * step_in, step_in)], sem_in.at[i]
        )
        copy.start()
        copies.append(copy)
    for copy in copies:
        copy.wait()


def logits_kernel(
    split_chips, shares, tok, dout, disp, comb, router_t, terms_out, left, right, ends
):
    images, slots, count = disp.shape
    chips, rows, main = shares.shape
    width = tok.shape[2]
    summed = []
    for slot in range(slots):
        total = shares[slot * split_chips].astype(F32)
        for chip in range(1, split_chips):
            total = total + shares[slot * split_chips + chip].astype(F32)
        summed.append(total)
    unpack(images, ends, jnp.stack(summed))
    stacked = jnp.concatenate(
        [
            jnp.concatenate(summed, axis=0),
            ends[...].reshape(slots * rows, width - main),
        ],
        axis=1,
    )
    stacked_b = stacked.astype(BF16)
    by_dout = {}
    by_tok = {}
    grads = {}

    def products(b):
        by_dout[b] = dot(stacked_b, dout[b], NT)
        by_tok[b] = dot(stacked_b, tok[b], NT)

    def logits_grad(b):
        grad_comb = jnp.concatenate(
            [by_dout[b][s * rows + b : s * rows + b + 1] for s in range(slots)], axis=0
        )
        at = images + b
        grad_disp = jnp.concatenate(
            [by_tok[b][s * rows + at : s * rows + at + 1] for s in range(slots)], axis=0
        )
        dispatch = disp[b]
        combine = comb[b]
        grads[b] = dispatch * (
            grad_disp - jnp.sum(dispatch * grad_disp, axis=1, keepdims=True)
        ) + combine * (grad_comb - jnp.sum(combine * grad_comb, axis=0, keepdims=True))

    terms = jnp.zeros((slots, width), F32)
    for step in range(images + 2):
        if step < images:
            products(step)
        if 0 <= step - 1 < images:
            logits_grad(step - 1)
        if 0 <= step - 2 < images:
            terms = terms + dot(grads[step - 2].astype(BF16), tok[step - 2])
    terms = terms.astype(BF16)
    terms_out[...] = jnp.broadcast_to(terms[None], terms_out.shape)
    for b in range(images):
        left[b] = jnp.concatenate([disp[b], grads[b]], axis=0)
        right[b] = jnp.concatenate(
            [stacked[s * rows + images + b : s * rows + images + b + 1] for s in range(slots)]
            + [router_t[...].astype(F32)],
            axis=0,
        )


def tokens_kernel(left, right, grad_tokens, buf, sems):
    images, parts = buf.shape[:2]
    step = buf.shape[2]
    copies = []
    for b in range(images):
        rhs = right[b].astype(BF16)
        for i in range(parts):
            lhs = left[b, :, i * step : (i + 1) * step].astype(BF16)
            buf[b, i] = dot(lhs, rhs, TN).astype(BF16)
            copy = pltpu.make_async_copy(
                buf.at[b, i], grad_tokens.at[b, pl.ds(i * step, step)], sems.at[b, i]
            )
            copy.start()
            copies.append(copy)
    for copy in copies:
        copy.wait()


def sum_kernel(terms, total):
    total[...] = jnp.sum(terms[...].astype(F32), axis=0)


def swap_chips(blocks):
    count = lax.axis_size("expert")
    groups = [list(range(core, count, 2)) for core in range(2)]
    return lax.all_to_all(
        blocks, "expert", split_axis=0, concat_axis=0, axis_index_groups=groups, tiled=True
    )


def swap_cores(block):
    count = lax.axis_size("expert")
    return lax.ppermute(block, "expert", [(device, device ^ 1) for device in range(count)])


def per_device(tokens, router, w_in, w_out, d_out):
    devices = lax.axis_size("expert")
    chips = devices // 2
    slots = router.shape[1]
    split_chips = chips // slots
    images, count, width = tokens.shape
    hidden_units = w_in.shape[2]
    rows, main, extra = block_shape(images, width)
    half = chips * rows
    router_t = router.T
    big = images * count * width
    weight = width * hidden_units

    blocks, tok, dout, disp, comb = call(
        rows_kernel,
        (
            vmem_out((slots, rows, main), BF16),
            vmem_out((images, count, width), BF16),
            vmem_out((images, count, width), BF16),
            vmem_out((images, slots, count), F32),
            vmem_out((images, slots, count), F32),
        ),
        tuple(in_hbm(array) for array in (tokens, router_t, d_out)),
        (VMEM,) * 5,
        (HBM,) * 3,
        [
            pltpu.VMEM((slots, width), BF16),
            pltpu.VMEM((slots, rows, main), F32),
            pltpu.SemaphoreType.DMA((images, 4)),
            pltpu.SemaphoreType.DMA((images,)),
            pltpu.SemaphoreType.DMA((2,)),
        ],
        (6 * slots * big, 4 * big),
        limit=56 * MIB,
    )
    send = call(
        functools.partial(repeat_kernel, split_chips),
        vmem_out((chips, rows, main), BF16),
        (in_vmem(blocks), in_vmem(tok), in_vmem(dout)),
        VMEM,
        (VMEM,) * 3,
        (),
        (4 * half * weight, 40 * weight),
    )
    near = swap_chips(send)
    far = swap_cores(near)
    w_one, w_two = in_vmem(w_in[0]), in_vmem(w_out[0])
    inner = (
        vmem_out((half, width), BF16),
        vmem_out((half, hidden_units), BF16),
        vmem_out((half, hidden_units), BF16),
    )
    hidden_near = call(
        functools.partial(near_kernel, images),
        inner,
        (in_vmem(near), w_one, w_two),
        (VMEM,) * 3,
        (VMEM,) * 3,
        [pltpu.VMEM((chips, rows, extra), F32)],
        (4 * half * weight, 4 * weight),
    )
    hidden_near = [in_vmem(array) for array in hidden_near]
    other, *hidden_far = call(
        functools.partial(far_kernel, images),
        (vmem_out((chips, rows, main), BF16),) + inner,
        (in_vmem(far), w_one, w_two, hidden_near[1]),
        (VMEM,) * 4,
        (VMEM,) * 4,
        [
            pltpu.VMEM((chips, rows, extra), F32),
            pltpu.VMEM((chips, rows, main), F32),
        ],
        (8 * half * weight, 4 * weight),
    )
    hidden_far = [in_vmem(array) for array in hidden_far]
    received = swap_cores(other)
    own = call(
        functools.partial(own_kernel, images),
        vmem_out((chips, rows, main), F32),
        (hidden_near[1], hidden_near[2], w_one, w_two),
        VMEM,
        (VMEM,) * 4,
        (),
        (4 * half * weight, 4 * weight),
    )
    total = call(
        add_kernel,
        vmem_out((chips, rows, main), BF16),
        (in_vmem(own), in_vmem(received)),
        VMEM,
        (VMEM,) * 2,
        (),
        (half * main, 8 * half * main),
    )
    shares = swap_chips(total)
    parts = 5
    g_in, g_out = call(
        functools.partial(weights_kernel, images),
        (
            jax.ShapeDtypeStruct((width, hidden_units), BF16),
            jax.ShapeDtypeStruct((hidden_units, width), BF16),
        ),
        (*hidden_near, *hidden_far),
        (HBM,) * 2,
        (VMEM,) * 6,
        [
            pltpu.VMEM((parts, width // parts, hidden_units), BF16),
            pltpu.VMEM((parts, hidden_units // parts, width), BF16),
            pltpu.SemaphoreType.DMA((parts,)),
            pltpu.SemaphoreType.DMA((parts,)),
        ],
        (8 * half * weight, 4 * weight),
    )
    terms, left, right = call(
        functools.partial(logits_kernel, split_chips),
        (
            vmem_out((devices, slots, width), BF16),
            vmem_out((images, 2 * slots, count), F32),
            vmem_out((images, 2 * slots, width), F32),
        ),
        (
            in_vmem(shares),
            in_vmem(tok),
            in_vmem(dout),
            in_vmem(disp),
            in_vmem(comb),
            router_t,
        ),
        (VMEM,) * 3,
        (VMEM,) * 6,
        [pltpu.VMEM((slots, rows, extra), F32)],
        (6 * slots * big, 4 * big),
    )
    terms = lax.all_to_all(terms, "expert", split_axis=0, concat_axis=0, tiled=True)
    pieces = 2
    grad_tokens = call(
        tokens_kernel,
        jax.ShapeDtypeStruct(tokens.shape, BF16),
        (in_vmem(left), in_vmem(right)),
        HBM,
        (VMEM,) * 2,
        [
            pltpu.VMEM((images, pieces, count // pieces, width), BF16),
            pltpu.SemaphoreType.DMA((images, pieces)),
        ],
        (4 * slots * big, 2 * big),
    )
    grad_router = call(
        sum_kernel,
        jax.ShapeDtypeStruct((slots, width), F32),
        (in_vmem(terms),),
        VMEM,
        (VMEM,),
        (),
        (devices * slots * width, 2 * devices * slots * width),
    )
    return (grad_tokens, g_in[None], g_out[None], grad_router.T)


def solution(mesh):
    in_specs = (
        P(("groups", "expert"), None, None),
        P(None, "groups"),
        P(("groups", "expert"), None, None),
        P(("groups", "expert"), None, None),
        P(("groups", "expert"), None, None),
    )
    out_specs = (
        P(("groups", "expert"), None, None),
        P(("groups", "expert"), None, None),
        P(("groups", "expert"), None, None),
        P(None, "groups"),
    )
    return jax.shard_map(
        per_device, mesh=mesh, in_specs=in_specs, out_specs=out_specs, check_vma=False
    )
```
